32 devices in a mesh: tile: 4 (over y, x), date: 8 (over z, core).
Axes of the slice: x: 2, y: 2, z: 4, core: 2. Of those that a mesh axis runs over, the one named last changes fastest.
Arguments:
- layer_input: bfloat16 [32, 32, 1024], P('tile', 'date'), may hold values from -6 to 6
- head_input: bfloat16 [32, 32, 1024], P('tile', 'date'), may hold values from -6 to 6
- out_grad: bfloat16 [32, 32, 1024], P('tile', 'date'), may hold values from -6 to 6
- sensor_ids: int32 [32], P('date'), may hold values from 0 to 1
- valid_mask: int32 [32, 32], P('tile', 'date'), may hold values 0 or 1
- sensor_table: float32 [2, 1024], replicated, may hold values from -4 to 4
- proj_weight: bfloat16 [1024, 264], replicated, may hold values from -0.09375 to 0.09375
- step_bias: float32 [8], replicated, may hold values from -4 to -2
- decay_log: float32 [8], replicated, may hold values from -4 to 0
- skip_gain: float32 [8], replicated, may hold values from 0.5 to 1.5
Outputs:
- value_grad: bfloat16 [32, 32, 1024], P('tile', 'date')
- input_grad: bfloat16 [32, 32, 1024], P('tile', 'date')
- weight_grad: float32 [1024, 264], replicated
- table_grad: float32 [2, 1024], replicated
- head_grads: float32 [3, 8], replicated
The draws below stay inside these ranges and needn't reach their ends.
All inputs are finite; a program needn't handle non-finite values. No bound on the sum of `valid_mask` on one device may be relied on, other than what follows from the above.
Results may differ from the reference program's by a relative error of at most 0.0088.
Values may be sent and summed in bfloat16 or wider, within the bound.
No kernel may reach another device: no remote copies, remote signals or barrier semaphores. Data moves between devices by JAX's collectives and lax.ppermute only.
A program may use at most 64 MiB of HBM per device.

```python
import math
import jax
import jax.numpy as jnp
from jax import lax

D = 1024
H = 8
P_SIZE = 128
N = 128
SPAN = 64
L = 32
PIX = 32
N_TILE = 4


def set_ends(values, own_key, least, high):
    extent = values.shape
    index_at = [jax.random.randint(jax.random.fold_in(own_key, axis), (), 0, extent[axis]) for axis in range(len(extent))]
    values = values.at[tuple(index_at)].set(least)
    longest = extent.index(max(extent))
    index_at[longest] = (index_at[longest] + 1) % extent[longest]
    return values.at[tuple(index_at)].set(high)


def block_levels(rng, dims, split, low, high):
    def one(dim, shards_of):
        steps = jax.random.uniform(jax.random.fold_in(jax.random.fold_in(rng, 6), dim), (shards_of,), jnp.float32, low / len(split), high / len(split))
        return jnp.repeat(jnp.exp(steps), dims[dim] // shards_of).reshape((-1,) + (1,) * (len(dims) - dim - 1))

    factor_of = one(*split[0])
    for cut in split[1:]:
        factor_of = factor_of * one(*cut)
    return factor_of


def centred(own_key, dims, scale, limit, split=(), held_as=jnp.bfloat16):
    gain = block_levels(own_key, dims, split, -0.22, 0.18) if split else 1.0
    values = jax.random.normal(own_key, dims, jnp.float32) * scale * gain
    return jnp.minimum(jnp.maximum(values, -limit), limit).astype(held_as)


def setup_inputs(seed: int = 0) -> dict:
    key_list = jax.random.split(jax.random.key(seed), 11)
    layer_input = centred(key_list[0], (PIX, L, D), 1.0, 6.0, ((0, 4), (1, 8)))
    head_input = centred(key_list[1], (PIX, L, H * P_SIZE), 1.0, 6.0, ((0, 4), (1, 8)))
    out_grad = centred(key_list[2], (PIX, L, H * P_SIZE), 1.0, 6.0, ((0, 4), (1, 8)))
    sensor_ids = set_ends(jax.random.randint(key_list[3], (L,), 0, 2), jax.random.fold_in(key_list[3], 1), 0, 1).astype(jnp.int32)
    valid_mask = set_ends((jax.random.randint(key_list[4], (PIX, L), 0, 5) < 4).astype(jnp.int32), jax.random.fold_in(key_list[4], 1), 0, 1)
    sensor_table = centred(key_list[5], (2, D), 1.0, 4.0, (), jnp.float32)
    proj_weight = centred(key_list[6], (D, 2 * N + H), (4 * D) ** -0.5, 0.09375)
    step_bias = jnp.clip(jax.random.uniform(key_list[7], (H,), jnp.float32, -4.0, -2.0), -4.0, -2.0)
    decay_log = jnp.clip(jax.random.uniform(key_list[8], (H,), jnp.float32, -4.0, 0.0), -4.0, 0.0)
    skip_gain = jnp.clip(jax.random.uniform(key_list[9], (H,), jnp.float32, 0.5, 1.5), 0.5, 1.5)
    return dict(layer_input=layer_input, head_input=head_input, out_grad=out_grad, sensor_ids=sensor_ids, valid_mask=valid_mask, sensor_table=sensor_table, proj_weight=proj_weight, step_bias=step_bias, decay_log=decay_log, skip_gain=skip_gain)


HIGHEST_PREC = lax.Precision.HIGHEST
NEG_FILL = -1e+30

def span_scan(values_in, keys_in, reads_in, step_in, decay_in, skip_in, block_len):
    series, length, head_count, width_p = values_in.shape
    states_n = keys_in.shape[2]
    block_count = length // block_len
    decay_rate = -jnp.exp(decay_in)
    values_blk = values_in.reshape(series, block_count, block_len, head_count, width_p)
    keys_b = keys_in.reshape(series, block_count, block_len, states_n)
    reads_c = reads_in.reshape(series, block_count, block_len, states_n)
    step_blocks = step_in.reshape(series, block_count, block_len, head_count)
    weighted = values_blk * step_blocks[..., None]
    log_decay = jnp.cumsum(step_blocks * decay_rate, axis=2)
    log_heads = jnp.swapaxes(log_decay, 2, 3)
    row_ids = lax.broadcasted_iota(jnp.int32, (block_len, block_len), 0)
    col_ids = lax.broadcasted_iota(jnp.int32, (block_len, block_len), 1)
    causal = row_ids >= col_ids
    gap_logs = log_heads[..., :, None] - log_heads[..., None, :]
    kernel = jnp.exp(jnp.where(causal, gap_logs, NEG_FILL))
    scores = jnp.einsum('scin,scjn->scij', reads_c, keys_b, precision=HIGHEST_PREC)
    mixed_kernel = kernel * scores[:, :, None]
    within_block = jnp.einsum('schij,scjhp->scihp', mixed_kernel, weighted, precision=HIGHEST_PREC)
    to_block_end = jnp.exp(log_decay[:, :, -1:, :] - log_decay)
    block_states = jnp.einsum('scjn,scjhp->schnp', keys_b, weighted * to_block_end[..., None], precision=HIGHEST_PREC)
    block_totals = jnp.exp(log_decay[:, :, -1, :])

    def advance(state_carry, block_item):
        block_total, block_state = block_item
        return (state_carry * block_total[:, :, None, None] + block_state, state_carry)
    zero_state = jnp.zeros((series, head_count, states_n, width_p), dtype=values_in.dtype)
    _, entering = lax.scan(advance, zero_state, (jnp.moveaxis(block_totals, 1, 0), jnp.moveaxis(block_states, 1, 0)))
    entering = jnp.moveaxis(entering, 0, 1)
    from_earlier = jnp.einsum('scin,schnp->scihp', reads_c, entering, precision=HIGHEST_PREC) * jnp.exp(log_decay)[..., None]
    result = within_block + from_earlier + skip_in[:, None] * values_blk
    return result.reshape(series, length, head_count, width_p)

def reference(layer_input, head_input, out_grad, sensor_ids, valid_mask, sensor_table, proj_weight, step_bias, decay_log, skip_gain):
    pixel_count, length, model_d = layer_input.shape
    head_count = step_bias.shape[0]
    width_hp = head_input.shape[2]
    width_p = width_hp // head_count
    states_n = (proj_weight.shape[1] - head_count) // 2
    block_len = min(SPAN, length)
    is_second = (sensor_ids == 1)[None, :, None]
    sensor_embed = jnp.where(is_second, sensor_table[1], sensor_table[0])
    mixed_in = (layer_input.astype(jnp.float32) + sensor_embed).astype(jnp.bfloat16)
    flat_in = mixed_in.reshape(pixel_count * length, model_d)
    projected = jnp.dot(flat_in, proj_weight, preferred_element_type=jnp.float32).reshape(pixel_count, length, -1)
    pair_proj = projected[:, :, :2 * states_n].astype(jnp.bfloat16)
    step_pre = projected[:, :, 2 * states_n:] + step_bias
    valid_gate = valid_mask.astype(jnp.float32)[:, :, None]
    step_sizes = (valid_gate * jax.nn.softplus(step_pre)).astype(jnp.bfloat16)

    def local_scan(values_in, keys_in, reads_in, step_in, decay_in, skip_in):
        return span_scan(values_in, keys_in, reads_in, step_in, decay_in, skip_in, block_len)

    def one_group(group_item):
        group_values, cotangent, pair_blk, step_blk = group_item
        group_size = group_values.shape[0]
        _, pullback = jax.vjp(local_scan, group_values.astype(jnp.float32).reshape(group_size, length, head_count, width_p), pair_blk[..., :states_n].astype(jnp.float32), pair_blk[..., states_n:].astype(jnp.float32), step_blk.astype(jnp.float32), decay_log, skip_gain)
        grad_values, grad_b, grad_c, grad_steps, grad_decay, grad_skip = pullback(cotangent.astype(jnp.float32).reshape(group_size, length, head_count, width_p))
        return (grad_values.reshape(group_size, length, width_hp).astype(jnp.bfloat16), jnp.concatenate([grad_b, grad_c], axis=-1).astype(jnp.bfloat16), grad_steps.astype(jnp.bfloat16), grad_decay, grad_skip)

    def by_groups(array):
        return array.reshape((N_TILE, pixel_count // N_TILE) + array.shape[1:])
    results = lax.map(one_group, (by_groups(head_input), by_groups(out_grad), by_groups(pair_proj), by_groups(step_sizes)))
    value_grad = results[0].reshape(pixel_count, length, width_hp)
    pair_grad = results[1].reshape(pixel_count, length, 2 * states_n)
    step_grad = results[2].reshape(pixel_count, length, head_count)
    decay_part = lax.optimization_barrier(jnp.sum(results[3], axis=0))
    skip_part = lax.optimization_barrier(jnp.sum(results[4], axis=0))
    raw_grad = step_grad.astype(jnp.float32) * valid_gate * jax.nn.sigmoid(step_pre)
    proj_grad = jnp.concatenate([pair_grad, raw_grad.astype(jnp.bfloat16)], axis=-1).reshape(pixel_count * length, -1)
    grad_scale = 1.0 / math.sqrt(pixel_count * length)
    weight_grad = jnp.dot(flat_in.T, proj_grad, preferred_element_type=jnp.float32) * grad_scale
    flat_grad = jnp.dot(proj_grad, proj_weight.T, preferred_element_type=jnp.float32)
    input_grad = flat_grad.astype(jnp.bfloat16).reshape(pixel_count, length, model_d)
    flat_back = flat_grad.reshape(pixel_count, length, model_d)
    second_sum = lax.optimization_barrier(jnp.sum(jnp.where(is_second, flat_back, 0.0), axis=(0, 1)))
    first_sum = lax.optimization_barrier(jnp.sum(jnp.where(is_second, 0.0, flat_back), axis=(0, 1)))
    table_grad = jnp.stack([first_sum, second_sum]) * grad_scale
    head_grads = jnp.stack([decay_part, lax.optimization_barrier(jnp.sum(raw_grad, axis=(0, 1))), skip_part]) * grad_scale
    return (value_grad, input_grad, weight_grad, table_grad, head_grads)
```

```python
import functools
import math

import jax
import jax.numpy as jnp
from jax import lax
from jax.experimental import pallas as pl
from jax.experimental.pallas import tpu as pltpu
from jax.sharding import PartitionSpec as P

NEG_FILL = -1e30
HIGHEST_PREC = lax.Precision.HIGHEST
F32 = jnp.float32
BF16 = jnp.bfloat16
LANES = 128
EXT = 384
SLAB_ROWS = 320
WIDE = SLAB_ROWS // 8


def nt(a, b, precision=None):
    return lax.dot_general(
        a, b, (((1,), (1,)), ((), ())), preferred_element_type=F32, precision=precision
    )


def nn(a, b, precision=None):
    return lax.dot_general(
        a, b, (((1,), (0,)), ((), ())), preferred_element_type=F32, precision=precision
    )


def tn(a, b):
    return lax.dot_general(a, b, (((0,), (0,)), ((), ())), preferred_element_type=F32)


def split(x):
    high = x.astype(BF16)
    return high, (x - high.astype(F32)).astype(BF16)


def series_kernel(heads, model_d, tiles, slab, recv, w_t, params, send, back, sel):
    length = recv.shape[0]
    width_p = model_d // heads
    states = (w_t.shape[0] - heads) // 2
    mixed = recv[:, :model_d]
    aux = recv[:, 3 * model_d :].astype(F32)
    gate = aux[:, 0:1]
    ids = aux[:, 1:2]
    bias = params[0:1, :heads]
    rate = -jnp.exp(params[1:2, :heads])
    projected = nt(mixed, w_t[...])
    keys = projected[:, :states].astype(BF16)
    reads = projected[:, states : 2 * states].astype(BF16)
    step_pre = projected[:, 2 * states :] + bias
    softplus = jnp.maximum(step_pre, 0.0) + jnp.log1p(jnp.exp(-jnp.abs(step_pre)))
    steps_b = (gate * softplus).astype(BF16)
    steps = steps_b.astype(F32)

    row = lax.broadcasted_iota(jnp.int32, (length, length), 0)
    col = lax.broadcasted_iota(jnp.int32, (length, length), 1)
    upper = col >= row
    upper_f = upper.astype(F32)
    eye = (col == row).astype(F32)
    lower_b = (row >= col).astype(BF16)
    head_row = lax.broadcasted_iota(jnp.int32, (heads, heads), 0)
    head_col = lax.broadcasted_iota(jnp.int32, (heads, heads), 1)
    eye_h = (head_row == head_col).astype(F32)
    rate_col = jnp.sum(eye_h * rate, axis=1, keepdims=True)
    log_col = nn(lower_b, steps_b) * rate
    steps_t = nt(eye_h.astype(BF16), steps_b).astype(BF16)
    log_row = nn(steps_t, upper.astype(BF16)) * rate_col
    scores_t = nt(keys, reads)

    pair_t = jnp.zeros((length, length), F32)
    weighted_cols, read_rows, skip_cols = [], [], []
    for h in range(heads):
        lo = model_d + h * width_p
        x_h = recv[:, lo : lo + width_p]
        g_h = recv[:, lo + model_d : lo + model_d + width_p]
        dt_h = steps[:, h : h + 1]
        gap = log_row[h : h + 1, :] - log_col[:, h : h + 1]
        decay = jnp.exp(jnp.where(upper, gap, NEG_FILL))
        cross = nt(x_h, g_h)
        mix = decay * scores_t
        pair_t = pair_t + decay * cross * dt_h
        both = mix * cross
        weighted = jnp.sum(both, axis=1, keepdims=True)
        weighted_cols.append(weighted)
        read_rows.append(jnp.sum(both * dt_h, axis=0, keepdims=True))
        skip_cols.append(jnp.sum(cross * eye, axis=1, keepdims=True))
        value = nn(mix.astype(BF16), g_h) * dt_h + params[2 + h : 3 + h, :width_p] * g_h.astype(F32)
        back[:, h * width_p : (h + 1) * width_p] = value.astype(BF16)

    weighted = jnp.concatenate(weighted_cols, axis=1)
    read_sum = jnp.concatenate(read_rows, axis=0)
    skip_terms = jnp.concatenate(skip_cols, axis=1)
    later = nt(upper_f, read_sum, HIGHEST_PREC) - nn(upper_f, steps * weighted, HIGHEST_PREC)
    step_grad = (weighted + rate * later).astype(BF16).astype(F32)
    decay_terms = steps * later * rate
    pair_b = pair_t.astype(BF16)
    grad_keys = nn(pair_b, reads)
    grad_reads = tn(pair_b, keys)
    raw = step_grad * gate * jax.nn.sigmoid(step_pre)
    parts = []
    for term in (raw, decay_terms, skip_terms):
        high, low = split(term)
        parts += [high.astype(F32), low.astype(F32)]
    tail = jnp.concatenate(
        parts + [jnp.zeros((length, EXT - 2 * states - 6 * heads), F32)], axis=1
    )
    ext = jnp.concatenate([grad_keys, grad_reads, tail], axis=1).astype(BF16)
    back[:, model_d:] = ext
    for t in range(tiles):
        send[t, :, :EXT] = ext
        send[t, :, EXT:] = recv[:, t * slab : (t + 1) * slab]
    ids_row = jnp.sum(eye * ids, axis=0, keepdims=True)
    sel[...] = jnp.concatenate([1.0 - ids_row, ids_row, jnp.zeros((14, length), F32)], axis=0).astype(
        BF16
    )


def lane_pad(x, width):
    if x.shape[1] == width:
        return x
    return jnp.concatenate([x, jnp.zeros((x.shape[0], width - x.shape[1]), x.dtype)], axis=1)


def sum_rows(sums):
    high = sums.astype(BF16).astype(F32)
    low = (sums - high).astype(BF16).astype(F32)
    rows = jnp.concatenate([high, low, jnp.zeros((4, EXT), F32)], axis=0)
    return [rows[:, b * LANES : (b + 1) * LANES] for b in range(EXT // LANES)]


def rows_sum(block):
    rows = jnp.concatenate([block[8 * b : 8 * b + 8, :] for b in range(EXT // LANES)], axis=1)
    return rows[0:2] + rows[2:4]


def slab_kernel(cols, core, recv, sel, keep, keep_sums, give):
    tiles, length, width = recv.shape
    slab = width - EXT
    half = slab // 2
    ext = recv[:, :, :EXT].reshape(tiles * length, EXT)
    tokens = recv[:, :, EXT:].reshape(tiles * length, slab)
    part = tn(ext, tokens)[:cols]
    sums = jnp.zeros((16, EXT), F32)
    for t in range(tiles):
        sums = sums + nn(sel[...], recv[t, :, :EXT])
    sums = sums[0:2]
    mine = core[0] == 0
    first = lane_pad(part[:, :half], LANES)
    second = lane_pad(part[:, half:], LANES)
    keep[...] = jnp.where(mine, first, second)
    keep_sums[...] = sums
    other = jnp.where(mine, second, first)
    give[...] = jnp.concatenate(
        [other, jnp.zeros((24, LANES), F32)] + sum_rows(sums) + [jnp.zeros((8, LANES), F32)], axis=0
    ).astype(BF16)


def join_kernel(cols, keep, keep_sums, got, pair, send):
    levels = send.shape[0]
    model_d = send.shape[2]
    total = keep[...] + got[:cols, :].astype(F32)
    sums = keep_sums[...] + rows_sum(got[288:312, :].astype(F32))
    sums_r = sum_rows(sums)
    for z in range(levels):
        rows = pair[z].astype(F32)
        ext = [rows[:, model_d + b * LANES : model_d + (b + 1) * LANES] for b in range(EXT // LANES)]
        tall = jnp.concatenate([total] + ext + sums_r + [jnp.zeros((8, LANES), F32)], axis=0)
        wide = jnp.concatenate([tall[k * WIDE : (k + 1) * WIDE] for k in range(8)], axis=1)
        send[z] = jnp.concatenate([wide, rows[:, :model_d]], axis=0).astype(BF16)


def total_kernel(tiles, recv, send, rest):
    levels = recv.shape[0]
    total = recv[0, :WIDE, :].astype(F32)
    for z in range(1, levels):
        total = total + recv[z, :WIDE, :].astype(F32)
    tall = jnp.concatenate([total[:, k * LANES : (k + 1) * LANES] for k in range(8)], axis=0)
    slab = tall[:272].astype(BF16)
    for t in range(tiles):
        send[t] = slab
    rest[...] = tall[288:312]


def local_kernel(heads, scale, recv, sums_in, w_t, value, inputs, table, head):
    levels = recv.shape[0]
    model_d = w_t.shape[1]
    cols = w_t.shape[0]
    w = w_t[...]
    ext_rows, value_rows = [], []
    for z in range(levels):
        block = recv[z].astype(F32)
        tall = jnp.concatenate([block[:WIDE, k * LANES : (k + 1) * LANES] for k in range(8)], axis=0)
        ext_rows.append(
            jnp.concatenate([tall[264 + 8 * b : 272 + 8 * b] for b in range(EXT // LANES)], axis=1)
        )
        value_rows.append(block[WIDE:])
    ext = jnp.concatenate(ext_rows, axis=0).astype(BF16)[:, :cols]
    value[...] = jnp.concatenate(value_rows, axis=0).astype(BF16)
    inputs[...] = nn(ext, w).astype(BF16)
    sums = rows_sum(sums_in[...])
    high, low = split(sums[:, :cols])
    table[...] = (nn(high, w) + nn(low, w)) * scale
    both = sums[0:1] + sums[1:2]
    at = cols - heads
    rows = []
    for k in (2, 0, 4):
        lo = at + k * heads
        rows.append(both[:, lo : lo + heads] + both[:, lo + heads : lo + 2 * heads])
    head[...] = jnp.concatenate(rows, axis=0) * scale


def gather_kernel(cols, half, scale, core, own, other, out):
    tiles = own.shape[0]
    mine = core[0] == 0
    for t in range(tiles):
        a = own[t].astype(F32)
        b = other[t].astype(F32)
        first = jnp.where(mine, a, b)[:cols, :half]
        second = jnp.where(mine, b, a)[:cols, :half]
        out[:, 2 * half * t : 2 * half * (t + 1)] = jnp.concatenate([first, second], axis=1) * scale


VMEM = pl.BlockSpec(memory_space=pltpu.VMEM)
SMEM = pl.BlockSpec(memory_space=pltpu.SMEM)


def call(kernel, outs, ins, smem=0):
    return pl.pallas_call(
        kernel,
        out_shape=[jax.ShapeDtypeStruct(s, d) for s, d in outs],
        in_specs=[SMEM] * smem + [VMEM] * (len(ins) - smem),
        out_specs=[VMEM] * len(outs),
        compiler_params=pltpu.CompilerParams(vmem_limit_bytes=48 * 1024 * 1024),
    )(*ins)


def on_device(
    layer_input,
    head_input,
    out_grad,
    sensor_ids,
    valid_mask,
    sensor_table,
    proj_weight,
    step_bias,
    decay_log,
    skip_gain,
):
    pixel_dev, dates_dev, model_d = layer_input.shape
    heads = step_bias.shape[0]
    cols = proj_weight.shape[1]
    tiles = lax.axis_size("tile")
    dates = lax.axis_size("date")
    assert pixel_dev == dates and dates % 2 == 0
    levels = dates // 2
    length = dates * dates_dev
    slab = model_d // tiles
    half = slab // 2
    core = lax.axis_index("date") % 2
    core_s = core.astype(jnp.int32).reshape(1)
    w_t = proj_weight.T
    scale = 1.0 / math.sqrt(pixel_dev * dates_dev * tiles * dates)
    swap = [(i, i ^ 1) for i in range(dates)]
    planes = [[2 * z + c for z in range(levels)] for c in range(2)]

    is_second = (sensor_ids == 1)[None, :, None]
    sensor_embed = jnp.where(is_second, sensor_table[1], sensor_table[0])
    mixed_in = (layer_input.astype(F32) + sensor_embed).astype(BF16)
    mask_col = valid_mask.astype(BF16)[:, :, None]
    ids_col = jnp.broadcast_to(is_second.astype(BF16), mask_col.shape)
    aux = jnp.concatenate(
        [mask_col, ids_col, jnp.zeros((pixel_dev, dates_dev, LANES - 2), BF16)], axis=-1
    )
    packed = jnp.concatenate([mixed_in, head_input, out_grad, aux], axis=-1)
    series = lax.all_to_all(packed, "date", split_axis=0, concat_axis=0, tiled=True).reshape(
        length, 3 * model_d + LANES
    )

    width_p = model_d // heads
    params = jnp.zeros((16, LANES), F32)
    params = params.at[0, :heads].set(step_bias).at[1, :heads].set(decay_log)
    params = params.at[2 : 2 + heads, :].set(jnp.broadcast_to(skip_gain[:, None], (heads, LANES)))
    send_t, back, sel = call(
        functools.partial(series_kernel, heads, model_d, tiles, slab),
        [
            ((tiles, length, EXT + slab), BF16),
            ((length, model_d + EXT), BF16),
            ((16, length), BF16),
        ],
        [series, w_t, params],
    )
    recv_t = lax.all_to_all(send_t, "tile", split_axis=0, concat_axis=0, tiled=True)
    back = back.reshape(levels, 2, dates_dev, model_d + EXT)
    back_own = lax.dynamic_index_in_dim(back, core, 1, keepdims=False)
    back_give = lax.dynamic_index_in_dim(back, 1 - core, 1, keepdims=False)
    back_got = lax.ppermute(back_give, "date", swap)
    is_first = core == 0
    pair = jnp.concatenate(
        [jnp.where(is_first, back_own, back_got), jnp.where(is_first, back_got, back_own)], axis=1
    )

    keep, keep_sums, give = call(
        functools.partial(slab_kernel, cols),
        [((cols, LANES), F32), ((2, EXT), F32), ((SLAB_ROWS, LANES), BF16)],
        [core_s, recv_t, sel],
        1,
    )
    got = lax.ppermute(give, "date", swap)
    (send_z,) = call(
        functools.partial(join_kernel, cols),
        [((levels, WIDE + 2 * dates_dev, model_d), BF16)],
        [keep, keep_sums, got, pair],
    )
    recv_z = lax.all_to_all(
        send_z, "date", split_axis=0, concat_axis=0, tiled=True, axis_index_groups=planes
    )
    send_g, sums = call(
        functools.partial(total_kernel, tiles),
        [((tiles, 272, LANES), BF16), ((24, LANES), F32)],
        [recv_z],
    )
    recv_g = lax.all_to_all(send_g, "tile", split_axis=0, concat_axis=0, tiled=True)
    value, inputs, table, head = call(
        functools.partial(local_kernel, heads, scale),
        [
            ((length, model_d), BF16),
            ((length, model_d), BF16),
            ((2, model_d), F32),
            ((3, heads), F32),
        ],
        [recv_z, sums, w_t],
    )
    other_g = lax.ppermute(recv_g, "date", swap)
    (weight_t,) = call(
        functools.partial(gather_kernel, cols, half, scale),
        [((cols, model_d), F32)],
        [core_s, recv_g, other_g],
        1,
    )
    return (
        value.reshape(pixel_dev, dates_dev, model_d),
        inputs.reshape(pixel_dev, dates_dev, model_d),
        weight_t.T,
        table,
        head,
    )


def solution(mesh):
    in_specs = (
        P("tile", "date", None),
        P("tile", "date", None),
        P("tile", "date", None),
        P("date"),
        P("tile", "date"),
        P(),
        P(),
        P(),
        P(),
        P(),
    )
    out_specs = (P("tile", "date", None), P("tile", "date", None), P(), P(), P())
    return jax.shard_map(
        on_device, mesh=mesh, in_specs=in_specs, out_specs=out_specs, check_vma=False
    )
```

```python
import functools
import math

import jax
import jax.numpy as jnp
from jax import lax
from jax.experimental import pallas as pl
from jax.experimental.pallas import tpu as pltpu
from jax.sharding import PartitionSpec as P

NEG_FILL = -1e30
HIGHEST_PREC = lax.Precision.HIGHEST
F32 = jnp.float32
BF16 = jnp.bfloat16
LANES = 128
EXT = 384


def nt(a, b, precision=None):
    return lax.dot_general(
        a, b, (((1,), (1,)), ((), ())), preferred_element_type=F32, precision=precision
    )


def nn(a, b, precision=None):
    return lax.dot_general(
        a, b, (((1,), (0,)), ((), ())), preferred_element_type=F32, precision=precision
    )


def tn(a, b):
    return lax.dot_general(a, b, (((0,), (0,)), ((), ())), preferred_element_type=F32)


def split(x):
    high = x.astype(BF16)
    return high, (x - high.astype(F32)).astype(BF16)


def series_kernel(heads, model_d, dates, core, recv, w_t, params, send, own, give, sel):
    length = recv.shape[0]
    tiles, _, width = send.shape
    slab = width - EXT
    width_p = model_d // heads
    states = (w_t.shape[0] - heads) // 2
    mixed = recv[:, :model_d]
    aux = recv[:, 3 * model_d :].astype(F32)
    gate = aux[:, 0:1]
    ids = aux[:, 1:2]
    bias = params[:, :heads]
    rate = -jnp.exp(params[:, heads : 2 * heads])
    skip = params[:, 2 * heads : 3 * heads]
    projected = nt(mixed, w_t[...])
    keys = projected[:, :states].astype(BF16)
    reads = projected[:, states : 2 * states].astype(BF16)
    step_pre = projected[:, 2 * states :] + bias
    softplus = jnp.maximum(step_pre, 0.0) + jnp.log1p(jnp.exp(-jnp.abs(step_pre)))
    steps_b = (gate * softplus).astype(BF16)
    steps = steps_b.astype(F32)

    row = lax.broadcasted_iota(jnp.int32, (length, length), 0)
    col = lax.broadcasted_iota(jnp.int32, (length, length), 1)
    upper = col >= row
    upper_f = upper.astype(F32)
    eye = (col == row).astype(F32)
    lower_b = (row >= col).astype(BF16)
    head_row = lax.broadcasted_iota(jnp.int32, (heads, heads), 0)
    head_col = lax.broadcasted_iota(jnp.int32, (heads, heads), 1)
    eye_h = (head_row == head_col).astype(F32)
    rate_col = jnp.sum(eye_h * rate, axis=1, keepdims=True)
    log_col = nn(lower_b, steps_b) * rate
    steps_t = nt(eye_h.astype(BF16), steps_b).astype(BF16)
    log_row = nn(steps_t, upper.astype(BF16)) * rate_col
    scores_t = nt(keys, reads)

    pair_t = jnp.zeros((length, length), F32)
    value_parts, weighted_cols, read_rows, skip_cols = [], [], [], []
    for h in range(heads):
        lo = model_d + h * width_p
        x_h = recv[:, lo : lo + width_p]
        g_h = recv[:, lo + model_d : lo + model_d + width_p]
        dt_h = steps[:, h : h + 1]
        gap = log_row[h : h + 1, :] - log_col[:, h : h + 1]
        decay = jnp.exp(jnp.where(upper, gap, NEG_FILL))
        cross = nt(x_h, g_h)
        mix = decay * scores_t
        pair_t = pair_t + decay * cross * dt_h
        both = mix * cross
        weighted = jnp.sum(both, axis=1, keepdims=True)
        weighted_cols.append(weighted)
        read_rows.append(jnp.sum(both * dt_h, axis=0, keepdims=True))
        skip_cols.append(jnp.sum(cross * eye, axis=1, keepdims=True))
        value_parts.append(nn(mix.astype(BF16), g_h) * dt_h + skip[:, h : h + 1] * g_h.astype(F32))

    weighted = jnp.concatenate(weighted_cols, axis=1)
    read_sum = jnp.concatenate(read_rows, axis=0)
    skip_terms = jnp.concatenate(skip_cols, axis=1)
    later = nt(upper_f, read_sum, HIGHEST_PREC) - nn(upper_f, steps * weighted, HIGHEST_PREC)
    step_grad = (weighted + rate * later).astype(BF16).astype(F32)
    decay_terms = steps * later * rate
    pair_b = pair_t.astype(BF16)
    grad_keys = nn(pair_b, reads)
    grad_reads = tn(pair_b, keys)
    raw = step_grad * gate * jax.nn.sigmoid(step_pre)
    parts = []
    for term in (raw, decay_terms, skip_terms):
        high, low = split(term)
        parts += [high.astype(F32), low.astype(F32)]
    tail = jnp.concatenate(
        parts + [jnp.zeros((length, EXT - 2 * states - 6 * heads), F32)], axis=1
    )
    ext_f = jnp.concatenate([grad_keys, grad_reads, tail], axis=1)
    ext = ext_f.astype(BF16)
    back = jnp.concatenate(value_parts + [ext_f], axis=1)
    first = core[0] == 0
    own_rows, give_rows = [], []
    for at in range(0, length, 2 * dates):
        a, b = back[at : at + dates], back[at + dates : at + 2 * dates]
        own_rows.append(jnp.where(first, a, b))
        give_rows.append(jnp.where(first, b, a))
    own[...] = jnp.concatenate(own_rows, axis=0).astype(BF16)
    give[...] = jnp.concatenate(give_rows, axis=0).astype(BF16)
    for t in range(tiles):
        send[t, :, :EXT] = ext
        send[t, :, EXT:] = recv[:, t * slab : (t + 1) * slab]
    ids_row = jnp.sum(eye * ids, axis=0, keepdims=True)
    sel[...] = jnp.concatenate([1.0 - ids_row, ids_row, jnp.zeros((14, length), F32)], axis=0).astype(
        BF16
    )


def pack_kernel(ids_in, mask_in, table_in, layer, values, cotangent, out, ids, mask_t, table, layer_v, packed, sems):
    pixels, dates, model_d = layer.shape
    small = [
        pltpu.make_async_copy(ids_in, ids, sems.at[0]),
        pltpu.make_async_copy(mask_in, mask_t, sems.at[1]),
        pltpu.make_async_copy(table_in, table, sems.at[2]),
        pltpu.make_async_copy(layer, layer_v, sems.at[3]),
    ]
    large = [
        pltpu.make_async_copy(values, packed.at[:, :, model_d : 2 * model_d], sems.at[4]),
        pltpu.make_async_copy(cotangent, packed.at[:, :, 2 * model_d : 3 * model_d], sems.at[5]),
    ]
    for copy in small + large:
        copy.start()
    for copy in small:
        copy.wait()
    rows = [jnp.where(ids[i] == 1, table[1:2, :], table[0:1, :]) for i in range(dates)]
    embed = jnp.concatenate(rows, axis=0)
    row = lax.broadcasted_iota(jnp.int32, (dates, LANES), 0)
    lane = lax.broadcasted_iota(jnp.int32, (dates, LANES), 1)
    second = jnp.zeros((dates, LANES), F32)
    for i in range(dates):
        second = jnp.where((row == i) & (lane == 1), (ids[i] == 1).astype(F32), second)
    gate = mask_t[...].astype(F32)
    for p in range(pixels):
        packed[p, :, 3 * model_d :] = jnp.where(lane == 0, gate[:, p : p + 1], second).astype(BF16)
        packed[p, :, :model_d] = (layer_v[p].astype(F32) + embed).astype(BF16)
    for copy in large:
        copy.wait()
    store = pltpu.make_async_copy(packed, out, sems.at[0])
    store.start()
    store.wait()


def lane_pad(x, width):
    if x.shape[1] == width:
        return x
    return jnp.concatenate([x, jnp.zeros((x.shape[0], width - x.shape[1]), x.dtype)], axis=1)


def sum_rows(sums):
    high = sums.astype(BF16).astype(F32)
    low = (sums - high).astype(BF16).astype(F32)
    rows = jnp.concatenate([high, low, jnp.zeros((4, EXT), F32)], axis=0)
    return [rows[:, b * LANES : (b + 1) * LANES] for b in range(EXT // LANES)]


def rows_sum(block):
    rows = jnp.concatenate([block[8 * b : 8 * b + 8, :] for b in range(EXT // LANES)], axis=1)
    return rows[0:2] + rows[2:4]


def slab_kernel(cols, core, recv, sel, keep, keep_sums, give):
    tiles, length, width = recv.shape
    slab = width - EXT
    half = slab // 2
    ext = recv[:, :, :EXT].reshape(tiles * length, EXT)
    tokens = recv[:, :, EXT:].reshape(tiles * length, slab)
    part = tn(ext, tokens)[:cols]
    sums = jnp.zeros((16, EXT), F32)
    for t in range(tiles):
        sums = sums + nn(sel[...], recv[t, :, :EXT])
    sums = sums[0:2]
    mine = core[0] == 0
    first = lane_pad(part[:, :half], LANES)
    second = lane_pad(part[:, half:], LANES)
    keep[...] = jnp.where(mine, first, second)
    keep_sums[...] = sums
    other = jnp.where(mine, second, first)
    give[...] = jnp.concatenate(
        [other] + sum_rows(sums), axis=0
    ).astype(BF16)


def join_kernel(cols, dates, core, keep, keep_sums, got, own, other, send):
    levels = send.shape[0]
    first = core[0] == 0
    model_d = own.shape[1] - EXT
    total = keep[...] + got[:cols, :].astype(F32)
    sums = sum_rows(keep_sums[...] + rows_sum(got[cols : cols + 24, :].astype(F32)))
    pair_sums = jnp.concatenate([sums[0][:4], sums[1][:4]], axis=0)
    mine, theirs = own[...].astype(F32), other[...].astype(F32)
    firsts, seconds = jnp.where(first, mine, theirs), jnp.where(first, theirs, mine)
    lane = lax.broadcasted_iota(jnp.int32, (8, LANES), 1)
    last = pltpu.roll(sums[2], 64, 1)
    pad = [jnp.zeros((8, LANES), F32)] * ((send.shape[1] - cols - 32) // 8 - model_d // LANES)
    for z in range(levels):
        at = z * dates
        rows = jnp.concatenate([firsts[at : at + dates], seconds[at : at + dates]], axis=0)
        ext = [rows[:, model_d + b * LANES : model_d + (b + 1) * LANES] for b in range(EXT // LANES)]
        misc = jnp.where(lane < 64, ext[2], last)
        value = [rows[:, b * LANES : (b + 1) * LANES] for b in range(model_d // LANES)]
        send[z] = jnp.concatenate([total, ext[0], ext[1], misc, pair_sums] + value + pad, axis=0).astype(BF16)


def total_kernel(cols, recv, send, rest):
    levels = recv.shape[0]
    total = recv[0].astype(F32)
    for z in range(1, levels):
        total = total + recv[z].astype(F32)
    slab = total[:272].astype(BF16)
    for t in range(send.shape[0]):
        send[t] = slab
    rest[...] = total[cols + 16 : cols + 32]


def local_kernel(heads, scale, recv, rest, w_t, value, inputs, table, head):
    levels = recv.shape[0]
    model_d = w_t.shape[1]
    cols = w_t.shape[0]
    dates = value.shape[1]
    w = w_t[...]
    ext_rows = []
    for z in range(levels):
        rows = recv[z].astype(F32)
        ext_rows.append(jnp.concatenate([rows[cols + 8 * b : cols + 8 * b + 8] for b in range(3)], axis=1))
        at = cols + 32
        values = jnp.concatenate([rows[at + 8 * b : at + 8 * b + 8] for b in range(model_d // LANES)], axis=1)
        for c in range(2):
            value[2 * z + c] = values[c * dates : (c + 1) * dates].astype(BF16)
    grads = nn(jnp.concatenate(ext_rows, axis=0).astype(BF16)[:, :cols], w)
    for p in range(2 * levels):
        inputs[p] = grads[p * dates : (p + 1) * dates].astype(BF16)
    last = pltpu.roll(rest[0:8, :], 64, 1)
    sums = jnp.concatenate([rest[8:12, :], rest[12:16, :], last[0:4]], axis=1)
    sums = sums[0:2] + sums[2:4]
    high, low = split(sums[:, :cols])
    table[...] = (nn(high, w) + nn(low, w)) * scale
    both = sums[0:1] + sums[1:2]
    at = cols - heads
    rows = []
    for k in (2, 0, 4):
        lo = at + k * heads
        rows.append(both[:, lo : lo + heads] + both[:, lo + heads : lo + 2 * heads])
    head[...] = jnp.concatenate(rows, axis=0) * scale


def gather_kernel(cols, half, scale, core, own, other, out):
    tiles = own.shape[0]
    mine = core[0] == 0
    for t in range(tiles):
        a = own[t].astype(F32)
        b = other[t].astype(F32)
        first = jnp.where(mine, a, b)[:cols, :half]
        second = jnp.where(mine, b, a)[:cols, :half]
        out[:, 2 * half * t : 2 * half * (t + 1)] = jnp.concatenate([first, second], axis=1) * scale


VMEM = pl.BlockSpec(memory_space=pltpu.VMEM)
SMEM = pl.BlockSpec(memory_space=pltpu.SMEM)
HBM = pl.BlockSpec(memory_space=pltpu.HBM)


def call(kernel, outs, ins, smem=0):
    return pl.pallas_call(
        kernel,
        out_shape=[jax.ShapeDtypeStruct(s, d) for s, d in outs],
        in_specs=[SMEM] * smem + [VMEM] * (len(ins) - smem),
        out_specs=[VMEM] * len(outs),
        compiler_params=pltpu.CompilerParams(vmem_limit_bytes=48 * 1024 * 1024),
    )(*ins)


def on_device(
    layer_input,
    head_input,
    out_grad,
    sensor_ids,
    valid_mask,
    sensor_table,
    proj_weight,
    step_bias,
    decay_log,
    skip_gain,
):
    pixel_dev, dates_dev, model_d = layer_input.shape
    heads = step_bias.shape[0]
    cols = proj_weight.shape[1]
    tiles = lax.axis_size("tile")
    dates = lax.axis_size("date")
    assert pixel_dev == dates and dates % 2 == 0
    levels = dates // 2
    length = dates * dates_dev
    slab = model_d // tiles
    half = slab // 2
    core = lax.axis_index("date") % 2
    core_s = core.astype(jnp.int32).reshape(1)
    w_t = proj_weight.T
    scale = 1.0 / math.sqrt(pixel_dev * dates_dev * tiles * dates)
    swap = [(i, i ^ 1) for i in range(dates)]
    planes = [[2 * z + c for z in range(levels)] for c in range(2)]

    packed = pl.pallas_call(
        pack_kernel,
        out_shape=jax.ShapeDtypeStruct((pixel_dev, dates_dev, 3 * model_d + LANES), BF16),
        in_specs=[HBM] * 6,
        out_specs=HBM,
        scratch_shapes=[
            pltpu.SMEM((dates_dev,), jnp.int32),
            pltpu.VMEM((dates_dev, pixel_dev), jnp.int32),
            pltpu.VMEM((2, model_d), F32),
            pltpu.VMEM((pixel_dev, dates_dev, model_d), BF16),
            pltpu.VMEM((pixel_dev, dates_dev, 3 * model_d + LANES), BF16),
            pltpu.SemaphoreType.DMA((6,)),
        ],
        compiler_params=pltpu.CompilerParams(vmem_limit_bytes=64 * 1024 * 1024),
    )(sensor_ids, valid_mask.T, sensor_table, layer_input, head_input, out_grad)
    series = lax.all_to_all(packed, "date", split_axis=0, concat_axis=0, tiled=True).reshape(
        length, 3 * model_d + LANES
    )

    rows_core = length // 2
    send_t, own, give_rows, sel = call(
        functools.partial(series_kernel, heads, model_d, dates_dev),
        [
            ((tiles, length, EXT + slab), BF16),
            ((rows_core, model_d + EXT), BF16),
            ((rows_core, model_d + EXT), BF16),
            ((16, length), BF16),
        ],
        [core_s, series, w_t, jnp.concatenate([step_bias, decay_log, skip_gain])[None]],
        1,
    )
    recv_t = lax.all_to_all(send_t, "tile", split_axis=0, concat_axis=0, tiled=True)
    give_rows, recv_t = lax.optimization_barrier((give_rows, recv_t))
    other = lax.ppermute(give_rows, "date", swap)
    keep, keep_sums, give = call(
        functools.partial(slab_kernel, cols),
        [((cols, LANES), F32), ((2, EXT), F32), ((cols + 24, LANES), BF16)],
        [core_s, recv_t, sel],
        1,
    )
    got = lax.ppermute(give, "date", swap)
    rows_z = -(-(cols + 32 + model_d // 16) // 16) * 16
    (send_z,) = call(
        functools.partial(join_kernel, cols, dates_dev),
        [((levels, rows_z, LANES), BF16)],
        [core_s, keep, keep_sums, got, own, other],
        1,
    )
    recv_z = lax.all_to_all(
        send_z, "date", split_axis=0, concat_axis=0, tiled=True, axis_index_groups=planes
    )
    send_g, rest = call(
        functools.partial(total_kernel, cols),
        [((tiles, 272, LANES), BF16), ((16, LANES), F32)],
        [recv_z],
    )
    recv_g = lax.all_to_all(send_g, "tile", split_axis=0, concat_axis=0, tiled=True)
    value, inputs, table, head = call(
        functools.partial(local_kernel, heads, scale),
        [
            ((pixel_dev, dates_dev, model_d), BF16),
            ((pixel_dev, dates_dev, model_d), BF16),
            ((2, model_d), F32),
            ((3, heads), F32),
        ],
        [recv_z, rest, w_t],
    )
    other_g = lax.ppermute(recv_g, "date", swap)
    (weight_t,) = call(
        functools.partial(gather_kernel, cols, half, scale),
        [((cols, model_d), F32)],
        [core_s, recv_g, other_g],
        1,
    )
    return (
        value,
        inputs,
        weight_t.T,
        table,
        head,
    )


def solution(mesh):
    in_specs = (
        P("tile", "date", None),
        P("tile", "date", None),
        P("tile", "date", None),
        P("date"),
        P("tile", "date"),
        P(),
        P(),
        P(),
        P(),
        P(),
    )
    out_specs = (P("tile", "date", None), P("tile", "date", None), P(), P(), P())
    return jax.shard_map(
        on_device, mesh=mesh, in_specs=in_specs, out_specs=out_specs, check_vma=False
    )
```

```python
import functools
import math

import jax
import jax.numpy as jnp
from jax import lax
from jax.experimental import pallas as pl
from jax.experimental.pallas import tpu as pltpu
from jax.sharding import PartitionSpec as P

NEG_FILL = -1e30
HIGHEST_PREC = lax.Precision.HIGHEST
F32 = jnp.float32
BF16 = jnp.bfloat16
LANES = 128
EXT = 384


def nt(a, b, precision=None):
    return lax.dot_general(
        a, b, (((1,), (1,)), ((), ())), preferred_element_type=F32, precision=precision
    )


def nn(a, b, precision=None):
    return lax.dot_general(
        a, b, (((1,), (0,)), ((), ())), preferred_element_type=F32, precision=precision
    )


def tn(a, b):
    return lax.dot_general(a, b, (((0,), (0,)), ((), ())), preferred_element_type=F32)


def split(x):
    high = x.astype(BF16)
    return high, (x - high.astype(F32)).astype(BF16)


def series_kernel(heads, model_d, dates, core, recv, w_t, send, own, give, sel):
    length = recv.shape[0]
    tiles, _, width = send.shape
    slab = width - EXT
    width_p = model_d // heads
    states = (w_t.shape[0] - heads) // 2
    mixed = recv[:, :model_d]
    aux = recv[:, 3 * model_d :].astype(F32)
    gate = aux[:, 0:1]
    ids = aux[:, 1:2]
    params = []
    for at in range(2, 2 + 9 * heads, 3 * heads):
        params.append(sum(aux[0:1, at + k * heads : at + (k + 1) * heads] for k in range(3)))
    bias, rate, skip = params[0], -jnp.exp(params[1]), params[2]
    projected = nt(mixed, w_t[...])
    keys = projected[:, :states].astype(BF16)
    reads = projected[:, states : 2 * states].astype(BF16)
    step_pre = projected[:, 2 * states :] + bias
    softplus = jnp.maximum(step_pre, 0.0) + jnp.log1p(jnp.exp(-jnp.abs(step_pre)))
    steps_b = (gate * softplus).astype(BF16)
    steps = steps_b.astype(F32)

    row = lax.broadcasted_iota(jnp.int32, (length, length), 0)
    col = lax.broadcasted_iota(jnp.int32, (length, length), 1)
    upper = col >= row
    upper_f = upper.astype(F32)
    eye = (col == row).astype(F32)
    lower_b = (row >= col).astype(BF16)
    head_row = lax.broadcasted_iota(jnp.int32, (heads, heads), 0)
    head_col = lax.broadcasted_iota(jnp.int32, (heads, heads), 1)
    eye_h = (head_row == head_col).astype(F32)
    rate_col = jnp.sum(eye_h * rate, axis=1, keepdims=True)
    log_col = nn(lower_b, steps_b) * rate
    steps_t = nt(eye_h.astype(BF16), steps_b).astype(BF16)
    log_row = nn(steps_t, upper.astype(BF16)) * rate_col
    scores_t = nt(keys, reads)

    pair_t = jnp.zeros((length, length), F32)
    value_parts, weighted_cols, read_rows, skip_cols = [], [], [], []
    for h in range(heads):
        lo = model_d + h * width_p
        x_h = recv[:, lo : lo + width_p]
        g_h = recv[:, lo + model_d : lo + model_d + width_p]
        dt_h = steps[:, h : h + 1]
        gap = log_row[h : h + 1, :] - log_col[:, h : h + 1]
        decay = jnp.exp(jnp.where(upper, gap, NEG_FILL))
        cross = nt(x_h, g_h)
        mix = decay * scores_t
        pair_t = pair_t + decay * cross * dt_h
        both = mix * cross
        weighted = jnp.sum(both, axis=1, keepdims=True)
        weighted_cols.append(weighted)
        read_rows.append(jnp.sum(both * dt_h, axis=0, keepdims=True))
        skip_cols.append(jnp.sum(cross * eye, axis=1, keepdims=True))
        value_parts.append(nn(mix.astype(BF16), g_h) * dt_h + skip[:, h : h + 1] * g_h.astype(F32))

    weighted = jnp.concatenate(weighted_cols, axis=1)
    read_sum = jnp.concatenate(read_rows, axis=0)
    skip_terms = jnp.concatenate(skip_cols, axis=1)
    later = nt(upper_f, read_sum, HIGHEST_PREC) - nn(upper_f, steps * weighted, HIGHEST_PREC)
    step_grad = (weighted + rate * later).astype(BF16).astype(F32)
    decay_terms = steps * later * rate
    pair_b = pair_t.astype(BF16)
    grad_keys = nn(pair_b, reads)
    grad_reads = tn(pair_b, keys)
    raw = step_grad * gate * jax.nn.sigmoid(step_pre)
    parts = []
    for term in (raw, decay_terms, skip_terms):
        high, low = split(term)
        parts += [high.astype(F32), low.astype(F32)]
    tail = jnp.concatenate(
        parts + [jnp.zeros((length, EXT - 2 * states - 6 * heads), F32)], axis=1
    )
    ext_f = jnp.concatenate([grad_keys, grad_reads, tail], axis=1)
    ext = ext_f.astype(BF16)
    back = jnp.concatenate(value_parts + [ext_f], axis=1)
    first = core[0] == 0
    own_rows, give_rows = [], []
    for at in range(0, length, 2 * dates):
        a, b = back[at : at + dates], back[at + dates : at + 2 * dates]
        own_rows.append(jnp.where(first, a, b))
        give_rows.append(jnp.where(first, b, a))
    own[...] = jnp.concatenate(own_rows, axis=0).astype(BF16)
    give[...] = jnp.concatenate(give_rows, axis=0).astype(BF16)
    for t in range(tiles):
        send[t, :, :EXT] = ext
        send[t, :, EXT:] = recv[:, t * slab : (t + 1) * slab]
    ids_row = jnp.sum(eye * ids, axis=0, keepdims=True)
    sel[...] = jnp.concatenate([1.0 - ids_row, ids_row, jnp.zeros((14, length), F32)], axis=0).astype(
        BF16
    )


def pack_kernel(core, ids_in, mask_in, table_in, bias_in, decay_in, skip_in, layer, values, cotangent, out, ids, mask_t, table, params, layer_v, sems):
    pixels, dates, model_d = layer.shape
    small = [
        pltpu.make_async_copy(ids_in, ids, sems.at[0]),
        pltpu.make_async_copy(mask_in, mask_t, sems.at[1]),
        pltpu.make_async_copy(table_in, table, sems.at[2]),
        pltpu.make_async_copy(layer, layer_v, sems.at[3]),
        pltpu.make_async_copy(bias_in, params.at[0:1], sems.at[6]),
        pltpu.make_async_copy(decay_in, params.at[1:2], sems.at[7]),
        pltpu.make_async_copy(skip_in, params.at[2:3], sems.at[8]),
    ]
    large = [
        pltpu.make_async_copy(values, out.at[:, :, model_d : 2 * model_d], sems.at[4]),
        pltpu.make_async_copy(cotangent, out.at[:, :, 2 * model_d : 3 * model_d], sems.at[5]),
    ]
    for copy in small + large:
        copy.start()
    for copy in small:
        copy.wait()
    rows = [jnp.where(ids[i] == 1, table[1:2, :], table[0:1, :]) for i in range(dates)]
    embed = jnp.concatenate(rows, axis=0)
    row = lax.broadcasted_iota(jnp.int32, (dates, LANES), 0)
    lane = lax.broadcasted_iota(jnp.int32, (dates, LANES), 1)
    second = jnp.zeros((dates, LANES), F32)
    for i in range(dates):
        second = jnp.where((row == i) & (lane == 1), (ids[i] == 1).astype(F32), second)
    gate = mask_t[...].astype(F32)
    at = 2
    for k in range(3):
        rest = params[k : k + 1, :]
        for _ in range(3):
            term = rest.astype(BF16).astype(F32)
            rest = rest - term
            term = jnp.concatenate([jnp.zeros((1, at), F32), term, jnp.zeros((1, LANES - at - term.shape[1]), F32)], axis=1)
            second = second + term
            at = at + params.shape[1]
    for p in range(pixels):
        out[p, :, 3 * model_d :] = jnp.where(lane == 0, gate[:, p : p + 1], second).astype(BF16)
        out[p, :, :model_d] = (layer_v[p].astype(F32) + embed).astype(BF16)
    for copy in large:
        copy.wait()


def lane_pad(x, width):
    if x.shape[1] == width:
        return x
    return jnp.concatenate([x, jnp.zeros((x.shape[0], width - x.shape[1]), x.dtype)], axis=1)


def sum_rows(sums):
    high = sums.astype(BF16).astype(F32)
    low = (sums - high).astype(BF16).astype(F32)
    rows = jnp.concatenate([high, low, jnp.zeros((4, EXT), F32)], axis=0)
    return [rows[:, b * LANES : (b + 1) * LANES] for b in range(EXT // LANES)]


def rows_sum(block):
    rows = jnp.concatenate([block[8 * b : 8 * b + 8, :] for b in range(EXT // LANES)], axis=1)
    return rows[0:2] + rows[2:4]


def slab_kernel(cols, core, recv, sel, rows, keep, keep_sums, give):
    tiles, length, width = recv.shape
    slab = width - EXT
    half = slab // 2
    ext = recv[:, :, :EXT].reshape(tiles * length, EXT)
    tokens = recv[:, :, EXT:].reshape(tiles * length, slab)
    part = tn(ext, tokens)[:cols]
    sums = jnp.zeros((16, EXT), F32)
    for t in range(tiles):
        sums = sums + nn(sel[...], recv[t, :, :EXT])
    sums = sums[0:2]
    mine = core[0] == 0
    first = lane_pad(part[:, :half], LANES)
    second = lane_pad(part[:, half:], LANES)
    keep[...] = jnp.where(mine, first, second)
    keep_sums[...] = sums
    other = jnp.where(mine, second, first)
    blocks = [rows[:, b * LANES : (b + 1) * LANES].astype(F32) for b in range(rows.shape[1] // LANES)]
    give[...] = jnp.concatenate([other] + sum_rows(sums) + blocks, axis=0).astype(BF16)


def join_kernel(cols, dates, core, keep, keep_sums, got, own, send):
    levels = send.shape[0]
    first = core[0] == 0
    model_d = own.shape[1] - EXT
    total = keep[...] + got[:cols, :].astype(F32)
    sums = sum_rows(keep_sums[...] + rows_sum(got[cols : cols + 24, :].astype(F32)))
    pair_sums = jnp.concatenate([sums[0][:4], sums[1][:4]], axis=0)
    mine, count = own[...].astype(F32), own.shape[0]
    tall = got[cols + 24 :, :].astype(F32)
    theirs = jnp.concatenate([tall[k : k + count] for k in range(0, tall.shape[0], count)], axis=1)
    firsts, seconds = jnp.where(first, mine, theirs), jnp.where(first, theirs, mine)
    lane = lax.broadcasted_iota(jnp.int32, (8, LANES), 1)
    last = pltpu.roll(sums[2], 64, 1)
    pad = [jnp.zeros((8, LANES), F32)] * ((send.shape[1] - cols - 32) // 8 - model_d // LANES)
    for z in range(levels):
        at = z * dates
        rows = jnp.concatenate([firsts[at : at + dates], seconds[at : at + dates]], axis=0)
        ext = [rows[:, model_d + b * LANES : model_d + (b + 1) * LANES] for b in range(EXT // LANES)]
        misc = jnp.where(lane < 64, ext[2], last)
        value = [rows[:, b * LANES : (b + 1) * LANES] for b in range(model_d // LANES)]
        send[z] = jnp.concatenate([total, ext[0], ext[1], misc, pair_sums] + value + pad, axis=0).astype(BF16)


def total_kernel(cols, recv, send, rest):
    levels = recv.shape[0]
    total = recv[0].astype(F32)
    for z in range(1, levels):
        total = total + recv[z].astype(F32)
    slab = total[:272].astype(BF16)
    for t in range(send.shape[0]):
        send[t] = slab
    rest[...] = total[cols + 16 : cols + 32]


def store_half(cols, scale, core, half, slabs, weight, held, sems):
    copies = []
    for t in range(slabs.shape[0]):
        held[t] = slabs[t].astype(F32)[:cols] * scale
        at = pl.multiple_of((2 * t + core) * half, half)
        copies.append(pltpu.make_async_copy(held.at[t], weight.at[:, pl.ds(at, half)], sems.at[t]))
        copies[-1].start()
    return copies


def half_kernel(cols, scale, half, core, slabs, weight_in, weight, held, sems):
    for copy in store_half(cols, scale, 1 - core[0], half, slabs, weight, held, sems):
        copy.wait()


def local_weight_kernel(heads, scale, cols, half, core, slabs, recv, rest, w_t, *refs):
    outs, held_outs = refs[:5], refs[5:10]
    held, sems, out_sems = held_outs[4], refs[10], refs[11]
    copies = store_half(cols, scale, core[0], half, slabs, outs[4], held, sems)
    moves = [pltpu.make_async_copy(held_outs[k], outs[k], out_sems.at[k]) for k in range(4)]
    local_kernel(heads, scale, recv, rest, w_t, *held_outs[:4], moves)
    for copy in copies + moves:
        copy.wait()


def local_kernel(heads, scale, recv, rest, w_t, value, inputs, table, head, moves=()):
    levels = recv.shape[0]
    model_d = w_t.shape[1]
    cols = w_t.shape[0]
    dates = value.shape[1]
    w = w_t[...]
    ext_rows = []
    for z in range(levels):
        rows = recv[z].astype(F32)
        ext_rows.append(jnp.concatenate([rows[cols + 8 * b : cols + 8 * b + 8] for b in range(3)], axis=1))
        at = cols + 32
        values = jnp.concatenate([rows[at + 8 * b : at + 8 * b + 8] for b in range(model_d // LANES)], axis=1)
        for c in range(2):
            value[2 * z + c] = values[c * dates : (c + 1) * dates].astype(BF16)
    for move in moves[:1]:
        move.start()
    grads = nn(jnp.concatenate(ext_rows, axis=0).astype(BF16)[:, :cols], w)
    for p in range(2 * levels):
        inputs[p] = grads[p * dates : (p + 1) * dates].astype(BF16)
    for move in moves[1:2]:
        move.start()
    last = pltpu.roll(rest[0:8, :], 64, 1)
    sums = jnp.concatenate([rest[8:12, :], rest[12:16, :], last[0:4]], axis=1)
    sums = sums[0:2] + sums[2:4]
    high, low = split(sums[:, :cols])
    table[...] = (nn(high, w) + nn(low, w)) * scale
    both = sums[0:1] + sums[1:2]
    at = cols - heads
    rows = []
    for k in (2, 0, 4):
        lo = at + k * heads
        rows.append(both[:, lo : lo + heads] + both[:, lo + heads : lo + 2 * heads])
    head[...] = jnp.concatenate(rows, axis=0) * scale
    for move in moves[2:]:
        move.start()


def gather_kernel(cols, half, scale, core, own, other, out):
    tiles = own.shape[0]
    mine = core[0] == 0
    for t in range(tiles):
        a = own[t].astype(F32)
        b = other[t].astype(F32)
        first = jnp.where(mine, a, b)[:cols, :half]
        second = jnp.where(mine, b, a)[:cols, :half]
        out[:, 2 * half * t : 2 * half * (t + 1)] = jnp.concatenate([first, second], axis=1) * scale


VMEM = pl.BlockSpec(memory_space=pltpu.VMEM)
SMEM = pl.BlockSpec(memory_space=pltpu.SMEM)
HBM = pl.BlockSpec(memory_space=pltpu.HBM)


def call(kernel, outs, ins, smem=0):
    return pl.pallas_call(
        kernel,
        out_shape=[jax.ShapeDtypeStruct(s, d) for s, d in outs],
        in_specs=[SMEM] * smem + [VMEM] * (len(ins) - smem),
        out_specs=[VMEM] * len(outs),
        compiler_params=pltpu.CompilerParams(vmem_limit_bytes=48 * 1024 * 1024),
    )(*ins)


def on_device(
    layer_input,
    head_input,
    out_grad,
    sensor_ids,
    valid_mask,
    sensor_table,
    proj_weight,
    step_bias,
    decay_log,
    skip_gain,
):
    pixel_dev, dates_dev, model_d = layer_input.shape
    heads = step_bias.shape[0]
    cols = proj_weight.shape[1]
    tiles = lax.axis_size("tile")
    dates = lax.axis_size("date")
    assert pixel_dev == dates and dates % 2 == 0
    levels = dates // 2
    length = dates * dates_dev
    slab = model_d // tiles
    half = slab // 2
    core = lax.axis_index("date") % 2
    core_s = core.astype(jnp.int32).reshape(1)
    w_t = proj_weight.T
    scale = 1.0 / math.sqrt(pixel_dev * dates_dev * tiles * dates)
    swap = [(i, i ^ 1) for i in range(dates)]
    planes = [[2 * z + c for z in range(levels)] for c in range(2)]

    operands = [
        sensor_ids,
        valid_mask.T,
        sensor_table,
        step_bias[None],
        decay_log[None],
        skip_gain[None],
        layer_input,
        head_input,
        out_grad,
    ]
    packed = pl.pallas_call(
        pack_kernel,
        out_shape=jax.ShapeDtypeStruct((pixel_dev, dates_dev, 3 * model_d + LANES), BF16),
        in_specs=[SMEM] + [HBM] * 9,
        out_specs=VMEM,
        scratch_shapes=[
            pltpu.SMEM((dates_dev,), jnp.int32),
            pltpu.VMEM((dates_dev, pixel_dev), jnp.int32),
            pltpu.VMEM((2, model_d), F32),
            pltpu.VMEM((3, heads), F32),
            pltpu.VMEM((pixel_dev, dates_dev, model_d), BF16),
            pltpu.SemaphoreType.DMA((9,)),
        ],
        compiler_params=pltpu.CompilerParams(vmem_limit_bytes=16 * 1024 * 1024),
    )(core_s, *[pltpu.with_memory_space_constraint(operand, pltpu.HBM) for operand in operands])
    series = lax.all_to_all(packed, "date", split_axis=0, concat_axis=0, tiled=True).reshape(
        length, 3 * model_d + LANES
    )

    rows_core = length // 2
    send_t, own, give_rows, sel = call(
        functools.partial(series_kernel, heads, model_d, dates_dev),
        [
            ((tiles, length, EXT + slab), BF16),
            ((rows_core, model_d + EXT), BF16),
            ((rows_core, model_d + EXT), BF16),
            ((16, length), BF16),
        ],
        [core_s, series, w_t],
        1,
    )
    recv_t = lax.all_to_all(send_t, "tile", split_axis=0, concat_axis=0, tiled=True)
    rows_give = cols + 24 + rows_core * (model_d + EXT) // LANES
    keep, keep_sums, give = call(
        functools.partial(slab_kernel, cols),
        [((cols, LANES), F32), ((2, EXT), F32), ((rows_give, LANES), BF16)],
        [core_s, recv_t, sel, give_rows],
        1,
    )
    got = lax.ppermute(give, "date", swap)
    rows_z = -(-(cols + 32 + model_d // 16) // 16) * 16
    (send_z,) = call(
        functools.partial(join_kernel, cols, dates_dev),
        [((levels, rows_z, LANES), BF16)],
        [core_s, keep, keep_sums, got, own],
        1,
    )
    recv_z = lax.all_to_all(
        send_z, "date", split_axis=0, concat_axis=0, tiled=True, axis_index_groups=planes
    )
    send_g, rest = call(
        functools.partial(total_kernel, cols),
        [((tiles, 272, LANES), BF16), ((16, LANES), F32)],
        [recv_z],
    )
    recv_g = lax.all_to_all(send_g, "tile", split_axis=0, concat_axis=0, tiled=True)
    local_outs = [
        ((pixel_dev, dates_dev, model_d), BF16),
        ((pixel_dev, dates_dev, model_d), BF16),
        ((2, model_d), F32),
        ((3, heads), F32),
    ]
    other_g = lax.ppermute(recv_g, "date", swap)
    if half % LANES == 0:
        weight_shape = jax.ShapeDtypeStruct((cols, model_d), F32)
        held = [pltpu.VMEM((tiles, cols, half), F32), pltpu.SemaphoreType.DMA((tiles,))]
        limit = pltpu.CompilerParams(vmem_limit_bytes=48 * 1024 * 1024)
        value, inputs, table, head, weight_t = pl.pallas_call(
            functools.partial(local_weight_kernel, heads, scale, cols, half),
            out_shape=[jax.ShapeDtypeStruct(s, d) for s, d in local_outs] + [weight_shape],
            in_specs=[SMEM] + [VMEM] * 4,
            out_specs=[HBM] * 5,
            scratch_shapes=[pltpu.VMEM(s, d) for s, d in local_outs]
            + held
            + [pltpu.SemaphoreType.DMA((4,))],
            compiler_params=limit,
        )(core_s, recv_g, recv_z, rest, w_t)
        weight_t = pl.pallas_call(
            functools.partial(half_kernel, cols, scale, half),
            out_shape=weight_shape,
            in_specs=[SMEM, VMEM, HBM],
            out_specs=HBM,
            scratch_shapes=held,
            input_output_aliases={2: 0},
            compiler_params=limit,
        )(core_s, other_g, weight_t)
    else:
        value, inputs, table, head = call(
            functools.partial(local_kernel, heads, scale), local_outs, [recv_z, rest, w_t]
        )
        (weight_t,) = call(
            functools.partial(gather_kernel, cols, half, scale),
            [((cols, model_d), F32)],
            [core_s, recv_g, other_g],
            1,
        )
    return (
        value,
        inputs,
        weight_t.T,
        table,
        head,
    )


def solution(mesh):
    in_specs = (
        P("tile", "date", None),
        P("tile", "date", None),
        P("tile", "date", None),
        P("date"),
        P("tile", "date"),
        P(),
        P(),
        P(),
        P(),
        P(),
    )
    out_specs = (P("tile", "date", None), P("tile", "date", None), P(), P(), P())
    return jax.shard_map(
        on_device, mesh=mesh, in_specs=in_specs, out_specs=out_specs, check_vma=False
    )
```

```python
import functools
import math

import jax
import jax.numpy as jnp
from jax import lax
from jax.experimental import pallas as pl
from jax.experimental.pallas import tpu as pltpu
from jax.sharding import PartitionSpec as P

NEG_FILL = -1e30
HIGHEST_PREC = lax.Precision.HIGHEST
F32 = jnp.float32
BF16 = jnp.bfloat16
LANES = 128
EXT = 384


def nt(a, b, precision=None):
    return lax.dot_general(
        a, b, (((1,), (1,)), ((), ())), preferred_element_type=F32, precision=precision
    )


def nn(a, b, precision=None):
    return lax.dot_general(
        a, b, (((1,), (0,)), ((), ())), preferred_element_type=F32, precision=precision
    )


def tn(a, b):
    return lax.dot_general(a, b, (((0,), (0,)), ((), ())), preferred_element_type=F32)


def split(x):
    high = x.astype(BF16)
    return high, (x - high.astype(F32)).astype(BF16)


def series_kernel(heads, model_d, dates, core, recv, w_t, send, own, give, sel):
    length = recv.shape[0]
    tiles, _, width = send.shape
    slab = width - EXT
    width_p = model_d // heads
    states = (w_t.shape[0] - heads) // 2
    mixed = recv[:, :model_d]
    aux = recv[:, 3 * model_d :].astype(F32)
    gate = aux[:, 0:1]
    ids = aux[:, 1:2]
    params = []
    for at in range(2, 2 + 9 * heads, 3 * heads):
        params.append(sum(aux[0:1, at + k * heads : at + (k + 1) * heads] for k in range(3)))
    bias, rate, skip = params[0], -jnp.exp(params[1]), params[2]
    projected = nt(mixed, w_t[...])
    keys = projected[:, :states].astype(BF16)
    reads = projected[:, states : 2 * states].astype(BF16)
    step_pre = projected[:, 2 * states :] + bias
    softplus = jnp.maximum(step_pre, 0.0) + jnp.log1p(jnp.exp(-jnp.abs(step_pre)))
    steps_b = (gate * softplus).astype(BF16)
    steps = steps_b.astype(F32)

    row = lax.broadcasted_iota(jnp.int32, (length, length), 0)
    col = lax.broadcasted_iota(jnp.int32, (length, length), 1)
    upper = col >= row
    upper_f = upper.astype(F32)
    eye = (col == row).astype(F32)
    lower_b = (row >= col).astype(BF16)
    head_row = lax.broadcasted_iota(jnp.int32, (heads, heads), 0)
    head_col = lax.broadcasted_iota(jnp.int32, (heads, heads), 1)
    eye_h = (head_row == head_col).astype(F32)
    rate_col = jnp.sum(eye_h * rate, axis=1, keepdims=True)
    log_col = nn(lower_b, steps_b) * rate
    steps_t = nt(eye_h.astype(BF16), steps_b).astype(BF16)
    log_row = nn(steps_t, upper.astype(BF16)) * rate_col
    scores_t = nt(keys, reads)

    pair_t = jnp.zeros((length, length), F32)
    value_parts, weighted_cols, read_rows, skip_cols = [], [], [], []
    for h in range(heads):
        lo = model_d + h * width_p
        x_h = recv[:, lo : lo + width_p]
        g_h = recv[:, lo + model_d : lo + model_d + width_p]
        dt_h = steps[:, h : h + 1]
        gap = log_row[h : h + 1, :] - log_col[:, h : h + 1]
        decay = jnp.exp(jnp.where(upper, gap, NEG_FILL))
        cross = nt(x_h, g_h)
        mix = decay * scores_t
        pair_t = pair_t + decay * cross * dt_h
        both = mix * cross
        weighted = jnp.sum(both, axis=1, keepdims=True)
        weighted_cols.append(weighted)
        read_rows.append(jnp.sum(both * dt_h, axis=0, keepdims=True))
        skip_cols.append(jnp.sum(cross * eye, axis=1, keepdims=True))
        value_parts.append(nn(mix.astype(BF16), g_h) * dt_h + skip[:, h : h + 1] * g_h.astype(F32))

    weighted = jnp.concatenate(weighted_cols, axis=1)
    read_sum = jnp.concatenate(read_rows, axis=0)
    skip_terms = jnp.concatenate(skip_cols, axis=1)
    later = nt(upper_f, read_sum, HIGHEST_PREC) - nn(upper_f, steps * weighted, HIGHEST_PREC)
    step_grad = (weighted + rate * later).astype(BF16).astype(F32)
    decay_terms = steps * later * rate
    pair_b = pair_t.astype(BF16)
    grad_keys = nn(pair_b, reads)
    grad_reads = tn(pair_b, keys)
    raw = step_grad * gate * jax.nn.sigmoid(step_pre)
    parts = []
    for term in (raw, decay_terms, skip_terms):
        high, low = split(term)
        parts += [high.astype(F32), low.astype(F32)]
    tail = jnp.concatenate(
        parts + [jnp.zeros((length, EXT - 2 * states - 6 * heads), F32)], axis=1
    )
    ext_f = jnp.concatenate([grad_keys, grad_reads, tail], axis=1)
    ext = ext_f.astype(BF16)
    back = jnp.concatenate(value_parts + [ext_f], axis=1)
    first = core[0] == 0
    own_rows, give_rows = [], []
    for at in range(0, length, 2 * dates):
        a, b = back[at : at + dates], back[at + dates : at + 2 * dates]
        own_rows.append(jnp.where(first, a, b))
        give_rows.append(jnp.where(first, b, a))
    own[...] = jnp.concatenate(own_rows, axis=0).astype(BF16)
    give[...] = jnp.concatenate(give_rows, axis=0).astype(BF16)
    for t in range(tiles):
        send[t, :, :EXT] = ext
        send[t, :, EXT:] = recv[:, t * slab : (t + 1) * slab]
    ids_row = jnp.sum(eye * ids, axis=0, keepdims=True)
    sel[...] = jnp.concatenate([1.0 - ids_row, ids_row, jnp.zeros((14, length), F32)], axis=0).astype(
        BF16
    )


def pack_kernel(core, ids_in, mask_in, table_in, bias_in, decay_in, skip_in, layer, values, cotangent, out, ids, mask_t, table, params, layer_v, sems):
    pixels, dates, model_d = layer.shape
    small = [
        pltpu.make_async_copy(ids_in, ids, sems.at[0]),
        pltpu.make_async_copy(mask_in, mask_t, sems.at[1]),
        pltpu.make_async_copy(table_in, table, sems.at[2]),
        pltpu.make_async_copy(layer, layer_v, sems.at[3]),
        pltpu.make_async_copy(bias_in, params.at[0:1], sems.at[6]),
        pltpu.make_async_copy(decay_in, params.at[1:2], sems.at[7]),
        pltpu.make_async_copy(skip_in, params.at[2:3], sems.at[8]),
    ]
    large = [
        pltpu.make_async_copy(values, out.at[:, :, model_d : 2 * model_d], sems.at[4]),
        pltpu.make_async_copy(cotangent, out.at[:, :, 2 * model_d : 3 * model_d], sems.at[5]),
    ]
    for copy in small + large:
        copy.start()
    for copy in small:
        copy.wait()
    rows = [jnp.where(ids[i] == 1, table[1:2, :], table[0:1, :]) for i in range(dates)]
    embed = jnp.concatenate(rows, axis=0)
    row = lax.broadcasted_iota(jnp.int32, (dates, LANES), 0)
    lane = lax.broadcasted_iota(jnp.int32, (dates, LANES), 1)
    second = jnp.zeros((dates, LANES), F32)
    for i in range(dates):
        second = jnp.where((row == i) & (lane == 1), (ids[i] == 1).astype(F32), second)
    gate = mask_t[...].astype(F32)
    at = 2
    for k in range(3):
        rest = params[k : k + 1, :]
        for _ in range(3):
            term = rest.astype(BF16).astype(F32)
            rest = rest - term
            term = jnp.concatenate([jnp.zeros((1, at), F32), term, jnp.zeros((1, LANES - at - term.shape[1]), F32)], axis=1)
            second = second + term
            at = at + params.shape[1]
    for p in range(pixels):
        out[p, :, 3 * model_d :] = jnp.where(lane == 0, gate[:, p : p + 1], second).astype(BF16)
        out[p, :, :model_d] = (layer_v[p].astype(F32) + embed).astype(BF16)
    for copy in large:
        copy.wait()


def lane_pad(x, width):
    if x.shape[1] == width:
        return x
    return jnp.concatenate([x, jnp.zeros((x.shape[0], width - x.shape[1]), x.dtype)], axis=1)


def sum_rows(sums):
    high = sums.astype(BF16).astype(F32)
    low = (sums - high).astype(BF16).astype(F32)
    rows = jnp.concatenate([high, low, jnp.zeros((4, EXT), F32)], axis=0)
    return [rows[:, b * LANES : (b + 1) * LANES] for b in range(EXT // LANES)]


def rows_sum(block):
    rows = jnp.concatenate([block[8 * b : 8 * b + 8, :] for b in range(EXT // LANES)], axis=1)
    return rows[0:2] + rows[2:4]


def slab_kernel(cols, core, recv, sel, rows, keep, keep_sums, give):
    tiles, length, width = recv.shape
    slab = width - EXT
    half = slab // 2
    ext = recv[:, :, :EXT].reshape(tiles * length, EXT)
    tokens = recv[:, :, EXT:].reshape(tiles * length, slab)
    part = tn(ext, tokens)[:cols]
    sums = jnp.zeros((16, EXT), F32)
    for t in range(tiles):
        sums = sums + nn(sel[...], recv[t, :, :EXT])
    sums = sums[0:2]
    mine = core[0] == 0
    first = lane_pad(part[:, :half], LANES)
    second = lane_pad(part[:, half:], LANES)
    keep[...] = jnp.where(mine, first, second)
    keep_sums[...] = sums
    other = jnp.where(mine, second, first)
    blocks = [rows[:, b * LANES : (b + 1) * LANES].astype(F32) for b in range(rows.shape[1] // LANES)]
    give[...] = jnp.concatenate([other] + sum_rows(sums) + blocks, axis=0).astype(BF16)


def join_kernel(cols, dates, core, keep, keep_sums, got, own, send):
    levels = send.shape[0]
    first = core[0] == 0
    model_d = own.shape[1] - EXT
    total = keep[...] + got[:cols, :].astype(F32)
    sums = sum_rows(keep_sums[...] + rows_sum(got[cols : cols + 24, :].astype(F32)))
    pair_sums = jnp.concatenate([sums[0][:4], sums[1][:4]], axis=0)
    mine, count = own[...].astype(F32), own.shape[0]
    tall = got[cols + 24 :, :].astype(F32)
    theirs = jnp.concatenate([tall[k : k + count] for k in range(0, tall.shape[0], count)], axis=1)
    firsts, seconds = jnp.where(first, mine, theirs), jnp.where(first, theirs, mine)
    lane = lax.broadcasted_iota(jnp.int32, (8, LANES), 1)
    last = pltpu.roll(sums[2], 64, 1)
    pad = [jnp.zeros((8, LANES), F32)] * ((send.shape[1] - cols - 32) // 8 - model_d // LANES)
    for z in range(levels):
        at = z * dates
        rows = jnp.concatenate([firsts[at : at + dates], seconds[at : at + dates]], axis=0)
        ext = [rows[:, model_d + b * LANES : model_d + (b + 1) * LANES] for b in range(EXT // LANES)]
        misc = jnp.where(lane < 64, ext[2], last)
        value = [rows[:, b * LANES : (b + 1) * LANES] for b in range(model_d // LANES)]
        send[z] = jnp.concatenate([total, ext[0], ext[1], misc, pair_sums] + value + pad, axis=0).astype(BF16)


def total_kernel(cols, recv, send, rest):
    levels = recv.shape[0]
    total = recv[0].astype(F32)
    for z in range(1, levels):
        total = total + recv[z].astype(F32)
    slab = total[:272].astype(BF16)
    for t in range(send.shape[0]):
        send[t] = slab
    rest[...] = total[cols + 16 : cols + 32]


def store_half(cols, scale, core, half, slabs, weight, held, sems):
    copies = []
    for t in range(slabs.shape[0]):
        held[t] = slabs[t].astype(F32)[:cols] * scale
        at = pl.multiple_of((2 * t + core) * half, half)
        copies.append(pltpu.make_async_copy(held.at[t], weight.at[:, pl.ds(at, half)], sems.at[t]))
        copies[-1].start()
    return copies


def half_kernel(cols, scale, half, core, slabs, weight_in, weight, held, sems):
    for copy in store_half(cols, scale, 1 - core[0], half, slabs, weight, held, sems):
        copy.wait()


def local_weight_kernel(heads, scale, cols, half, core, slabs, recv, rest, w_t, *refs):
    outs, held_outs = refs[:5], refs[5:10]
    held, sems, out_sems = held_outs[4], refs[10], refs[11]
    copies = store_half(cols, scale, core[0], half, slabs, outs[4], held, sems)
    moves = [pltpu.make_async_copy(held_outs[k], outs[k], out_sems.at[k]) for k in range(4)]
    local_kernel(heads, scale, recv, rest, w_t, *held_outs[:4], moves)
    for copy in copies + moves:
        copy.wait()


def local_kernel(heads, scale, recv, rest, w_t, value, inputs, table, head, moves=()):
    levels = recv.shape[0]
    model_d = w_t.shape[1]
    cols = w_t.shape[0]
    dates = value.shape[1]
    w = w_t[...]
    ext_rows = []
    for z in range(levels):
        rows = recv[z].astype(F32)
        ext_rows.append(jnp.concatenate([rows[cols + 8 * b : cols + 8 * b + 8] for b in range(3)], axis=1))
        at = cols + 32
        values = jnp.concatenate([rows[at + 8 * b : at + 8 * b + 8] for b in range(model_d // LANES)], axis=1)
        for c in range(2):
            value[2 * z + c] = values[c * dates : (c + 1) * dates].astype(BF16)
    for move in moves[:1]:
        move.start()
    grads = nn(jnp.concatenate(ext_rows, axis=0).astype(BF16)[:, :cols], w)
    for p in range(2 * levels):
        inputs[p] = grads[p * dates : (p + 1) * dates].astype(BF16)
    for move in moves[1:2]:
        move.start()
    last = pltpu.roll(rest[0:8, :], 64, 1)
    sums = jnp.concatenate([rest[8:12, :], rest[12:16, :], last[0:4]], axis=1)
    sums = sums[0:2] + sums[2:4]
    high, low = split(sums[:, :cols])
    table[...] = (nn(high, w) + nn(low, w)) * scale
    both = sums[0:1] + sums[1:2]
    at = cols - heads
    rows = []
    for k in (2, 0, 4):
        lo = at + k * heads
        rows.append(both[:, lo : lo + heads] + both[:, lo + heads : lo + 2 * heads])
    head[...] = jnp.concatenate(rows, axis=0) * scale
    for move in moves[2:]:
        move.start()


def gather_kernel(cols, half, scale, core, own, other, out):
    tiles = own.shape[0]
    mine = core[0] == 0
    for t in range(tiles):
        a = own[t].astype(F32)
        b = other[t].astype(F32)
        first = jnp.where(mine, a, b)[:cols, :half]
        second = jnp.where(mine, b, a)[:cols, :half]
        out[:, 2 * half * t : 2 * half * (t + 1)] = jnp.concatenate([first, second], axis=1) * scale


VMEM = pl.BlockSpec(memory_space=pltpu.VMEM)
SMEM = pl.BlockSpec(memory_space=pltpu.SMEM)
HBM = pl.BlockSpec(memory_space=pltpu.HBM)


def call(kernel, outs, ins, smem=0):
    return pl.pallas_call(
        kernel,
        out_shape=[jax.ShapeDtypeStruct(s, d) for s, d in outs],
        in_specs=[SMEM] * smem + [VMEM] * (len(ins) - smem),
        out_specs=[VMEM] * len(outs),
        compiler_params=pltpu.CompilerParams(vmem_limit_bytes=48 * 1024 * 1024),
    )(*ins)


def on_device(
    layer_input,
    head_input,
    out_grad,
    sensor_ids,
    valid_mask,
    sensor_table,
    proj_weight,
    step_bias,
    decay_log,
    skip_gain,
):
    pixel_dev, dates_dev, model_d = layer_input.shape
    heads = step_bias.shape[0]
    cols = proj_weight.shape[1]
    tiles = lax.axis_size("tile")
    dates = lax.axis_size("date")
    assert pixel_dev == dates and dates % 2 == 0
    levels = dates // 2
    length = dates * dates_dev
    slab = model_d // tiles
    half = slab // 2
    core = lax.axis_index("date") % 2
    core_s = core.astype(jnp.int32).reshape(1)
    w_t = proj_weight.T
    scale = 1.0 / math.sqrt(pixel_dev * dates_dev * tiles * dates)
    swap = [(i, i ^ 1) for i in range(dates)]
    planes = [[2 * z + c for z in range(levels)] for c in range(2)]

    operands = [
        sensor_ids,
        valid_mask.T,
        sensor_table,
        step_bias[None],
        decay_log[None],
        skip_gain[None],
        layer_input,
        head_input,
        out_grad,
    ]
    packed = pl.pallas_call(
        pack_kernel,
        out_shape=jax.ShapeDtypeStruct((pixel_dev, dates_dev, 3 * model_d + LANES), BF16),
        in_specs=[SMEM] + [HBM] * 9,
        out_specs=VMEM,
        scratch_shapes=[
            pltpu.SMEM((dates_dev,), jnp.int32),
            pltpu.VMEM((dates_dev, pixel_dev), jnp.int32),
            pltpu.VMEM((2, model_d), F32),
            pltpu.VMEM((3, heads), F32),
            pltpu.VMEM((pixel_dev, dates_dev, model_d), BF16),
            pltpu.SemaphoreType.DMA((9,)),
        ],
        compiler_params=pltpu.CompilerParams(vmem_limit_bytes=16 * 1024 * 1024),
    )(core_s, *[pltpu.with_memory_space_constraint(operand, pltpu.HBM) for operand in operands])
    series = lax.all_to_all(packed, "date", split_axis=0, concat_axis=0, tiled=True).reshape(
        length, 3 * model_d + LANES
    )

    rows_core = length // 2
    send_t, own, give_rows, sel = call(
        functools.partial(series_kernel, heads, model_d, dates_dev),
        [
            ((tiles, length, EXT + slab), BF16),
            ((rows_core, model_d + EXT), BF16),
            ((rows_core, model_d + EXT), BF16),
            ((16, length), BF16),
        ],
        [core_s, series, w_t],
        1,
    )
    mixed = [
        [t * dates + 2 * z + (c + t) % 2 for t in range(tiles)] for z in range(levels) for c in range(2)
    ]
    recv_t = lax.all_to_all(
        send_t, ("tile", "date"), split_axis=0, concat_axis=0, tiled=True, axis_index_groups=mixed
    )
    rows_give = cols + 24 + rows_core * (model_d + EXT) // LANES
    keep, keep_sums, give = call(
        functools.partial(slab_kernel, cols),
        [((cols, LANES), F32), ((2, EXT), F32), ((rows_give, LANES), BF16)],
        [core_s, recv_t, sel, give_rows],
        1,
    )
    got = lax.ppermute(give, "date", swap)
    rows_z = -(-(cols + 32 + model_d // 16) // 16) * 16
    (send_z,) = call(
        functools.partial(join_kernel, cols, dates_dev),
        [((levels, rows_z, LANES), BF16)],
        [core_s, keep, keep_sums, got, own],
        1,
    )
    recv_z = lax.all_to_all(
        send_z, "date", split_axis=0, concat_axis=0, tiled=True, axis_index_groups=planes
    )
    send_g, rest = call(
        functools.partial(total_kernel, cols),
        [((tiles, 272, LANES), BF16), ((16, LANES), F32)],
        [recv_z],
    )
    recv_g = lax.all_to_all(send_g, "tile", split_axis=0, concat_axis=0, tiled=True)
    local_outs = [
        ((pixel_dev, dates_dev, model_d), BF16),
        ((pixel_dev, dates_dev, model_d), BF16),
        ((2, model_d), F32),
        ((3, heads), F32),
    ]
    other_g = lax.ppermute(recv_g, "date", swap)
    if half % LANES == 0:
        weight_shape = jax.ShapeDtypeStruct((cols, model_d), F32)
        held = [pltpu.VMEM((tiles, cols, half), F32), pltpu.SemaphoreType.DMA((tiles,))]
        limit = pltpu.CompilerParams(vmem_limit_bytes=48 * 1024 * 1024)
        value, inputs, table, head, weight_t = pl.pallas_call(
            functools.partial(local_weight_kernel, heads, scale, cols, half),
            out_shape=[jax.ShapeDtypeStruct(s, d) for s, d in local_outs] + [weight_shape],
            in_specs=[SMEM] + [VMEM] * 4,
            out_specs=[HBM] * 5,
            scratch_shapes=[pltpu.VMEM(s, d) for s, d in local_outs]
            + held
            + [pltpu.SemaphoreType.DMA((4,))],
            compiler_params=limit,
        )(core_s, recv_g, recv_z, rest, w_t)
        weight_t = pl.pallas_call(
            functools.partial(half_kernel, cols, scale, half),
            out_shape=weight_shape,
            in_specs=[SMEM, VMEM, HBM],
            out_specs=HBM,
            scratch_shapes=held,
            input_output_aliases={2: 0},
            compiler_params=limit,
        )(core_s, other_g, weight_t)
    else:
        value, inputs, table, head = call(
            functools.partial(local_kernel, heads, scale), local_outs, [recv_z, rest, w_t]
        )
        (weight_t,) = call(
            functools.partial(gather_kernel, cols, half, scale),
            [((cols, model_d), F32)],
            [core_s, recv_g, other_g],
            1,
        )
    return (
        value,
        inputs,
        weight_t.T,
        table,
        head,
    )


def solution(mesh):
    in_specs = (
        P("tile", "date", None),
        P("tile", "date", None),
        P("tile", "date", None),
        P("date"),
        P("tile", "date"),
        P(),
        P(),
        P(),
        P(),
        P(),
    )
    out_specs = (P("tile", "date", None), P("tile", "date", None), P(), P(), P())
    return jax.shard_map(
        on_device, mesh=mesh, in_specs=in_specs, out_specs=out_specs, check_vma=False
    )
```

```python
import functools
import math

import jax
import jax.numpy as jnp
from jax import lax
from jax.experimental import pallas as pl
from jax.experimental.pallas import tpu as pltpu
from jax.sharding import PartitionSpec as P

NEG_FILL = -1e30
HIGHEST_PREC = lax.Precision.HIGHEST
F32 = jnp.float32
BF16 = jnp.bfloat16
LANES = 128
EXT = 384


def nt(a, b, precision=None):
    return lax.dot_general(
        a, b, (((1,), (1,)), ((), ())), preferred_element_type=F32, precision=precision
    )


def nn(a, b, precision=None):
    return lax.dot_general(
        a, b, (((1,), (0,)), ((), ())), preferred_element_type=F32, precision=precision
    )


def tn(a, b):
    return lax.dot_general(a, b, (((0,), (0,)), ((), ())), preferred_element_type=F32)


def split(x):
    high = x.astype(BF16)
    return high, (x - high.astype(F32)).astype(BF16)


def series_kernel(heads, model_d, dates, core, recv, w_t, send, own, give, sel):
    length = recv.shape[0]
    tiles, _, width = send.shape
    slab = width - EXT
    width_p = model_d // heads
    states = (w_t.shape[0] - heads) // 2
    mixed = recv[:, :model_d]
    aux = recv[:, 3 * model_d :].astype(F32)
    gate = aux[:, 0:1]
    ids = aux[:, 1:2]
    params = []
    for at in range(2, 2 + 9 * heads, 3 * heads):
        params.append(sum(aux[0:1, at + k * heads : at + (k + 1) * heads] for k in range(3)))
    bias, rate, skip = params[0], -jnp.exp(params[1]), params[2]
    projected = nt(mixed, w_t[...])
    keys = projected[:, :states].astype(BF16)
    reads = projected[:, states : 2 * states].astype(BF16)
    step_pre = projected[:, 2 * states :] + bias
    softplus = jnp.maximum(step_pre, 0.0) + jnp.log1p(jnp.exp(-jnp.abs(step_pre)))
    steps_b = (gate * softplus).astype(BF16)
    steps = steps_b.astype(F32)

    row = lax.broadcasted_iota(jnp.int32, (length, length), 0)
    col = lax.broadcasted_iota(jnp.int32, (length, length), 1)
    upper = col >= row
    upper_f = upper.astype(F32)
    eye = (col == row).astype(F32)
    lower_b = (row >= col).astype(BF16)
    head_row = lax.broadcasted_iota(jnp.int32, (heads, heads), 0)
    head_col = lax.broadcasted_iota(jnp.int32, (heads, heads), 1)
    eye_h = (head_row == head_col).astype(F32)
    rate_col = jnp.sum(eye_h * rate, axis=1, keepdims=True)
    log_col = nn(lower_b, steps_b) * rate
    steps_t = nt(eye_h.astype(BF16), steps_b).astype(BF16)
    log_row = nn(steps_t, upper.astype(BF16)) * rate_col
    scores_t = nt(keys, reads)

    pair_t = jnp.zeros((length, length), F32)
    value_parts, weighted_cols, read_rows, skip_cols = [], [], [], []
    for h in range(heads):
        lo = model_d + h * width_p
        x_h = recv[:, lo : lo + width_p]
        g_h = recv[:, lo + model_d : lo + model_d + width_p]
        dt_h = steps[:, h : h + 1]
        gap = log_row[h : h + 1, :] - log_col[:, h : h + 1]
        decay = jnp.exp(jnp.where(upper, gap, NEG_FILL))
        cross = nt(x_h, g_h)
        mix = decay * scores_t
        pair_t = pair_t + decay * cross * dt_h
        both = mix * cross
        weighted = jnp.sum(both, axis=1, keepdims=True)
        weighted_cols.append(weighted)
        read_rows.append(jnp.sum(both * dt_h, axis=0, keepdims=True))
        skip_cols.append(jnp.sum(cross * eye, axis=1, keepdims=True))
        value_parts.append(nn(mix.astype(BF16), g_h) * dt_h + skip[:, h : h + 1] * g_h.astype(F32))

    weighted = jnp.concatenate(weighted_cols, axis=1)
    read_sum = jnp.concatenate(read_rows, axis=0)
    skip_terms = jnp.concatenate(skip_cols, axis=1)
    later = nt(upper_f, read_sum, HIGHEST_PREC) - nn(upper_f, steps * weighted, HIGHEST_PREC)
    step_grad = (weighted + rate * later).astype(BF16).astype(F32)
    decay_terms = steps * later * rate
    pair_b = pair_t.astype(BF16)
    grad_keys = nn(pair_b, reads)
    grad_reads = tn(pair_b, keys)
    raw = step_grad * gate * jax.nn.sigmoid(step_pre)
    terms = jnp.concatenate(
        [raw, decay_terms, skip_terms, jnp.zeros((length, LANES - 3 * heads), F32)], axis=1
    )
    high = terms.astype(BF16).astype(F32)
    tail = high + pltpu.roll(terms - high, 3 * heads, 1)
    ext_f = jnp.concatenate([grad_keys, grad_reads, tail], axis=1)
    ext = ext_f.astype(BF16)
    back = jnp.concatenate(value_parts + [ext_f], axis=1)
    first = core[0] == 0
    own_rows, give_rows = [], []
    for at in range(0, length, 2 * dates):
        a, b = back[at : at + dates], back[at + dates : at + 2 * dates]
        own_rows.append(jnp.where(first, a, b))
        give_rows.append(jnp.where(first, b, a))
    own[...] = jnp.concatenate(own_rows, axis=0).astype(BF16)
    give[...] = jnp.concatenate(give_rows, axis=0).astype(BF16)
    for t in range(tiles):
        send[t, :, :EXT] = ext
        send[t, :, EXT:] = recv[:, t * slab : (t + 1) * slab]
    ids_row = jnp.sum(eye * ids, axis=0, keepdims=True)
    sel[...] = jnp.concatenate([1.0 - ids_row, ids_row, jnp.zeros((14, length), F32)], axis=0).astype(
        BF16
    )


def pack_kernel(core, ids_in, mask_in, table_in, bias_in, decay_in, skip_in, layer, values, cotangent, out, ids, mask_t, table, params, layer_v, sems):
    pixels, dates, model_d = layer.shape
    small = [
        pltpu.make_async_copy(ids_in, ids, sems.at[0]),
        pltpu.make_async_copy(mask_in, mask_t, sems.at[1]),
        pltpu.make_async_copy(table_in, table, sems.at[2]),
        pltpu.make_async_copy(layer, layer_v, sems.at[3]),
        pltpu.make_async_copy(bias_in, params.at[0:1], sems.at[6]),
        pltpu.make_async_copy(decay_in, params.at[1:2], sems.at[7]),
        pltpu.make_async_copy(skip_in, params.at[2:3], sems.at[8]),
    ]
    large = [
        pltpu.make_async_copy(values, out.at[:, :, model_d : 2 * model_d], sems.at[4]),
        pltpu.make_async_copy(cotangent, out.at[:, :, 2 * model_d : 3 * model_d], sems.at[5]),
    ]
    for copy in small[3:4] + large + small[:3] + small[4:]:
        copy.start()
    for copy in small:
        copy.wait()
    rows = [jnp.where(ids[i] == 1, table[1:2, :], table[0:1, :]) for i in range(dates)]
    embed = jnp.concatenate(rows, axis=0)
    row = lax.broadcasted_iota(jnp.int32, (dates, LANES), 0)
    lane = lax.broadcasted_iota(jnp.int32, (dates, LANES), 1)
    second = jnp.zeros((dates, LANES), F32)
    for i in range(dates):
        second = jnp.where((row == i) & (lane == 1), (ids[i] == 1).astype(F32), second)
    gate = mask_t[...].astype(F32)
    at = 2
    for k in range(3):
        rest = params[k : k + 1, :]
        for _ in range(3):
            term = rest.astype(BF16).astype(F32)
            rest = rest - term
            term = jnp.concatenate([jnp.zeros((1, at), F32), term, jnp.zeros((1, LANES - at - term.shape[1]), F32)], axis=1)
            second = second + term
            at = at + params.shape[1]
    for p in range(pixels):
        out[p, :, 3 * model_d :] = jnp.where(lane == 0, gate[:, p : p + 1], second).astype(BF16)
        out[p, :, :model_d] = (layer_v[p].astype(F32) + embed).astype(BF16)
    for copy in large:
        copy.wait()


def lane_pad(x, width):
    if x.shape[1] == width:
        return x
    return jnp.concatenate([x, jnp.zeros((x.shape[0], width - x.shape[1]), x.dtype)], axis=1)


def sum_rows(sums):
    high = sums.astype(BF16).astype(F32)
    low = (sums - high).astype(BF16).astype(F32)
    rows = jnp.concatenate([high, low, jnp.zeros((4, EXT), F32)], axis=0)
    return [rows[:, b * LANES : (b + 1) * LANES] for b in range(EXT // LANES)]


def rows_sum(block):
    rows = jnp.concatenate([block[8 * b : 8 * b + 8, :] for b in range(EXT // LANES)], axis=1)
    return rows[0:2] + rows[2:4]


def slab_kernel(cols, core, recv, sel, rows, keep, keep_sums, give):
    tiles, length, width = recv.shape
    slab = width - EXT
    half = slab // 2
    ext = recv[:, :, :EXT].reshape(tiles * length, EXT)
    tokens = recv[:, :, EXT:].reshape(tiles * length, slab)
    part = tn(ext, tokens)[:cols]
    sums = jnp.zeros((16, EXT), F32)
    for t in range(tiles):
        sums = sums + nn(sel[...], recv[t, :, :EXT])
    sums = sums[0:2]
    mine = core[0] == 0
    first = lane_pad(part[:, :half], LANES)
    second = lane_pad(part[:, half:], LANES)
    keep[...] = jnp.where(mine, first, second)
    keep_sums[...] = sums
    other = jnp.where(mine, second, first)
    blocks = [rows[:, b * LANES : (b + 1) * LANES].astype(F32) for b in range(rows.shape[1] // LANES)]
    give[...] = jnp.concatenate([other] + sum_rows(sums) + blocks, axis=0).astype(BF16)


def join_kernel(cols, dates, core, keep, keep_sums, got, own, send):
    levels = send.shape[0]
    first = core[0] == 0
    model_d = own.shape[1] - EXT
    total = keep[...] + got[:cols, :].astype(F32)
    sums = sum_rows(keep_sums[...] + rows_sum(got[cols : cols + 24, :].astype(F32)))
    pair_sums = jnp.concatenate([sums[0][:4], sums[1][:4]], axis=0)
    mine, count = own[...].astype(F32), own.shape[0]
    tall = got[cols + 24 :, :].astype(F32)
    theirs = jnp.concatenate([tall[k : k + count] for k in range(0, tall.shape[0], count)], axis=1)
    firsts, seconds = jnp.where(first, mine, theirs), jnp.where(first, theirs, mine)
    lane = lax.broadcasted_iota(jnp.int32, (8, LANES), 1)
    last = pltpu.roll(sums[2], 64, 1)
    for z in range(levels):
        at = z * dates
        rows = jnp.concatenate([firsts[at : at + dates], seconds[at : at + dates]], axis=0)
        ext = [rows[:, model_d + b * LANES : model_d + (b + 1) * LANES] for b in range(EXT // LANES)]
        misc = jnp.where(lane < 64, ext[2], last)
        value = [rows[:, b * LANES : (b + 1) * LANES] for b in range(model_d // LANES)]
        send[z] = jnp.concatenate([total, ext[0], ext[1], misc, pair_sums] + value, axis=0).astype(BF16)


def total_kernel(cols, recv, send, rest):
    levels = recv.shape[0]
    total = recv[0].astype(F32)
    for z in range(1, levels):
        total = total + recv[z].astype(F32)
    slab = total[:cols].astype(BF16)
    for t in range(send.shape[0]):
        send[t] = slab
    rest[...] = total[cols + 16 : cols + 32]


def store_half(cols, scale, core, half, slabs, weight, held, sems):
    copies = []
    for t in range(slabs.shape[0]):
        held[t] = slabs[t].astype(F32)[:cols] * scale
        at = pl.multiple_of((2 * t + core) * half, half)
        copies.append(pltpu.make_async_copy(held.at[t], weight.at[:, pl.ds(at, half)], sems.at[t]))
        copies[-1].start()
    return copies


def half_kernel(cols, scale, half, core, slabs, weight_in, weight, held, sems):
    for copy in store_half(cols, scale, 1 - core[0], half, slabs, weight, held, sems):
        copy.wait()


def local_weight_kernel(heads, scale, cols, half, core, slabs, recv, rest, w_t, *refs):
    outs, held_outs = refs[:5], refs[5:10]
    held, sems, out_sems = held_outs[4], refs[10], refs[11]
    copies = store_half(cols, scale, core[0], half, slabs, outs[4], held, sems)
    moves = [pltpu.make_async_copy(held_outs[k], outs[k], out_sems.at[k]) for k in range(4)]
    local_kernel(heads, scale, recv, rest, w_t, *held_outs[:4], moves)
    for copy in copies + moves:
        copy.wait()


def local_kernel(heads, scale, recv, rest, w_t, value, inputs, table, head, moves=()):
    levels = recv.shape[0]
    model_d = w_t.shape[1]
    cols = w_t.shape[0]
    dates = value.shape[1]
    w = w_t[...]
    ext_rows = []
    for z in range(levels):
        rows = recv[z].astype(F32)
        ext_rows.append(jnp.concatenate([rows[cols + 8 * b : cols + 8 * b + 8] for b in range(3)], axis=1))
        at = cols + 32
        values = jnp.concatenate([rows[at + 8 * b : at + 8 * b + 8] for b in range(model_d // LANES)], axis=1)
        for c in range(2):
            value[2 * z + c] = values[c * dates : (c + 1) * dates].astype(BF16)
    for move in moves[:1]:
        move.start()
    grads = nn(jnp.concatenate(ext_rows, axis=0).astype(BF16)[:, :cols], w)
    for p in range(2 * levels):
        inputs[p] = grads[p * dates : (p + 1) * dates].astype(BF16)
    for move in moves[1:2]:
        move.start()
    last = pltpu.roll(rest[0:8, :], 64, 1)
    sums = jnp.concatenate([rest[8:12, :], rest[12:16, :], last[0:4]], axis=1)
    sums = sums[0:2] + sums[2:4]
    high, low = split(sums[:, :cols])
    table[...] = (nn(high, w) + nn(low, w)) * scale
    both = sums[0:1] + sums[1:2]
    at = cols - heads
    rows = []
    for k in (1, 0, 2):
        lo = at + k * heads
        rows.append(both[:, lo : lo + heads] + both[:, lo + 3 * heads : lo + 4 * heads])
    head[...] = jnp.concatenate(rows, axis=0) * scale
    for move in moves[2:]:
        move.start()


def gather_kernel(cols, half, scale, core, own, other, out):
    tiles = own.shape[0]
    mine = core[0] == 0
    for t in range(tiles):
        a = own[t].astype(F32)
        b = other[t].astype(F32)
        first = jnp.where(mine, a, b)[:cols, :half]
        second = jnp.where(mine, b, a)[:cols, :half]
        out[:, 2 * half * t : 2 * half * (t + 1)] = jnp.concatenate([first, second], axis=1) * scale


VMEM = pl.BlockSpec(memory_space=pltpu.VMEM)
SMEM = pl.BlockSpec(memory_space=pltpu.SMEM)
HBM = pl.BlockSpec(memory_space=pltpu.HBM)


def call(kernel, outs, ins, smem=0):
    return pl.pallas_call(
        kernel,
        out_shape=[jax.ShapeDtypeStruct(s, d) for s, d in outs],
        in_specs=[SMEM] * smem + [VMEM] * (len(ins) - smem),
        out_specs=[VMEM] * len(outs),
        compiler_params=pltpu.CompilerParams(vmem_limit_bytes=48 * 1024 * 1024),
    )(*ins)


def on_device(
    layer_input,
    head_input,
    out_grad,
    sensor_ids,
    valid_mask,
    sensor_table,
    proj_weight,
    step_bias,
    decay_log,
    skip_gain,
):
    pixel_dev, dates_dev, model_d = layer_input.shape
    heads = step_bias.shape[0]
    cols = proj_weight.shape[1]
    tiles = lax.axis_size("tile")
    dates = lax.axis_size("date")
    assert pixel_dev == dates and dates % 2 == 0
    levels = dates // 2
    length = dates * dates_dev
    slab = model_d // tiles
    half = slab // 2
    core = lax.axis_index("date") % 2
    core_s = core.astype(jnp.int32).reshape(1)
    w_t = proj_weight.T
    scale = 1.0 / math.sqrt(pixel_dev * dates_dev * tiles * dates)
    swap = [(i, i ^ 1) for i in range(dates)]
    planes = [[2 * z + c for z in range(levels)] for c in range(2)]

    operands = [
        sensor_ids,
        valid_mask.T,
        sensor_table,
        step_bias[None],
        decay_log[None],
        skip_gain[None],
        layer_input,
        head_input,
        out_grad,
    ]
    packed = pl.pallas_call(
        pack_kernel,
        out_shape=jax.ShapeDtypeStruct((pixel_dev, dates_dev, 3 * model_d + LANES), BF16),
        in_specs=[SMEM] + [HBM] * 9,
        out_specs=VMEM,
        scratch_shapes=[
            pltpu.SMEM((dates_dev,), jnp.int32),
            pltpu.VMEM((dates_dev, pixel_dev), jnp.int32),
            pltpu.VMEM((2, model_d), F32),
            pltpu.VMEM((3, heads), F32),
            pltpu.VMEM((pixel_dev, dates_dev, model_d), BF16),
            pltpu.SemaphoreType.DMA((9,)),
        ],
        compiler_params=pltpu.CompilerParams(vmem_limit_bytes=16 * 1024 * 1024),
    )(core_s, *[pltpu.with_memory_space_constraint(operand, pltpu.HBM) for operand in operands])
    series = lax.all_to_all(packed, "date", split_axis=0, concat_axis=0, tiled=True).reshape(
        length, 3 * model_d + LANES
    )

    rows_core = length // 2
    send_t, own, give_rows, sel = call(
        functools.partial(series_kernel, heads, model_d, dates_dev),
        [
            ((tiles, length, EXT + slab), BF16),
            ((rows_core, model_d + EXT), BF16),
            ((rows_core, model_d + EXT), BF16),
            ((16, length), BF16),
        ],
        [core_s, series, w_t],
        1,
    )
    mixed = [
        [t * dates + 2 * z + (c + t) % 2 for t in range(tiles)] for z in range(levels) for c in range(2)
    ]
    recv_t = lax.all_to_all(
        send_t, ("tile", "date"), split_axis=0, concat_axis=0, tiled=True, axis_index_groups=mixed
    )
    rows_give = cols + 24 + rows_core * (model_d + EXT) // LANES
    keep, keep_sums, give = call(
        functools.partial(slab_kernel, cols),
        [((cols, LANES), F32), ((2, EXT), F32), ((rows_give, LANES), BF16)],
        [core_s, recv_t, sel, give_rows],
        1,
    )
    got = lax.ppermute(give, "date", swap)
    rows_z = cols + 32 + model_d // 16
    (send_z,) = call(
        functools.partial(join_kernel, cols, dates_dev),
        [((levels, rows_z, LANES), BF16)],
        [core_s, keep, keep_sums, got, own],
        1,
    )
    recv_z = lax.all_to_all(
        send_z, "date", split_axis=0, concat_axis=0, tiled=True, axis_index_groups=planes
    )
    send_g, rest = call(
        functools.partial(total_kernel, cols),
        [((tiles, cols, LANES), BF16), ((16, LANES), F32)],
        [recv_z],
    )
    recv_g = lax.all_to_all(send_g, "tile", split_axis=0, concat_axis=0, tiled=True)
    local_outs = [
        ((pixel_dev, dates_dev, model_d), BF16),
        ((pixel_dev, dates_dev, model_d), BF16),
        ((2, model_d), F32),
        ((3, heads), F32),
    ]
    other_g = lax.ppermute(recv_g, "date", swap)
    if half % LANES == 0:
        weight_shape = jax.ShapeDtypeStruct((cols, model_d), F32)
        held = [pltpu.VMEM((tiles, cols, half), F32), pltpu.SemaphoreType.DMA((tiles,))]
        limit = pltpu.CompilerParams(vmem_limit_bytes=48 * 1024 * 1024)
        value, inputs, table, head, weight_t = pl.pallas_call(
            functools.partial(local_weight_kernel, heads, scale, cols, half),
            out_shape=[jax.ShapeDtypeStruct(s, d) for s, d in local_outs] + [weight_shape],
            in_specs=[SMEM] + [VMEM] * 4,
            out_specs=[HBM] * 5,
            scratch_shapes=[pltpu.VMEM(s, d) for s, d in local_outs]
            + held
            + [pltpu.SemaphoreType.DMA((4,))],
            compiler_params=limit,
        )(core_s, recv_g, recv_z, rest, w_t)
        weight_t = pl.pallas_call(
            functools.partial(half_kernel, cols, scale, half),
            out_shape=weight_shape,
            in_specs=[SMEM, VMEM, HBM],
            out_specs=HBM,
            scratch_shapes=held,
            input_output_aliases={2: 0},
            compiler_params=limit,
        )(core_s, other_g, weight_t)
    else:
        value, inputs, table, head = call(
            functools.partial(local_kernel, heads, scale), local_outs, [recv_z, rest, w_t]
        )
        (weight_t,) = call(
            functools.partial(gather_kernel, cols, half, scale),
            [((cols, model_d), F32)],
            [core_s, recv_g, other_g],
            1,
        )
    return (
        value,
        inputs,
        weight_t.T,
        table,
        head,
    )


def solution(mesh):
    in_specs = (
        P("tile", "date", None),
        P("tile", "date", None),
        P("tile", "date", None),
        P("date"),
        P("tile", "date"),
        P(),
        P(),
        P(),
        P(),
        P(),
    )
    out_specs = (P("tile", "date", None), P("tile", "date", None), P(), P(), P())
    return jax.shard_map(
        on_device, mesh=mesh, in_specs=in_specs, out_specs=out_specs, check_vma=False
    )
```

```python
import functools
import math

import jax
import jax.numpy as jnp
from jax import lax
from jax.experimental import pallas as pl
from jax.experimental.pallas import tpu as pltpu
from jax.sharding import PartitionSpec as P

NEG_FILL = -1e30
HIGHEST_PREC = lax.Precision.HIGHEST
F32 = jnp.float32
BF16 = jnp.bfloat16
LANES = 128
EXT = 384


def nt(a, b, precision=None):
    return lax.dot_general(
        a, b, (((1,), (1,)), ((), ())), preferred_element_type=F32, precision=precision
    )


def nn(a, b, precision=None):
    return lax.dot_general(
        a, b, (((1,), (0,)), ((), ())), preferred_element_type=F32, precision=precision
    )


def tn(a, b):
    return lax.dot_general(a, b, (((0,), (0,)), ((), ())), preferred_element_type=F32)


def split(x):
    high = x.astype(BF16)
    return high, (x - high.astype(F32)).astype(BF16)


def bit_of(pos, bit):
    return lax.rem(lax.div(pos[0], 2**bit), 2)


def halves(arrays, span, first):
    kept, given = [], []
    for array in arrays:
        for at in range(0, array.shape[0], 2 * span):
            a, b = array[at : at + span], array[at + span : at + 2 * span]
            kept.append(jnp.where(first, a, b))
            given.append(jnp.where(first, b, a))
    return jnp.concatenate(kept, axis=0), jnp.concatenate(given, axis=0)


def series_kernel(heads, model_d, bit, span, pos, recv, w_t, send, own, give, sel):
    length = recv.shape[0]
    tiles, _, width = send.shape
    slab = width - EXT
    width_p = model_d // heads
    states = (w_t.shape[0] - heads) // 2
    mixed = recv[:, :model_d]
    aux = recv[:, 3 * model_d :].astype(F32)
    gate = aux[:, 0:1]
    ids = aux[:, 1:2]
    params = []
    for at in range(2, 2 + 9 * heads, 3 * heads):
        params.append(sum(aux[0:1, at + k * heads : at + (k + 1) * heads] for k in range(3)))
    bias, rate, skip = params[0], -jnp.exp(params[1]), params[2]
    projected = nt(mixed, w_t[...])
    keys = projected[:, :states].astype(BF16)
    reads = projected[:, states : 2 * states].astype(BF16)
    step_pre = projected[:, 2 * states :] + bias
    softplus = jnp.maximum(step_pre, 0.0) + jnp.log1p(jnp.exp(-jnp.abs(step_pre)))
    steps_b = (gate * softplus).astype(BF16)
    steps = steps_b.astype(F32)

    row = lax.broadcasted_iota(jnp.int32, (length, length), 0)
    col = lax.broadcasted_iota(jnp.int32, (length, length), 1)
    upper = col >= row
    upper_f = upper.astype(F32)
    eye = (col == row).astype(F32)
    lower_b = (row >= col).astype(BF16)
    head_row = lax.broadcasted_iota(jnp.int32, (heads, heads), 0)
    head_col = lax.broadcasted_iota(jnp.int32, (heads, heads), 1)
    eye_h = (head_row == head_col).astype(F32)
    rate_col = jnp.sum(eye_h * rate, axis=1, keepdims=True)
    log_col = nn(lower_b, steps_b) * rate
    steps_t = nt(eye_h.astype(BF16), steps_b).astype(BF16)
    log_row = nn(steps_t, upper.astype(BF16)) * rate_col
    scores_t = nt(keys, reads)

    pair_t = jnp.zeros((length, length), F32)
    value_parts, weighted_cols, read_rows, skip_cols = [], [], [], []
    for h in range(heads):
        lo = model_d + h * width_p
        x_h = recv[:, lo : lo + width_p]
        g_h = recv[:, lo + model_d : lo + model_d + width_p]
        dt_h = steps[:, h : h + 1]
        gap = log_row[h : h + 1, :] - log_col[:, h : h + 1]
        decay = jnp.exp(jnp.where(upper, gap, NEG_FILL))
        cross = nt(x_h, g_h)
        mix = decay * scores_t
        pair_t = pair_t + decay * cross * dt_h
        both = mix * cross
        weighted = jnp.sum(both, axis=1, keepdims=True)
        weighted_cols.append(weighted)
        read_rows.append(jnp.sum(both * dt_h, axis=0, keepdims=True))
        skip_cols.append(jnp.sum(cross * eye, axis=1, keepdims=True))
        value_parts.append(nn(mix.astype(BF16), g_h) * dt_h + skip[:, h : h + 1] * g_h.astype(F32))

    weighted = jnp.concatenate(weighted_cols, axis=1)
    read_sum = jnp.concatenate(read_rows, axis=0)
    skip_terms = jnp.concatenate(skip_cols, axis=1)
    later = nt(upper_f, read_sum, HIGHEST_PREC) - nn(upper_f, steps * weighted, HIGHEST_PREC)
    step_grad = (weighted + rate * later).astype(BF16).astype(F32)
    decay_terms = steps * later * rate
    pair_b = pair_t.astype(BF16)
    grad_keys = nn(pair_b, reads)
    grad_reads = tn(pair_b, keys)
    raw = step_grad * gate * jax.nn.sigmoid(step_pre)
    terms = jnp.concatenate(
        [raw, decay_terms, skip_terms, jnp.zeros((length, LANES - 3 * heads), F32)], axis=1
    )
    high = terms.astype(BF16).astype(F32)
    tail = high + pltpu.roll(terms - high, 3 * heads, 1)
    ext_f = jnp.concatenate([grad_keys, grad_reads, tail], axis=1)
    ext = ext_f.astype(BF16)
    back = jnp.concatenate(value_parts + [ext_f], axis=1)
    kept, given = halves([back], span, bit_of(pos, bit) == 0)
    own[...] = kept.astype(BF16)
    give[...] = given.astype(BF16)
    for t in range(tiles):
        send[t, :, :EXT] = ext
        send[t, :, EXT:] = recv[:, t * slab : (t + 1) * slab]
    ids_row = jnp.sum(eye * ids, axis=0, keepdims=True)
    sel[...] = jnp.concatenate([1.0 - ids_row, ids_row, jnp.zeros((14, length), F32)], axis=0).astype(
        BF16
    )


def pack_kernel(core, ids_in, mask_in, table_in, bias_in, decay_in, skip_in, layer, values, cotangent, out, ids, mask_t, table, params, layer_v, sems):
    pixels, dates, model_d = layer.shape
    small = [
        pltpu.make_async_copy(ids_in, ids, sems.at[0]),
        pltpu.make_async_copy(mask_in, mask_t, sems.at[1]),
        pltpu.make_async_copy(table_in, table, sems.at[2]),
        pltpu.make_async_copy(layer, layer_v, sems.at[3]),
        pltpu.make_async_copy(bias_in, params.at[0:1], sems.at[6]),
        pltpu.make_async_copy(decay_in, params.at[1:2], sems.at[7]),
        pltpu.make_async_copy(skip_in, params.at[2:3], sems.at[8]),
    ]
    large = [
        pltpu.make_async_copy(values, out.at[:, :, model_d : 2 * model_d], sems.at[4]),
        pltpu.make_async_copy(cotangent, out.at[:, :, 2 * model_d : 3 * model_d], sems.at[5]),
    ]
    for copy in small[3:4] + large + small[:3] + small[4:]:
        copy.start()
    for copy in small:
        copy.wait()
    rows = [jnp.where(ids[i] == 1, table[1:2, :], table[0:1, :]) for i in range(dates)]
    embed = jnp.concatenate(rows, axis=0)
    row = lax.broadcasted_iota(jnp.int32, (dates, LANES), 0)
    lane = lax.broadcasted_iota(jnp.int32, (dates, LANES), 1)
    second = jnp.zeros((dates, LANES), F32)
    for i in range(dates):
        second = jnp.where((row == i) & (lane == 1), (ids[i] == 1).astype(F32), second)
    gate = mask_t[...].astype(F32)
    at = 2
    for k in range(3):
        rest = params[k : k + 1, :]
        for _ in range(3):
            term = rest.astype(BF16).astype(F32)
            rest = rest - term
            term = jnp.concatenate([jnp.zeros((1, at), F32), term, jnp.zeros((1, LANES - at - term.shape[1]), F32)], axis=1)
            second = second + term
            at = at + params.shape[1]
    for p in range(pixels):
        out[p, :, 3 * model_d :] = jnp.where(lane == 0, gate[:, p : p + 1], second).astype(BF16)
        out[p, :, :model_d] = (layer_v[p].astype(F32) + embed).astype(BF16)
    for copy in large:
        copy.wait()


def lane_pad(x, width):
    if x.shape[1] == width:
        return x
    return jnp.concatenate([x, jnp.zeros((x.shape[0], width - x.shape[1]), x.dtype)], axis=1)


def sum_rows(sums):
    high = sums.astype(BF16).astype(F32)
    low = (sums - high).astype(BF16).astype(F32)
    rows = jnp.concatenate([high, low, jnp.zeros((4, EXT), F32)], axis=0)
    return [rows[:, b * LANES : (b + 1) * LANES] for b in range(EXT // LANES)]


def rows_sum(block):
    rows = jnp.concatenate([block[8 * b : 8 * b + 8, :] for b in range(EXT // LANES)], axis=1)
    return rows[0:2] + rows[2:4]


def slab_kernel(cols, pos, recv, sel, rows, keep, keep_sums, give):
    tiles, length, width = recv.shape
    slab = width - EXT
    half = slab // 2
    ext = recv[:, :, :EXT].reshape(tiles * length, EXT)
    tokens = recv[:, :, EXT:].reshape(tiles * length, slab)
    part = tn(ext, tokens)[:cols]
    sums = jnp.zeros((16, EXT), F32)
    for t in range(tiles):
        sums = sums + nn(sel[...], recv[t, :, :EXT])
    sums = sums[0:2]
    mine = bit_of(pos, 0) == 0
    first = lane_pad(part[:, :half], LANES)
    second = lane_pad(part[:, half:], LANES)
    keep[...] = jnp.where(mine, first, second)
    keep_sums[...] = sums
    other = jnp.where(mine, second, first)
    blocks = [rows[:, b * LANES : (b + 1) * LANES].astype(F32) for b in range(rows.shape[1] // LANES)]
    give[...] = jnp.concatenate([other] + sum_rows(sums) + blocks, axis=0).astype(BF16)


def join_kernel(cols, dates, pos, keep, keep_sums, got, own, send):
    levels = send.shape[0]
    first = bit_of(pos, 0) == 0
    model_d = own.shape[1] - EXT
    total = keep[...] + got[:cols, :].astype(F32)
    sums = sum_rows(keep_sums[...] + rows_sum(got[cols : cols + 24, :].astype(F32)))
    pair_sums = jnp.concatenate([sums[0][:4], sums[1][:4]], axis=0)
    mine, count = own[...].astype(F32), own.shape[0]
    tall = got[cols + 24 :, :].astype(F32)
    theirs = jnp.concatenate([tall[k : k + count] for k in range(0, tall.shape[0], count)], axis=1)
    firsts, seconds = jnp.where(first, mine, theirs), jnp.where(first, theirs, mine)
    lane = lax.broadcasted_iota(jnp.int32, (8, LANES), 1)
    last = pltpu.roll(sums[2], 64, 1)
    for z in range(levels):
        at = z * dates
        rows = jnp.concatenate([firsts[at : at + dates], seconds[at : at + dates]], axis=0)
        ext = [rows[:, model_d + b * LANES : model_d + (b + 1) * LANES] for b in range(EXT // LANES)]
        misc = jnp.where(lane < 64, ext[2], last)
        value = [rows[:, b * LANES : (b + 1) * LANES] for b in range(model_d // LANES)]
        send[z] = jnp.concatenate([total, ext[0], ext[1], misc, pair_sums] + value, axis=0).astype(BF16)


def total_kernel(cols, recv, send, rest):
    levels = recv.shape[0]
    total = recv[0].astype(F32)
    for z in range(1, levels):
        total = total + recv[z].astype(F32)
    slab = total[:cols].astype(BF16)
    for t in range(send.shape[0]):
        send[t] = slab
    rest[...] = total[cols + 16 : cols + 32]


def store_half(cols, scale, core, half, slabs, weight, held, sems):
    copies = []
    for t in range(slabs.shape[0]):
        held[t] = slabs[t].astype(F32)[:cols] * scale
        at = pl.multiple_of((2 * t + core) * half, half)
        copies.append(pltpu.make_async_copy(held.at[t], weight.at[:, pl.ds(at, half)], sems.at[t]))
        copies[-1].start()
    return copies


def half_kernel(cols, scale, half, pos, slabs, weight_in, weight, held, sems):
    for copy in store_half(cols, scale, 1 - bit_of(pos, 0), half, slabs, weight, held, sems):
        copy.wait()


def local_weight_kernel(heads, scale, cols, half, pos, slabs, recv, rest, w_t, *refs):
    outs, held_outs = refs[:5], refs[5:10]
    held, sems, out_sems = held_outs[4], refs[10], refs[11]
    copies = store_half(cols, scale, bit_of(pos, 0), half, slabs, outs[4], held, sems)
    moves = [pltpu.make_async_copy(held_outs[k], outs[k], out_sems.at[k]) for k in range(4)]
    local_kernel(heads, scale, recv, rest, w_t, *held_outs[:4], moves)
    for copy in copies + moves:
        copy.wait()


def write_sums(heads, scale, sums, w, table, head):
    cols = w.shape[0]
    high, low = split(sums[:, :cols])
    table[...] = (nn(high, w) + nn(low, w)) * scale
    both = sums[0:1] + sums[1:2]
    at = cols - heads
    rows = []
    for k in (1, 0, 2):
        lo = at + k * heads
        rows.append(both[:, lo : lo + heads] + both[:, lo + 3 * heads : lo + 4 * heads])
    head[...] = jnp.concatenate(rows, axis=0) * scale


def local_kernel(heads, scale, recv, rest, w_t, value, inputs, table, head, moves=()):
    levels = recv.shape[0]
    model_d = w_t.shape[1]
    cols = w_t.shape[0]
    dates = value.shape[1]
    w = w_t[...]
    ext_rows = []
    for z in range(levels):
        rows = recv[z].astype(F32)
        ext_rows.append(jnp.concatenate([rows[cols + 8 * b : cols + 8 * b + 8] for b in range(3)], axis=1))
        at = cols + 32
        values = jnp.concatenate([rows[at + 8 * b : at + 8 * b + 8] for b in range(model_d // LANES)], axis=1)
        for c in range(2):
            value[2 * z + c] = values[c * dates : (c + 1) * dates].astype(BF16)
    for move in moves[:1]:
        move.start()
    grads = nn(jnp.concatenate(ext_rows, axis=0).astype(BF16)[:, :cols], w)
    for p in range(2 * levels):
        inputs[p] = grads[p * dates : (p + 1) * dates].astype(BF16)
    for move in moves[1:2]:
        move.start()
    last = pltpu.roll(rest[0:8, :], 64, 1)
    sums = jnp.concatenate([rest[8:12, :], rest[12:16, :], last[0:4]], axis=1)
    sums = sums[0:2] + sums[2:4]
    write_sums(heads, scale, sums, w, table, head)
    for move in moves[2:]:
        move.start()


def gather_kernel(cols, half, scale, pos, own, other, out):
    tiles = own.shape[0]
    mine = bit_of(pos, 0) == 0
    for t in range(tiles):
        a = own[t].astype(F32)
        b = other[t].astype(F32)
        first = jnp.where(mine, a, b)[:cols, :half]
        second = jnp.where(mine, b, a)[:cols, :half]
        out[:, 2 * half * t : 2 * half * (t + 1)] = jnp.concatenate([first, second], axis=1) * scale


VMEM = pl.BlockSpec(memory_space=pltpu.VMEM)
SMEM = pl.BlockSpec(memory_space=pltpu.SMEM)
HBM = pl.BlockSpec(memory_space=pltpu.HBM)


def call(kernel, outs, ins, smem=0):
    return pl.pallas_call(
        kernel,
        out_shape=[jax.ShapeDtypeStruct(s, d) for s, d in outs],
        in_specs=[SMEM] * smem + [VMEM] * (len(ins) - smem),
        out_specs=[VMEM] * len(outs),
        compiler_params=pltpu.CompilerParams(vmem_limit_bytes=48 * 1024 * 1024),
    )(*ins)


def rows_block(rows):
    return [rows[:, b * LANES : (b + 1) * LANES] for b in range(rows.shape[1] // LANES)]


def block_rows(block, count):
    return jnp.concatenate([block[k : k + count] for k in range(0, block.shape[0], count)], axis=1)


def group_slab_kernel(cols, dates, pos, recv, sel, rows_own, rows_got, keep, keep_sums, rows_keep, give):
    peers, length, _ = recv.shape
    count = keep.shape[0]
    first = bit_of(pos, 0) == 0
    ext = recv[:, :, :EXT].reshape(peers * length, EXT)
    tokens = recv[:, :, EXT:].reshape(peers * length, LANES)
    part = tn(ext, tokens)[:cols]
    sums = jnp.zeros((16, EXT), F32)
    for t in range(peers):
        sums = sums + nn(sel[...], recv[t, :, :EXT])
    sums = sums[0:2]
    upper, lower = part[:count], part[cols - count :]
    keep[...] = jnp.where(first, upper, lower)
    keep_sums[...] = sums
    kept, given = halves([rows_own[...].astype(F32), rows_got[...].astype(F32)], dates, first)
    rows_keep[...] = kept.astype(BF16)
    give[...] = jnp.concatenate(
        [jnp.where(first, lower, upper)] + sum_rows(sums) + rows_block(given), axis=0
    ).astype(BF16)


def group_join_kernel(dates, pos, keep, keep_sums, rows_own, got, rows_keep, give):
    count = keep.shape[0]
    first = bit_of(pos, 2) == 0
    total = keep[...] + got[:count, :].astype(F32)
    sums = keep_sums[...] + rows_sum(got[count : count + 24, :].astype(F32))
    rows_got = block_rows(got[count + 24 :, :].astype(F32), rows_own.shape[0])
    kept, given = halves([rows_own[...].astype(F32), rows_got], dates, first)
    rows_keep[...] = kept.astype(BF16)
    give[...] = jnp.concatenate([total] + sum_rows(sums) + rows_block(given), axis=0).astype(BF16)


def group_total_kernel(own, got, send, rest):
    count = send.shape[1]
    total = own[: count + 24, :].astype(F32) + got[: count + 24, :].astype(F32)
    slab = total[:count].astype(BF16)
    for t in range(send.shape[0]):
        send[t] = slab
    rest[...] = total[count:]


def store_rows(cols, scale, core, slabs, weight, held, sems):
    count = slabs.shape[1]
    base = cols - count
    for t in range(slabs.shape[0]):
        held[:, t * LANES : (t + 1) * LANES] = slabs[t].astype(F32) * scale
    at = pl.multiple_of(core * base, 8)
    main = pltpu.make_async_copy(held.at[:base], weight.at[pl.ds(at, base)], sems.at[0])
    last = pltpu.make_async_copy(held.at[base:], weight.at[2 * base :], sems.at[1])
    main.start()

    @pl.when(core == 1)
    def _():
        last.start()

    def wait():
        main.wait()

        @pl.when(core == 1)
        def _():
            last.wait()

    return wait


def other_rows_kernel(cols, scale, pos, slabs, weight_in, weight, held, sems):
    store_rows(cols, scale, 1 - bit_of(pos, 0), slabs, weight, held, sems)()


def final_kernel(heads, scale, pos, slabs, rows_own, got, rest, w_t, *refs):
    outs, (value, inputs, table, head), (held, sems, out_sems) = refs[:5], refs[5:9], refs[9:]
    model_d, cols, dates = w_t.shape[1], w_t.shape[0], value.shape[1]
    wait = store_rows(cols, scale, bit_of(pos, 0), slabs, outs[4], held, sems)
    moves = [
        pltpu.make_async_copy(source, outs[k], out_sems.at[k])
        for k, source in enumerate((value, inputs, table, head))
    ]
    w = w_t[...]
    rows_got = block_rows(got[slabs.shape[1] + 24 :, :].astype(F32), rows_own.shape[0])
    rows = jnp.concatenate([rows_own[...].astype(F32), rows_got], axis=0)
    masks = [4 * high + core + 2 * low for high in range(2) for core in range(2) for low in range(2)]
    where_to = []
    for mask in masks:
        index = 0
        for bit in range(3):
            here = bit_of(pos, bit)
            index = index + 2**bit * (1 - here if mask >> bit & 1 else here)
        where_to.append(index)
    for k, pixel in enumerate(where_to):
        value[pixel] = rows[k * dates : (k + 1) * dates, :model_d].astype(BF16)
    moves[0].start()
    grads = nn(rows[:, model_d : model_d + EXT].astype(BF16)[:, :cols], w)
    for k, pixel in enumerate(where_to):
        inputs[pixel] = grads[k * dates : (k + 1) * dates].astype(BF16)
    moves[1].start()
    write_sums(heads, scale, rows_sum(rest[...]), w, table, head)
    for move in moves[2:]:
        move.start()
    wait()
    for move in moves:
        move.wait()


def finish_four_levels(series, w_t, date_s, heads, scale, pixel_dev, dates_dev, tiles, dates):
    length = series.shape[0]
    cols, model_d = w_t.shape
    peers = 2 * tiles
    wide = model_d + EXT
    count = (cols + 8) // 2
    half_rows = length // 2
    payload = count + 24 + half_rows * wide // LANES

    def groups(alternate):
        return [
            [t * dates + 4 * high + 2 * low + (c + alternate * t) % 2 for t in range(tiles) for low in range(2)]
            for high in range(2)
            for c in range(2)
        ]

    def across(bit):
        return [(i, i ^ 2**bit) for i in range(dates)]

    send_t, rows_own, rows_give, sel = call(
        functools.partial(series_kernel, heads, model_d, 1, 2 * dates_dev),
        [
            ((peers, length, EXT + LANES), BF16),
            ((half_rows, wide), BF16),
            ((half_rows, wide), BF16),
            ((16, length), BF16),
        ],
        [date_s, series, w_t],
        1,
    )
    recv_t = lax.all_to_all(
        send_t, ("tile", "date"), split_axis=0, concat_axis=0, tiled=True, axis_index_groups=groups(1)
    )
    rows_got = lax.ppermute(rows_give, "date", across(1))
    keep, keep_sums, rows_own, give = call(
        functools.partial(group_slab_kernel, cols, dates_dev),
        [((count, LANES), F32), ((2, EXT), F32), ((half_rows, wide), BF16), ((payload, LANES), BF16)],
        [date_s, recv_t, sel, rows_own, rows_got],
        1,
    )
    got = lax.ppermute(give, "date", across(0))
    rows_own, give = call(
        functools.partial(group_join_kernel, dates_dev),
        [((half_rows, wide), BF16), ((payload, LANES), BF16)],
        [date_s, keep, keep_sums, rows_own, got],
        1,
    )
    got = lax.ppermute(give, "date", across(2))
    send_g, rest = call(
        group_total_kernel, [((peers, count, LANES), BF16), ((24, LANES), F32)], [give, got]
    )
    recv_g = lax.all_to_all(
        send_g, ("tile", "date"), split_axis=0, concat_axis=0, tiled=True, axis_index_groups=groups(0)
    )
    other_g = lax.ppermute(recv_g, "date", across(0))
    outs = [
        jax.ShapeDtypeStruct((pixel_dev, dates_dev, model_d), BF16),
        jax.ShapeDtypeStruct((pixel_dev, dates_dev, model_d), BF16),
        jax.ShapeDtypeStruct((2, model_d), F32),
        jax.ShapeDtypeStruct((3, heads), F32),
        jax.ShapeDtypeStruct((cols, model_d), F32),
    ]
    held = [pltpu.VMEM((count, model_d), F32), pltpu.SemaphoreType.DMA((2,))]
    limit = pltpu.CompilerParams(vmem_limit_bytes=48 * 1024 * 1024)
    value, inputs, table, head, weight_t = pl.pallas_call(
        functools.partial(final_kernel, heads, scale),
        out_shape=outs,
        in_specs=[SMEM] + [VMEM] * 5,
        out_specs=[HBM] * 5,
        scratch_shapes=[pltpu.VMEM(o.shape, o.dtype) for o in outs[:4]]
        + held
        + [pltpu.SemaphoreType.DMA((4,))],
        compiler_params=limit,
    )(date_s, recv_g, rows_own, got, rest, w_t)
    weight_t = pl.pallas_call(
        functools.partial(other_rows_kernel, cols, scale),
        out_shape=outs[4],
        in_specs=[SMEM, VMEM, HBM],
        out_specs=HBM,
        scratch_shapes=held,
        input_output_aliases={2: 0},
        compiler_params=limit,
    )(date_s, other_g, weight_t)
    return value, inputs, weight_t.T, table, head


def finish_any(series, w_t, date_s, heads, scale, pixel_dev, dates_dev, tiles, dates):
    length = series.shape[0]
    cols, model_d = w_t.shape
    levels = dates // 2
    slab = model_d // tiles
    half = slab // 2
    swap = [(i, i ^ 1) for i in range(dates)]
    planes = [[2 * z + c for z in range(levels)] for c in range(2)]
    rows_core = length // 2
    send_t, own, give_rows, sel = call(
        functools.partial(series_kernel, heads, model_d, 0, dates_dev),
        [
            ((tiles, length, EXT + slab), BF16),
            ((rows_core, model_d + EXT), BF16),
            ((rows_core, model_d + EXT), BF16),
            ((16, length), BF16),
        ],
        [date_s, series, w_t],
        1,
    )
    mixed = [
        [t * dates + 2 * z + (c + t) % 2 for t in range(tiles)] for z in range(levels) for c in range(2)
    ]
    recv_t = lax.all_to_all(
        send_t, ("tile", "date"), split_axis=0, concat_axis=0, tiled=True, axis_index_groups=mixed
    )
    rows_give = cols + 24 + rows_core * (model_d + EXT) // LANES
    keep, keep_sums, give = call(
        functools.partial(slab_kernel, cols),
        [((cols, LANES), F32), ((2, EXT), F32), ((rows_give, LANES), BF16)],
        [date_s, recv_t, sel, give_rows],
        1,
    )
    got = lax.ppermute(give, "date", swap)
    rows_z = cols + 32 + model_d // 16
    (send_z,) = call(
        functools.partial(join_kernel, cols, dates_dev),
        [((levels, rows_z, LANES), BF16)],
        [date_s, keep, keep_sums, got, own],
        1,
    )
    recv_z = lax.all_to_all(
        send_z, "date", split_axis=0, concat_axis=0, tiled=True, axis_index_groups=planes
    )
    send_g, rest = call(
        functools.partial(total_kernel, cols),
        [((tiles, cols, LANES), BF16), ((16, LANES), F32)],
        [recv_z],
    )
    recv_g = lax.all_to_all(send_g, "tile", split_axis=0, concat_axis=0, tiled=True)
    local_outs = [
        ((pixel_dev, dates_dev, model_d), BF16),
        ((pixel_dev, dates_dev, model_d), BF16),
        ((2, model_d), F32),
        ((3, heads), F32),
    ]
    other_g = lax.ppermute(recv_g, "date", swap)
    if half % LANES == 0:
        weight_shape = jax.ShapeDtypeStruct((cols, model_d), F32)
        held = [pltpu.VMEM((tiles, cols, half), F32), pltpu.SemaphoreType.DMA((tiles,))]
        limit = pltpu.CompilerParams(vmem_limit_bytes=48 * 1024 * 1024)
        value, inputs, table, head, weight_t = pl.pallas_call(
            functools.partial(local_weight_kernel, heads, scale, cols, half),
            out_shape=[jax.ShapeDtypeStruct(s, d) for s, d in local_outs] + [weight_shape],
            in_specs=[SMEM] + [VMEM] * 4,
            out_specs=[HBM] * 5,
            scratch_shapes=[pltpu.VMEM(s, d) for s, d in local_outs]
            + held
            + [pltpu.SemaphoreType.DMA((4,))],
            compiler_params=limit,
        )(date_s, recv_g, recv_z, rest, w_t)
        weight_t = pl.pallas_call(
            functools.partial(half_kernel, cols, scale, half),
            out_shape=weight_shape,
            in_specs=[SMEM, VMEM, HBM],
            out_specs=HBM,
            scratch_shapes=held,
            input_output_aliases={2: 0},
            compiler_params=limit,
        )(date_s, other_g, weight_t)
    else:
        value, inputs, table, head = call(
            functools.partial(local_kernel, heads, scale), local_outs, [recv_z, rest, w_t]
        )
        (weight_t,) = call(
            functools.partial(gather_kernel, cols, half, scale),
            [((cols, model_d), F32)],
            [date_s, recv_g, other_g],
            1,
        )
    return (
        value,
        inputs,
        weight_t.T,
        table,
        head,
    )


def on_device(
    layer_input,
    head_input,
    out_grad,
    sensor_ids,
    valid_mask,
    sensor_table,
    proj_weight,
    step_bias,
    decay_log,
    skip_gain,
):
    pixel_dev, dates_dev, model_d = layer_input.shape
    heads = step_bias.shape[0]
    tiles = lax.axis_size("tile")
    dates = lax.axis_size("date")
    assert pixel_dev == dates and dates % 2 == 0
    levels = dates // 2
    length = dates * dates_dev
    slab = model_d // tiles
    half = slab // 2
    date_s = lax.axis_index("date").astype(jnp.int32).reshape(1)
    w_t = proj_weight.T
    scale = 1.0 / math.sqrt(pixel_dev * dates_dev * tiles * dates)

    operands = [
        sensor_ids,
        valid_mask.T,
        sensor_table,
        step_bias[None],
        decay_log[None],
        skip_gain[None],
        layer_input,
        head_input,
        out_grad,
    ]
    packed = pl.pallas_call(
        pack_kernel,
        out_shape=jax.ShapeDtypeStruct((pixel_dev, dates_dev, 3 * model_d + LANES), BF16),
        in_specs=[SMEM] + [HBM] * 9,
        out_specs=VMEM,
        scratch_shapes=[
            pltpu.SMEM((dates_dev,), jnp.int32),
            pltpu.VMEM((dates_dev, pixel_dev), jnp.int32),
            pltpu.VMEM((2, model_d), F32),
            pltpu.VMEM((3, heads), F32),
            pltpu.VMEM((pixel_dev, dates_dev, model_d), BF16),
            pltpu.SemaphoreType.DMA((9,)),
        ],
        compiler_params=pltpu.CompilerParams(vmem_limit_bytes=16 * 1024 * 1024),
    )(date_s, *[pltpu.with_memory_space_constraint(operand, pltpu.HBM) for operand in operands])
    series = lax.all_to_all(packed, "date", split_axis=0, concat_axis=0, tiled=True).reshape(
        length, 3 * model_d + LANES
    )

    if levels == 4 and model_d == 2 * LANES * tiles:
        finish = finish_four_levels
    else:
        finish = finish_any
    return finish(series, w_t, date_s, heads, scale, pixel_dev, dates_dev, tiles, dates)


def solution(mesh):
    in_specs = (
        P("tile", "date", None),
        P("tile", "date", None),
        P("tile", "date", None),
        P("date"),
        P("tile", "date"),
        P(),
        P(),
        P(),
        P(),
        P(),
    )
    out_specs = (P("tile", "date", None), P("tile", "date", None), P(), P(), P())
    return jax.shard_map(
        on_device, mesh=mesh, in_specs=in_specs, out_specs=out_specs, check_vma=False
    )
```

```python
import functools
import math

import jax
import jax.numpy as jnp
from jax import lax
from jax.experimental import pallas as pl
from jax.experimental.pallas import tpu as pltpu
from jax.sharding import PartitionSpec as P

NEG_FILL = -1e30
HIGHEST_PREC = lax.Precision.HIGHEST
F32 = jnp.float32
BF16 = jnp.bfloat16
LANES = 128
EXT = 384


def nt(a, b, precision=None):
    return lax.dot_general(
        a, b, (((1,), (1,)), ((), ())), preferred_element_type=F32, precision=precision
    )


def nn(a, b, precision=None):
    return lax.dot_general(
        a, b, (((1,), (0,)), ((), ())), preferred_element_type=F32, precision=precision
    )


def tn(a, b):
    return lax.dot_general(a, b, (((0,), (0,)), ((), ())), preferred_element_type=F32)


def split(x):
    high = x.astype(BF16)
    return high, (x - high.astype(F32)).astype(BF16)


def bit_of(pos, bit):
    return lax.rem(lax.div(pos[0], 2**bit), 2)


def halves(arrays, span, first):
    kept, given = [], []
    for array in arrays:
        for at in range(0, array.shape[0], 2 * span):
            a, b = array[at : at + span], array[at + span : at + 2 * span]
            kept.append(jnp.where(first, a, b))
            given.append(jnp.where(first, b, a))
    return jnp.concatenate(kept, axis=0), jnp.concatenate(given, axis=0)


def series_terms(heads, model_d, recv, w_t):
    length = recv.shape[0]
    width_p = model_d // heads
    states = (w_t.shape[0] - heads) // 2
    mixed = recv[:, :model_d]
    aux = recv[:, 3 * model_d :].astype(F32)
    gate = aux[:, 0:1]
    ids = aux[:, 1:2]
    params = []
    for at in range(2, 2 + 9 * heads, 3 * heads):
        params.append(sum(aux[0:1, at + k * heads : at + (k + 1) * heads] for k in range(3)))
    bias, rate, skip = params[0], -jnp.exp(params[1]), params[2]
    projected = nt(mixed, w_t[...])
    keys = projected[:, :states].astype(BF16)
    reads = projected[:, states : 2 * states].astype(BF16)
    step_pre = projected[:, 2 * states :] + bias
    softplus = jnp.maximum(step_pre, 0.0) + jnp.log1p(jnp.exp(-jnp.abs(step_pre)))
    steps_b = (gate * softplus).astype(BF16)
    steps = steps_b.astype(F32)

    row = lax.broadcasted_iota(jnp.int32, (length, length), 0)
    col = lax.broadcasted_iota(jnp.int32, (length, length), 1)
    upper = col >= row
    upper_f = upper.astype(F32)
    eye = (col == row).astype(F32)
    lower_b = (row >= col).astype(BF16)
    head_row = lax.broadcasted_iota(jnp.int32, (heads, heads), 0)
    head_col = lax.broadcasted_iota(jnp.int32, (heads, heads), 1)
    eye_h = (head_row == head_col).astype(F32)
    rate_col = jnp.sum(eye_h * rate, axis=1, keepdims=True)
    log_col = nn(lower_b, steps_b) * rate
    steps_t = nt(eye_h.astype(BF16), steps_b).astype(BF16)
    log_row = nn(steps_t, upper.astype(BF16)) * rate_col
    scores_t = nt(keys, reads)

    pair_t = jnp.zeros((length, length), F32)
    mixes, weighted_cols, read_rows, skip_cols = [], [], [], []
    for h in range(heads):
        lo = model_d + h * width_p
        x_h = recv[:, lo : lo + width_p]
        g_h = recv[:, lo + model_d : lo + model_d + width_p]
        dt_h = steps[:, h : h + 1]
        gap = log_row[h : h + 1, :] - log_col[:, h : h + 1]
        decay = jnp.exp(jnp.where(upper, gap, NEG_FILL))
        cross = nt(x_h, g_h)
        mix = decay * scores_t
        pair_t = pair_t + decay * cross * dt_h
        both = mix * cross
        weighted = jnp.sum(both, axis=1, keepdims=True)
        weighted_cols.append(weighted)
        read_rows.append(jnp.sum(both * dt_h, axis=0, keepdims=True))
        skip_cols.append(jnp.sum(cross * eye, axis=1, keepdims=True))
        mixes.append((mix.astype(BF16), g_h, dt_h, skip[:, h : h + 1]))

    weighted = jnp.concatenate(weighted_cols, axis=1)
    read_sum = jnp.concatenate(read_rows, axis=0)
    skip_terms = jnp.concatenate(skip_cols, axis=1)
    later = nt(upper_f, read_sum, HIGHEST_PREC) - nn(upper_f, steps * weighted, HIGHEST_PREC)
    step_grad = (weighted + rate * later).astype(BF16).astype(F32)
    decay_terms = steps * later * rate
    pair_b = pair_t.astype(BF16)
    grad_keys = nn(pair_b, reads)
    grad_reads = tn(pair_b, keys)
    raw = step_grad * gate * jax.nn.sigmoid(step_pre)
    terms = jnp.concatenate(
        [raw, decay_terms, skip_terms, jnp.zeros((length, LANES - 3 * heads), F32)], axis=1
    )
    ids_row = jnp.sum(eye * ids, axis=0, keepdims=True)
    return mixes, grad_keys, grad_reads, raw, terms, ids_row, eye_h


def value_columns(mixes):
    return [nn(mix, g_h) * dt_h + skip_h * g_h.astype(F32) for mix, g_h, dt_h, skip_h in mixes]


def sensor_rows(ids_row):
    zeros = jnp.zeros((14, ids_row.shape[1]), F32)
    return jnp.concatenate([1.0 - ids_row, ids_row, zeros], axis=0).astype(BF16)


def series_kernel(heads, model_d, bit, span, pos, recv, w_t, send, own, give, sel):
    tiles, _, width = send.shape
    slab = width - EXT
    mixes, grad_keys, grad_reads, _, terms, ids_row, _ = series_terms(heads, model_d, recv, w_t)
    high = terms.astype(BF16).astype(F32)
    tail = high + pltpu.roll(terms - high, 3 * heads, 1)
    ext_f = jnp.concatenate([grad_keys, grad_reads, tail], axis=1)
    ext = ext_f.astype(BF16)
    back = jnp.concatenate(value_columns(mixes) + [ext_f], axis=1)
    kept, given = halves([back], span, bit_of(pos, bit) == 0)
    own[...] = kept.astype(BF16)
    give[...] = given.astype(BF16)
    for t in range(tiles):
        send[t, :, :EXT] = ext
        send[t, :, EXT:] = recv[:, t * slab : (t + 1) * slab]
    sel[...] = sensor_rows(ids_row)


def group_series_kernel(heads, model_d, bit, span, pos, recv, w_t, send, own, give, sel, grads, sems):
    peers, length = send.shape[0], recv.shape[0]
    copies = []
    for t in range(peers):
        copies.append(
            pltpu.make_async_copy(
                recv.at[:, t * LANES : (t + 1) * LANES], send.at[t, :length], sems.at[0, t]
            )
        )
        copies[-1].start()
    mixes, grad_keys, grad_reads, raw, terms, ids_row, eye_h = series_terms(heads, model_d, recv, w_t)
    raw_b = raw.astype(BF16)
    raw_t = nt(eye_h.astype(BF16), raw_b)
    total = jnp.sum(terms, axis=0, keepdims=True)
    high = total.astype(BF16).astype(F32)
    misc = jnp.concatenate(
        [lane_pad(raw_t, LANES), high, total - high, jnp.zeros((6, LANES), F32)], axis=0
    )
    grads[...] = jnp.concatenate([grad_keys, grad_reads, misc], axis=0).astype(BF16)
    for t in range(peers):
        copies.append(pltpu.make_async_copy(grads, send.at[t, length:], sems.at[1, t]))
        copies[-1].start()
    back = jnp.concatenate(value_columns(mixes) + [grad_keys, grad_reads, lane_pad(raw, LANES)], axis=1)
    kept, given = halves([back], span, bit_of(pos, bit) == 0)
    own[...] = kept.astype(BF16)
    give[...] = given.astype(BF16)
    sel[...] = jnp.concatenate([sensor_rows(ids_row)] * peers, axis=1)
    for copy in copies:
        copy.wait()


def pack_kernel(core, ids_in, mask_in, table_in, bias_in, decay_in, skip_in, layer, values, cotangent, out, ids, mask_t, table, params, layer_v, sems):
    pixels, dates, model_d = layer.shape
    small = [
        pltpu.make_async_copy(ids_in, ids, sems.at[0]),
        pltpu.make_async_copy(mask_in, mask_t, sems.at[1]),
        pltpu.make_async_copy(table_in, table, sems.at[2]),
        pltpu.make_async_copy(layer, layer_v, sems.at[3]),
        pltpu.make_async_copy(bias_in, params.at[0:1], sems.at[6]),
        pltpu.make_async_copy(decay_in, params.at[1:2], sems.at[7]),
        pltpu.make_async_copy(skip_in, params.at[2:3], sems.at[8]),
    ]
    large = [
        pltpu.make_async_copy(values, out.at[:, :, model_d : 2 * model_d], sems.at[4]),
        pltpu.make_async_copy(cotangent, out.at[:, :, 2 * model_d : 3 * model_d], sems.at[5]),
    ]
    for copy in small[3:4] + large + small[:3] + small[4:]:
        copy.start()
    for copy in small:
        copy.wait()
    rows = [jnp.where(ids[i] == 1, table[1:2, :], table[0:1, :]) for i in range(dates)]
    embed = jnp.concatenate(rows, axis=0)
    row = lax.broadcasted_iota(jnp.int32, (dates, LANES), 0)
    lane = lax.broadcasted_iota(jnp.int32, (dates, LANES), 1)
    second = jnp.zeros((dates, LANES), F32)
    for i in range(dates):
        second = jnp.where((row == i) & (lane == 1), (ids[i] == 1).astype(F32), second)
    gate = mask_t[...].astype(F32)
    at = 2
    for k in range(3):
        rest = params[k : k + 1, :]
        for _ in range(3):
            term = rest.astype(BF16).astype(F32)
            rest = rest - term
            term = jnp.concatenate([jnp.zeros((1, at), F32), term, jnp.zeros((1, LANES - at - term.shape[1]), F32)], axis=1)
            second = second + term
            at = at + params.shape[1]
    for p in range(pixels):
        out[p, :, 3 * model_d :] = jnp.where(lane == 0, gate[:, p : p + 1], second).astype(BF16)
        out[p, :, :model_d] = (layer_v[p].astype(F32) + embed).astype(BF16)
    for copy in large:
        copy.wait()


def lane_pad(x, width):
    if x.shape[1] == width:
        return x
    return jnp.concatenate([x, jnp.zeros((x.shape[0], width - x.shape[1]), x.dtype)], axis=1)


def sum_rows(sums):
    high = sums.astype(BF16).astype(F32)
    low = (sums - high).astype(BF16).astype(F32)
    rows = jnp.concatenate([high, low, jnp.zeros((4, EXT), F32)], axis=0)
    return [rows[:, b * LANES : (b + 1) * LANES] for b in range(EXT // LANES)]


def rows_sum(block):
    rows = jnp.concatenate([block[8 * b : 8 * b + 8, :] for b in range(EXT // LANES)], axis=1)
    return rows[0:2] + rows[2:4]


def slab_kernel(cols, pos, recv, sel, rows, keep, keep_sums, give):
    tiles, length, width = recv.shape
    slab = width - EXT
    half = slab // 2
    ext = recv[:, :, :EXT].reshape(tiles * length, EXT)
    tokens = recv[:, :, EXT:].reshape(tiles * length, slab)
    part = tn(ext, tokens)[:cols]
    sums = jnp.zeros((16, EXT), F32)
    for t in range(tiles):
        sums = sums + nn(sel[...], recv[t, :, :EXT])
    sums = sums[0:2]
    mine = bit_of(pos, 0) == 0
    first = lane_pad(part[:, :half], LANES)
    second = lane_pad(part[:, half:], LANES)
    keep[...] = jnp.where(mine, first, second)
    keep_sums[...] = sums
    other = jnp.where(mine, second, first)
    blocks = [rows[:, b * LANES : (b + 1) * LANES].astype(F32) for b in range(rows.shape[1] // LANES)]
    give[...] = jnp.concatenate([other] + sum_rows(sums) + blocks, axis=0).astype(BF16)


def join_kernel(cols, dates, pos, keep, keep_sums, got, own, send):
    levels = send.shape[0]
    first = bit_of(pos, 0) == 0
    model_d = own.shape[1] - EXT
    total = keep[...] + got[:cols, :].astype(F32)
    sums = sum_rows(keep_sums[...] + rows_sum(got[cols : cols + 24, :].astype(F32)))
    pair_sums = jnp.concatenate([sums[0][:4], sums[1][:4]], axis=0)
    mine, count = own[...].astype(F32), own.shape[0]
    tall = got[cols + 24 :, :].astype(F32)
    theirs = jnp.concatenate([tall[k : k + count] for k in range(0, tall.shape[0], count)], axis=1)
    firsts, seconds = jnp.where(first, mine, theirs), jnp.where(first, theirs, mine)
    lane = lax.broadcasted_iota(jnp.int32, (8, LANES), 1)
    last = pltpu.roll(sums[2], 64, 1)
    for z in range(levels):
        at = z * dates
        rows = jnp.concatenate([firsts[at : at + dates], seconds[at : at + dates]], axis=0)
        ext = [rows[:, model_d + b * LANES : model_d + (b + 1) * LANES] for b in range(EXT // LANES)]
        misc = jnp.where(lane < 64, ext[2], last)
        value = [rows[:, b * LANES : (b + 1) * LANES] for b in range(model_d // LANES)]
        send[z] = jnp.concatenate([total, ext[0], ext[1], misc, pair_sums] + value, axis=0).astype(BF16)


def total_kernel(cols, recv, send, rest):
    levels = recv.shape[0]
    total = recv[0].astype(F32)
    for z in range(1, levels):
        total = total + recv[z].astype(F32)
    slab = total[:cols].astype(BF16)
    for t in range(send.shape[0]):
        send[t] = slab
    rest[...] = total[cols + 16 : cols + 32]


def store_half(cols, scale, core, half, slabs, weight, held, sems):
    copies = []
    for t in range(slabs.shape[0]):
        held[t] = slabs[t].astype(F32)[:cols] * scale
        at = pl.multiple_of((2 * t + core) * half, half)
        copies.append(pltpu.make_async_copy(held.at[t], weight.at[:, pl.ds(at, half)], sems.at[t]))
        copies[-1].start()
    return copies


def half_kernel(cols, scale, half, pos, slabs, weight_in, weight, held, sems):
    for copy in store_half(cols, scale, 1 - bit_of(pos, 0), half, slabs, weight, held, sems):
        copy.wait()


def local_weight_kernel(heads, scale, cols, half, pos, slabs, recv, rest, w_t, *refs):
    outs, held_outs = refs[:5], refs[5:10]
    held, sems, out_sems = held_outs[4], refs[10], refs[11]
    copies = store_half(cols, scale, bit_of(pos, 0), half, slabs, outs[4], held, sems)
    moves = [pltpu.make_async_copy(held_outs[k], outs[k], out_sems.at[k]) for k in range(4)]
    local_kernel(heads, scale, recv, rest, w_t, *held_outs[:4], moves)
    for copy in copies + moves:
        copy.wait()


def write_sums(heads, scale, sums, w, table, head):
    cols = w.shape[0]
    high, low = split(sums[:, :cols])
    table[...] = (nn(high, w) + nn(low, w)) * scale
    both = sums[0:1] + sums[1:2]
    at = cols - heads
    rows = []
    for k in (1, 0, 2):
        lo = at + k * heads
        rows.append(both[:, lo : lo + heads] + both[:, lo + 3 * heads : lo + 4 * heads])
    head[...] = jnp.concatenate(rows, axis=0) * scale


def local_kernel(heads, scale, recv, rest, w_t, value, inputs, table, head, moves=()):
    levels = recv.shape[0]
    model_d = w_t.shape[1]
    cols = w_t.shape[0]
    dates = value.shape[1]
    w = w_t[...]
    ext_rows = []
    for z in range(levels):
        rows = recv[z].astype(F32)
        ext_rows.append(jnp.concatenate([rows[cols + 8 * b : cols + 8 * b + 8] for b in range(3)], axis=1))
        at = cols + 32
        values = jnp.concatenate([rows[at + 8 * b : at + 8 * b + 8] for b in range(model_d // LANES)], axis=1)
        for c in range(2):
            value[2 * z + c] = values[c * dates : (c + 1) * dates].astype(BF16)
    for move in moves[:1]:
        move.start()
    grads = nn(jnp.concatenate(ext_rows, axis=0).astype(BF16)[:, :cols], w)
    for p in range(2 * levels):
        inputs[p] = grads[p * dates : (p + 1) * dates].astype(BF16)
    for move in moves[1:2]:
        move.start()
    last = pltpu.roll(rest[0:8, :], 64, 1)
    sums = jnp.concatenate([rest[8:12, :], rest[12:16, :], last[0:4]], axis=1)
    sums = sums[0:2] + sums[2:4]
    write_sums(heads, scale, sums, w, table, head)
    for move in moves[2:]:
        move.start()


def gather_kernel(cols, half, scale, pos, own, other, out):
    tiles = own.shape[0]
    mine = bit_of(pos, 0) == 0
    for t in range(tiles):
        a = own[t].astype(F32)
        b = other[t].astype(F32)
        first = jnp.where(mine, a, b)[:cols, :half]
        second = jnp.where(mine, b, a)[:cols, :half]
        out[:, 2 * half * t : 2 * half * (t + 1)] = jnp.concatenate([first, second], axis=1) * scale


VMEM = pl.BlockSpec(memory_space=pltpu.VMEM)
SMEM = pl.BlockSpec(memory_space=pltpu.SMEM)
HBM = pl.BlockSpec(memory_space=pltpu.HBM)


def call(kernel, outs, ins, smem=0):
    return pl.pallas_call(
        kernel,
        out_shape=[jax.ShapeDtypeStruct(s, d) for s, d in outs],
        in_specs=[SMEM] * smem + [VMEM] * (len(ins) - smem),
        out_specs=[VMEM] * len(outs),
        compiler_params=pltpu.CompilerParams(vmem_limit_bytes=48 * 1024 * 1024),
    )(*ins)


def rows_block(rows):
    return [rows[:, b * LANES : (b + 1) * LANES] for b in range(rows.shape[1] // LANES)]


def block_rows(block, count):
    return jnp.concatenate([block[k : k + count] for k in range(0, block.shape[0], count)], axis=1)


def pack_sums(sums):
    high = sums.astype(BF16).astype(F32)
    return jnp.concatenate([high, sums - high], axis=0)


def unpack_sums(rows):
    return rows[:8] + rows[8:16]


def group_slab_kernel(dates, pos, recv, sel, rows_own, rows_got, keep, keep_sums, rows_keep, give):
    peers = recv.shape[0]
    length = sel.shape[1] // peers
    count = keep.shape[0]
    first = bit_of(pos, 0) == 0
    tokens = recv[:, :length, :].reshape(peers * length, LANES)
    keys = recv[:, length : 2 * length, :].reshape(peers * length, LANES)
    reads = recv[:, 2 * length : 3 * length, :].reshape(peers * length, LANES)
    misc = [recv[t, 3 * length :, :] for t in range(peers)]
    raw_t = jnp.concatenate([m[:, :length] for m in misc], axis=1)
    part = jnp.concatenate([tn(keys, tokens), tn(reads, tokens), nn(raw_t, tokens)[: count - LANES]], axis=0)
    chosen = sel[...]
    head = sum(m.astype(F32) for m in misc)[8:10]
    sums = jnp.concatenate(
        [
            nn(chosen, keys)[0:2],
            nn(chosen, reads)[0:2],
            lane_pad(nt(chosen, raw_t)[0:2], LANES),
            head[0:1] + head[1:2],
            jnp.zeros((1, LANES), F32),
        ],
        axis=0,
    )
    upper, lower = part[:count], part[part.shape[0] - count :]
    keep[...] = jnp.where(first, upper, lower)
    keep_sums[...] = sums
    kept, given = halves([rows_own[...].astype(F32), rows_got[...].astype(F32)], dates, first)
    rows_keep[...] = kept.astype(BF16)
    give[...] = jnp.concatenate(
        [jnp.where(first, lower, upper), pack_sums(sums)] + rows_block(given), axis=0
    ).astype(BF16)


def group_join_kernel(dates, pos, keep, keep_sums, rows_own, got, rows_keep, give):
    count = keep.shape[0]
    first = bit_of(pos, 2) == 0
    there = got[...].astype(F32)
    total = keep[...] + there[:count]
    sums = keep_sums[...] + unpack_sums(there[count : count + 16])
    rows_got = block_rows(there[count + 16 :], rows_own.shape[0])
    kept, given = halves([rows_own[...].astype(F32), rows_got], dates, first)
    rows_keep[...] = kept.astype(BF16)
    give[...] = jnp.concatenate([total, pack_sums(sums)] + rows_block(given), axis=0).astype(BF16)


def group_total_kernel(own, got, send, rest):
    count = send.shape[1]
    total = (own[...].astype(F32) + got[...].astype(F32))[: count + 16]
    slab = total[:count].astype(BF16)
    for t in range(send.shape[0]):
        send[t] = slab
    rest[...] = unpack_sums(total[count:])


def store_rows(cols, scale, core, slabs, weight, held, sems):
    count = slabs.shape[1]
    base = cols - count
    for t in range(slabs.shape[0]):
        held[:, t * LANES : (t + 1) * LANES] = slabs[t].astype(F32) * scale
    at = pl.multiple_of(core * base, 8)
    main = pltpu.make_async_copy(held.at[:base], weight.at[pl.ds(at, base)], sems.at[0])
    last = pltpu.make_async_copy(held.at[base:], weight.at[2 * base :], sems.at[1])
    main.start()

    @pl.when(core == 1)
    def _():
        last.start()

    def wait():
        main.wait()

        @pl.when(core == 1)
        def _():
            last.wait()

    return wait


def other_rows_kernel(cols, scale, pos, slabs, weight_in, weight, held, sems):
    store_rows(cols, scale, 1 - bit_of(pos, 0), slabs, weight, held, sems)()


def final_kernel(heads, scale, pos, slabs, rows_own, got, rest, w_t, *refs):
    outs, (value, inputs, table, head), (held, sems, out_sems) = refs[:5], refs[5:9], refs[9:]
    model_d, cols, dates = w_t.shape[1], w_t.shape[0], value.shape[1]
    wait = store_rows(cols, scale, bit_of(pos, 0), slabs, outs[4], held, sems)
    moves = [
        pltpu.make_async_copy(source, outs[k], out_sems.at[k])
        for k, source in enumerate((value, inputs, table, head))
    ]
    w = w_t[...]
    rows_got = block_rows(got[...].astype(F32)[slabs.shape[1] + 16 :], rows_own.shape[0])
    rows = jnp.concatenate([rows_own[...].astype(F32), rows_got], axis=0)
    masks = [4 * high + core + 2 * low for high in range(2) for core in range(2) for low in range(2)]
    where_to = []
    for mask in masks:
        index = 0
        for bit in range(3):
            here = bit_of(pos, bit)
            index = index + 2**bit * (1 - here if mask >> bit & 1 else here)
        where_to.append(index)
    for k, pixel in enumerate(where_to):
        value[pixel] = rows[k * dates : (k + 1) * dates, :model_d].astype(BF16)
    moves[0].start()
    grads = nn(rows[:, model_d : model_d + EXT].astype(BF16)[:, :cols], w)
    for k, pixel in enumerate(where_to):
        inputs[pixel] = grads[k * dates : (k + 1) * dates].astype(BF16)
    moves[1].start()
    sums = jnp.concatenate([rest[0:2, :], rest[2:4, :], rest[4:6, :]], axis=1)[:, :cols]
    high, low = split(sums)
    table[...] = (nn(high, w) + nn(low, w)) * scale
    total = rest[6:7, :]
    head[...] = jnp.concatenate([total[:, k * heads : (k + 1) * heads] for k in (1, 0, 2)], axis=0) * scale
    for move in moves[2:]:
        move.start()
    wait()
    for move in moves:
        move.wait()


def finish_four_levels(series, w_t, date_s, heads, scale, pixel_dev, dates_dev, tiles, dates):
    length = series.shape[0]
    cols, model_d = w_t.shape
    peers = 2 * tiles
    wide = model_d + EXT
    count = (cols + 8) // 2
    half_rows = length // 2
    payload = count + 16 + half_rows * wide // LANES

    def groups(alternate):
        return [
            [t * dates + 4 * high + 2 * low + (c + alternate * t) % 2 for t in range(tiles) for low in range(2)]
            for high in range(2)
            for c in range(2)
        ]

    def across(bit):
        return [(i, i ^ 2**bit) for i in range(dates)]

    send_t, rows_own, rows_give, sel = pl.pallas_call(
        functools.partial(group_series_kernel, heads, model_d, 1, 2 * dates_dev),
        out_shape=[
            jax.ShapeDtypeStruct((peers, 3 * length + 16, LANES), BF16),
            jax.ShapeDtypeStruct((half_rows, wide), BF16),
            jax.ShapeDtypeStruct((half_rows, wide), BF16),
            jax.ShapeDtypeStruct((16, peers * length), BF16),
        ],
        in_specs=[SMEM, VMEM, VMEM],
        out_specs=[HBM, VMEM, VMEM, VMEM],
        scratch_shapes=[
            pltpu.VMEM((2 * length + 16, LANES), BF16),
            pltpu.SemaphoreType.DMA((2, peers)),
        ],
        compiler_params=pltpu.CompilerParams(vmem_limit_bytes=48 * 1024 * 1024),
    )(date_s, series, w_t)
    recv_t = lax.all_to_all(
        send_t, ("tile", "date"), split_axis=0, concat_axis=0, tiled=True, axis_index_groups=groups(1)
    )
    rows_got = lax.ppermute(rows_give, "date", across(1))
    keep, keep_sums, rows_own, give = call(
        functools.partial(group_slab_kernel, dates_dev),
        [((count, LANES), F32), ((8, LANES), F32), ((half_rows, wide), BF16), ((payload, LANES), BF16)],
        [date_s, recv_t, sel, rows_own, rows_got],
        1,
    )
    got = lax.ppermute(give, "date", across(0))
    rows_own, give = call(
        functools.partial(group_join_kernel, dates_dev),
        [((half_rows, wide), BF16), ((payload, LANES), BF16)],
        [date_s, keep, keep_sums, rows_own, got],
        1,
    )
    got = lax.ppermute(give, "date", across(2))
    send_g, rest = call(
        group_total_kernel, [((peers, count, LANES), BF16), ((8, LANES), F32)], [give, got]
    )
    recv_g = lax.all_to_all(
        send_g, ("tile", "date"), split_axis=0, concat_axis=0, tiled=True, axis_index_groups=groups(0)
    )
    other_g = lax.ppermute(recv_g, "date", across(0))
    outs = [
        jax.ShapeDtypeStruct((pixel_dev, dates_dev, model_d), BF16),
        jax.ShapeDtypeStruct((pixel_dev, dates_dev, model_d), BF16),
        jax.ShapeDtypeStruct((2, model_d), F32),
        jax.ShapeDtypeStruct((3, heads), F32),
        jax.ShapeDtypeStruct((cols, model_d), F32),
    ]
    held = [pltpu.VMEM((count, model_d), F32), pltpu.SemaphoreType.DMA((2,))]
    limit = pltpu.CompilerParams(vmem_limit_bytes=48 * 1024 * 1024)
    value, inputs, table, head, weight_t = pl.pallas_call(
        functools.partial(final_kernel, heads, scale),
        out_shape=outs,
        in_specs=[SMEM] + [VMEM] * 5,
        out_specs=[HBM] * 5,
        scratch_shapes=[pltpu.VMEM(o.shape, o.dtype) for o in outs[:4]]
        + held
        + [pltpu.SemaphoreType.DMA((4,))],
        compiler_params=limit,
    )(date_s, recv_g, rows_own, got, rest, w_t)
    weight_t = pl.pallas_call(
        functools.partial(other_rows_kernel, cols, scale),
        out_shape=outs[4],
        in_specs=[SMEM, VMEM, HBM],
        out_specs=HBM,
        scratch_shapes=held,
        input_output_aliases={2: 0},
        compiler_params=limit,
    )(date_s, other_g, weight_t)
    return value, inputs, weight_t.T, table, head


def finish_any(series, w_t, date_s, heads, scale, pixel_dev, dates_dev, tiles, dates):
    length = series.shape[0]
    cols, model_d = w_t.shape
    levels = dates // 2
    slab = model_d // tiles
    half = slab // 2
    swap = [(i, i ^ 1) for i in range(dates)]
    planes = [[2 * z + c for z in range(levels)] for c in range(2)]
    rows_core = length // 2
    send_t, own, give_rows, sel = call(
        functools.partial(series_kernel, heads, model_d, 0, dates_dev),
        [
            ((tiles, length, EXT + slab), BF16),
            ((rows_core, model_d + EXT), BF16),
            ((rows_core, model_d + EXT), BF16),
            ((16, length), BF16),
        ],
        [date_s, series, w_t],
        1,
    )
    mixed = [
        [t * dates + 2 * z + (c + t) % 2 for t in range(tiles)] for z in range(levels) for c in range(2)
    ]
    recv_t = lax.all_to_all(
        send_t, ("tile", "date"), split_axis=0, concat_axis=0, tiled=True, axis_index_groups=mixed
    )
    rows_give = cols + 24 + rows_core * (model_d + EXT) // LANES
    keep, keep_sums, give = call(
        functools.partial(slab_kernel, cols),
        [((cols, LANES), F32), ((2, EXT), F32), ((rows_give, LANES), BF16)],
        [date_s, recv_t, sel, give_rows],
        1,
    )
    got = lax.ppermute(give, "date", swap)
    rows_z = cols + 32 + model_d // 16
    (send_z,) = call(
        functools.partial(join_kernel, cols, dates_dev),
        [((levels, rows_z, LANES), BF16)],
        [date_s, keep, keep_sums, got, own],
        1,
    )
    recv_z = lax.all_to_all(
        send_z, "date", split_axis=0, concat_axis=0, tiled=True, axis_index_groups=planes
    )
    send_g, rest = call(
        functools.partial(total_kernel, cols),
        [((tiles, cols, LANES), BF16), ((16, LANES), F32)],
        [recv_z],
    )
    recv_g = lax.all_to_all(send_g, "tile", split_axis=0, concat_axis=0, tiled=True)
    local_outs = [
        ((pixel_dev, dates_dev, model_d), BF16),
        ((pixel_dev, dates_dev, model_d), BF16),
        ((2, model_d), F32),
        ((3, heads), F32),
    ]
    other_g = lax.ppermute(recv_g, "date", swap)
    if half % LANES == 0:
        weight_shape = jax.ShapeDtypeStruct((cols, model_d), F32)
        held = [pltpu.VMEM((tiles, cols, half), F32), pltpu.SemaphoreType.DMA((tiles,))]
        limit = pltpu.CompilerParams(vmem_limit_bytes=48 * 1024 * 1024)
        value, inputs, table, head, weight_t = pl.pallas_call(
            functools.partial(local_weight_kernel, heads, scale, cols, half),
            out_shape=[jax.ShapeDtypeStruct(s, d) for s, d in local_outs] + [weight_shape],
            in_specs=[SMEM] + [VMEM] * 4,
            out_specs=[HBM] * 5,
            scratch_shapes=[pltpu.VMEM(s, d) for s, d in local_outs]
            + held
            + [pltpu.SemaphoreType.DMA((4,))],
            compiler_params=limit,
        )(date_s, recv_g, recv_z, rest, w_t)
        weight_t = pl.pallas_call(
            functools.partial(half_kernel, cols, scale, half),
            out_shape=weight_shape,
            in_specs=[SMEM, VMEM, HBM],
            out_specs=HBM,
            scratch_shapes=held,
            input_output_aliases={2: 0},
            compiler_params=limit,
        )(date_s, other_g, weight_t)
    else:
        value, inputs, table, head = call(
            functools.partial(local_kernel, heads, scale), local_outs, [recv_z, rest, w_t]
        )
        (weight_t,) = call(
            functools.partial(gather_kernel, cols, half, scale),
            [((cols, model_d), F32)],
            [date_s, recv_g, other_g],
            1,
        )
    return (
        value,
        inputs,
        weight_t.T,
        table,
        head,
    )


def on_device(
    layer_input,
    head_input,
    out_grad,
    sensor_ids,
    valid_mask,
    sensor_table,
    proj_weight,
    step_bias,
    decay_log,
    skip_gain,
):
    pixel_dev, dates_dev, model_d = layer_input.shape
    heads = step_bias.shape[0]
    tiles = lax.axis_size("tile")
    dates = lax.axis_size("date")
    assert pixel_dev == dates and dates % 2 == 0
    levels = dates // 2
    length = dates * dates_dev
    slab = model_d // tiles
    half = slab // 2
    date_s = lax.axis_index("date").astype(jnp.int32).reshape(1)
    w_t = proj_weight.T
    scale = 1.0 / math.sqrt(pixel_dev * dates_dev * tiles * dates)

    operands = [
        sensor_ids,
        valid_mask.T,
        sensor_table,
        step_bias[None],
        decay_log[None],
        skip_gain[None],
        layer_input,
        head_input,
        out_grad,
    ]
    packed = pl.pallas_call(
        pack_kernel,
        out_shape=jax.ShapeDtypeStruct((pixel_dev, dates_dev, 3 * model_d + LANES), BF16),
        in_specs=[SMEM] + [HBM] * 9,
        out_specs=VMEM,
        scratch_shapes=[
            pltpu.SMEM((dates_dev,), jnp.int32),
            pltpu.VMEM((dates_dev, pixel_dev), jnp.int32),
            pltpu.VMEM((2, model_d), F32),
            pltpu.VMEM((3, heads), F32),
            pltpu.VMEM((pixel_dev, dates_dev, model_d), BF16),
            pltpu.SemaphoreType.DMA((9,)),
        ],
        compiler_params=pltpu.CompilerParams(vmem_limit_bytes=16 * 1024 * 1024),
    )(date_s, *[pltpu.with_memory_space_constraint(operand, pltpu.HBM) for operand in operands])
    series = lax.all_to_all(packed, "date", split_axis=0, concat_axis=0, tiled=True).reshape(
        length, 3 * model_d + LANES
    )

    if levels == 4 and model_d == 2 * LANES * tiles:
        finish = finish_four_levels
    else:
        finish = finish_any
    return finish(series, w_t, date_s, heads, scale, pixel_dev, dates_dev, tiles, dates)


def solution(mesh):
    in_specs = (
        P("tile", "date", None),
        P("tile", "date", None),
        P("tile", "date", None),
        P("date"),
        P("tile", "date"),
        P(),
        P(),
        P(),
        P(),
        P(),
    )
    out_specs = (P("tile", "date", None), P("tile", "date", None), P(), P(), P())
    return jax.shard_map(
        on_device, mesh=mesh, in_specs=in_specs, out_specs=out_specs, check_vma=False
    )
```

```python
import functools
import math

import jax
import jax.numpy as jnp
from jax import lax
from jax.experimental import pallas as pl
from jax.experimental.pallas import tpu as pltpu
from jax.sharding import PartitionSpec as P

NEG_FILL = -1e30
HIGHEST_PREC = lax.Precision.HIGHEST
F32 = jnp.float32
BF16 = jnp.bfloat16
LANES = 128
EXT = 384


def nt(a, b, precision=None):
    return lax.dot_general(
        a, b, (((1,), (1,)), ((), ())), preferred_element_type=F32, precision=precision
    )


def nn(a, b, precision=None):
    return lax.dot_general(
        a, b, (((1,), (0,)), ((), ())), preferred_element_type=F32, precision=precision
    )


def tn(a, b):
    return lax.dot_general(a, b, (((0,), (0,)), ((), ())), preferred_element_type=F32)


def split(x):
    high = x.astype(BF16)
    return high, (x - high.astype(F32)).astype(BF16)


def bit_of(pos, bit):
    return lax.rem(lax.div(pos[0], 2**bit), 2)


def halves(arrays, span, first):
    kept, given = [], []
    for array in arrays:
        for at in range(0, array.shape[0], 2 * span):
            a, b = array[at : at + span], array[at + span : at + 2 * span]
            kept.append(jnp.where(first, a, b))
            given.append(jnp.where(first, b, a))
    return jnp.concatenate(kept, axis=0), jnp.concatenate(given, axis=0)


def series_terms(heads, model_d, recv, w_t):
    length = recv.shape[0]
    width_p = model_d // heads
    states = (w_t.shape[0] - heads) // 2
    mixed = recv[:, :model_d]
    aux = recv[:, 3 * model_d :].astype(F32)
    gate = aux[:, 0:1]
    ids = aux[:, 1:2]
    params = []
    for at in range(2, 2 + 9 * heads, 3 * heads):
        params.append(sum(aux[0:1, at + k * heads : at + (k + 1) * heads] for k in range(3)))
    bias, rate, skip = params[0], -jnp.exp(params[1]), params[2]
    projected = nt(mixed, w_t[...])
    keys = projected[:, :states].astype(BF16)
    reads = projected[:, states : 2 * states].astype(BF16)
    step_pre = projected[:, 2 * states :] + bias
    softplus = jnp.maximum(step_pre, 0.0) + jnp.log1p(jnp.exp(-jnp.abs(step_pre)))
    steps_b = (gate * softplus).astype(BF16)
    steps = steps_b.astype(F32)

    row = lax.broadcasted_iota(jnp.int32, (length, length), 0)
    col = lax.broadcasted_iota(jnp.int32, (length, length), 1)
    upper = col >= row
    upper_f = upper.astype(F32)
    eye = (col == row).astype(F32)
    lower_b = (row >= col).astype(BF16)
    head_row = lax.broadcasted_iota(jnp.int32, (heads, heads), 0)
    head_col = lax.broadcasted_iota(jnp.int32, (heads, heads), 1)
    eye_h = (head_row == head_col).astype(F32)
    rate_col = jnp.sum(eye_h * rate, axis=1, keepdims=True)
    log_col = nn(lower_b, steps_b) * rate
    steps_t = nt(eye_h.astype(BF16), steps_b).astype(BF16)
    log_row = nn(steps_t, upper.astype(BF16)) * rate_col
    scores_t = nt(keys, reads)

    pair_t = jnp.zeros((length, length), F32)
    mixes, weighted_cols, read_rows, skip_cols = [], [], [], []
    for h in range(heads):
        lo = model_d + h * width_p
        x_h = recv[:, lo : lo + width_p]
        g_h = recv[:, lo + model_d : lo + model_d + width_p]
        dt_h = steps[:, h : h + 1]
        gap = log_row[h : h + 1, :] - log_col[:, h : h + 1]
        decay = jnp.exp(jnp.where(upper, gap, NEG_FILL))
        cross = nt(x_h, g_h)
        mix = decay * scores_t
        pair_t = pair_t + decay * cross * dt_h
        both = mix * cross
        weighted = jnp.sum(both, axis=1, keepdims=True)
        weighted_cols.append(weighted)
        read_rows.append(jnp.sum(both * dt_h, axis=0, keepdims=True))
        skip_cols.append(jnp.sum(cross * eye, axis=1, keepdims=True))
        mixes.append((mix.astype(BF16), g_h, dt_h, skip[:, h : h + 1]))

    weighted = jnp.concatenate(weighted_cols, axis=1)
    read_sum = jnp.concatenate(read_rows, axis=0)
    skip_terms = jnp.concatenate(skip_cols, axis=1)
    later = nt(upper_f, read_sum, HIGHEST_PREC) - nn(upper_f, steps * weighted, HIGHEST_PREC)
    step_grad = (weighted + rate * later).astype(BF16).astype(F32)
    decay_terms = steps * later * rate
    pair_b = pair_t.astype(BF16)
    grad_keys = nn(pair_b, reads)
    grad_reads = tn(pair_b, keys)
    raw = step_grad * gate * jax.nn.sigmoid(step_pre)
    terms = jnp.concatenate(
        [raw, decay_terms, skip_terms, jnp.zeros((length, LANES - 3 * heads), F32)], axis=1
    )
    ids_row = jnp.sum(eye * ids, axis=0, keepdims=True)
    return mixes, grad_keys, grad_reads, raw, terms, ids_row, eye_h


def value_columns(mixes):
    return [nn(mix, g_h) * dt_h + skip_h * g_h.astype(F32) for mix, g_h, dt_h, skip_h in mixes]


def sensor_rows(ids_row):
    zeros = jnp.zeros((14, ids_row.shape[1]), F32)
    return jnp.concatenate([1.0 - ids_row, ids_row, zeros], axis=0).astype(BF16)


def series_kernel(heads, model_d, bit, span, pos, recv, w_t, send, own, give, sel):
    tiles, _, width = send.shape
    slab = width - EXT
    mixes, grad_keys, grad_reads, _, terms, ids_row, _ = series_terms(heads, model_d, recv, w_t)
    high = terms.astype(BF16).astype(F32)
    tail = high + pltpu.roll(terms - high, 3 * heads, 1)
    ext_f = jnp.concatenate([grad_keys, grad_reads, tail], axis=1)
    ext = ext_f.astype(BF16)
    back = jnp.concatenate(value_columns(mixes) + [ext_f], axis=1)
    kept, given = halves([back], span, bit_of(pos, bit) == 0)
    own[...] = kept.astype(BF16)
    give[...] = given.astype(BF16)
    for t in range(tiles):
        send[t, :, :EXT] = ext
        send[t, :, EXT:] = recv[:, t * slab : (t + 1) * slab]
    sel[...] = sensor_rows(ids_row)


def group_series_kernel(heads, model_d, span, pos, recv, w_t, send, own, give_low, give_high, sel, grads, sems):
    peers, length = send.shape[0], recv.shape[0]
    copies = []
    for t in range(peers):
        copies.append(
            pltpu.make_async_copy(
                recv.at[:, t * LANES : (t + 1) * LANES], send.at[t, :length], sems.at[0, t]
            )
        )
        copies[-1].start()
    mixes, grad_keys, grad_reads, raw, terms, ids_row, eye_h = series_terms(heads, model_d, recv, w_t)
    raw_b = raw.astype(BF16)
    raw_t = nt(eye_h.astype(BF16), raw_b)
    total = jnp.sum(terms, axis=0, keepdims=True)
    high = total.astype(BF16).astype(F32)
    misc = jnp.concatenate(
        [lane_pad(raw_t, LANES), high, total - high, jnp.zeros((6, LANES), F32)], axis=0
    )
    grads[...] = jnp.concatenate([grad_keys, grad_reads, misc], axis=0).astype(BF16)
    for t in range(peers):
        copies.append(pltpu.make_async_copy(grads, send.at[t, length:], sems.at[1, t]))
        copies[-1].start()
    back = jnp.concatenate(value_columns(mixes) + [grad_keys, grad_reads, lane_pad(raw, LANES)], axis=1)
    kept, given = halves([back], span, bit_of(pos, 1) == 0)
    here, high_only = halves([kept], span, bit_of(pos, 2) == 0)
    low_only, both = halves([given], span, bit_of(pos, 2) == 0)
    own[...] = here.astype(BF16)
    give_high[...] = high_only.astype(BF16)
    give_low[...] = jnp.concatenate([low_only, both], axis=0).astype(BF16)
    sel[...] = jnp.concatenate([sensor_rows(ids_row)] * peers, axis=1)
    for copy in copies:
        copy.wait()


def pack_kernel(core, ids_in, mask_in, table_in, bias_in, decay_in, skip_in, layer, values, cotangent, out, ids, mask_t, table, params, layer_v, sems):
    pixels, dates, model_d = layer.shape
    small = [
        pltpu.make_async_copy(ids_in, ids, sems.at[0]),
        pltpu.make_async_copy(mask_in, mask_t, sems.at[1]),
        pltpu.make_async_copy(table_in, table, sems.at[2]),
        pltpu.make_async_copy(layer, layer_v, sems.at[3]),
        pltpu.make_async_copy(bias_in, params.at[0:1], sems.at[6]),
        pltpu.make_async_copy(decay_in, params.at[1:2], sems.at[7]),
        pltpu.make_async_copy(skip_in, params.at[2:3], sems.at[8]),
    ]
    large = [
        pltpu.make_async_copy(values, out.at[:, :, model_d : 2 * model_d], sems.at[4]),
        pltpu.make_async_copy(cotangent, out.at[:, :, 2 * model_d : 3 * model_d], sems.at[5]),
    ]
    for copy in small[3:4] + large + small[:3] + small[4:]:
        copy.start()
    for copy in small:
        copy.wait()
    rows = [jnp.where(ids[i] == 1, table[1:2, :], table[0:1, :]) for i in range(dates)]
    embed = jnp.concatenate(rows, axis=0)
    row = lax.broadcasted_iota(jnp.int32, (dates, LANES), 0)
    lane = lax.broadcasted_iota(jnp.int32, (dates, LANES), 1)
    second = jnp.zeros((dates, LANES), F32)
    for i in range(dates):
        second = jnp.where((row == i) & (lane == 1), (ids[i] == 1).astype(F32), second)
    gate = mask_t[...].astype(F32)
    at = 2
    for k in range(3):
        rest = params[k : k + 1, :]
        for _ in range(3):
            term = rest.astype(BF16).astype(F32)
            rest = rest - term
            term = jnp.concatenate([jnp.zeros((1, at), F32), term, jnp.zeros((1, LANES - at - term.shape[1]), F32)], axis=1)
            second = second + term
            at = at + params.shape[1]
    for p in range(pixels):
        out[p, :, 3 * model_d :] = jnp.where(lane == 0, gate[:, p : p + 1], second).astype(BF16)
        out[p, :, :model_d] = (layer_v[p].astype(F32) + embed).astype(BF16)
    for copy in large:
        copy.wait()


def lane_pad(x, width):
    if x.shape[1] == width:
        return x
    return jnp.concatenate([x, jnp.zeros((x.shape[0], width - x.shape[1]), x.dtype)], axis=1)


def sum_rows(sums):
    high = sums.astype(BF16).astype(F32)
    low = (sums - high).astype(BF16).astype(F32)
    rows = jnp.concatenate([high, low, jnp.zeros((4, EXT), F32)], axis=0)
    return [rows[:, b * LANES : (b + 1) * LANES] for b in range(EXT // LANES)]


def rows_sum(block):
    rows = jnp.concatenate([block[8 * b : 8 * b + 8, :] for b in range(EXT // LANES)], axis=1)
    return rows[0:2] + rows[2:4]


def slab_kernel(cols, pos, recv, sel, rows, keep, keep_sums, give):
    tiles, length, width = recv.shape
    slab = width - EXT
    half = slab // 2
    ext = recv[:, :, :EXT].reshape(tiles * length, EXT)
    tokens = recv[:, :, EXT:].reshape(tiles * length, slab)
    part = tn(ext, tokens)[:cols]
    sums = jnp.zeros((16, EXT), F32)
    for t in range(tiles):
        sums = sums + nn(sel[...], recv[t, :, :EXT])
    sums = sums[0:2]
    mine = bit_of(pos, 0) == 0
    first = lane_pad(part[:, :half], LANES)
    second = lane_pad(part[:, half:], LANES)
    keep[...] = jnp.where(mine, first, second)
    keep_sums[...] = sums
    other = jnp.where(mine, second, first)
    blocks = [rows[:, b * LANES : (b + 1) * LANES].astype(F32) for b in range(rows.shape[1] // LANES)]
    give[...] = jnp.concatenate([other] + sum_rows(sums) + blocks, axis=0).astype(BF16)


def join_kernel(cols, dates, pos, keep, keep_sums, got, own, send):
    levels = send.shape[0]
    first = bit_of(pos, 0) == 0
    model_d = own.shape[1] - EXT
    total = keep[...] + got[:cols, :].astype(F32)
    sums = sum_rows(keep_sums[...] + rows_sum(got[cols : cols + 24, :].astype(F32)))
    pair_sums = jnp.concatenate([sums[0][:4], sums[1][:4]], axis=0)
    mine, count = own[...].astype(F32), own.shape[0]
    tall = got[cols + 24 :, :].astype(F32)
    theirs = jnp.concatenate([tall[k : k + count] for k in range(0, tall.shape[0], count)], axis=1)
    firsts, seconds = jnp.where(first, mine, theirs), jnp.where(first, theirs, mine)
    lane = lax.broadcasted_iota(jnp.int32, (8, LANES), 1)
    last = pltpu.roll(sums[2], 64, 1)
    for z in range(levels):
        at = z * dates
        rows = jnp.concatenate([firsts[at : at + dates], seconds[at : at + dates]], axis=0)
        ext = [rows[:, model_d + b * LANES : model_d + (b + 1) * LANES] for b in range(EXT // LANES)]
        misc = jnp.where(lane < 64, ext[2], last)
        value = [rows[:, b * LANES : (b + 1) * LANES] for b in range(model_d // LANES)]
        send[z] = jnp.concatenate([total, ext[0], ext[1], misc, pair_sums] + value, axis=0).astype(BF16)


def total_kernel(cols, recv, send, rest):
    levels = recv.shape[0]
    total = recv[0].astype(F32)
    for z in range(1, levels):
        total = total + recv[z].astype(F32)
    slab = total[:cols].astype(BF16)
    for t in range(send.shape[0]):
        send[t] = slab
    rest[...] = total[cols + 16 : cols + 32]


def store_half(cols, scale, core, half, slabs, weight, held, sems):
    copies = []
    for t in range(slabs.shape[0]):
        held[t] = slabs[t].astype(F32)[:cols] * scale
        at = pl.multiple_of((2 * t + core) * half, half)
        copies.append(pltpu.make_async_copy(held.at[t], weight.at[:, pl.ds(at, half)], sems.at[t]))
        copies[-1].start()
    return copies


def half_kernel(cols, scale, half, pos, slabs, weight_in, weight, held, sems):
    for copy in store_half(cols, scale, 1 - bit_of(pos, 0), half, slabs, weight, held, sems):
        copy.wait()


def local_weight_kernel(heads, scale, cols, half, pos, slabs, recv, rest, w_t, *refs):
    outs, held_outs = refs[:5], refs[5:10]
    held, sems, out_sems = held_outs[4], refs[10], refs[11]
    copies = store_half(cols, scale, bit_of(pos, 0), half, slabs, outs[4], held, sems)
    moves = [pltpu.make_async_copy(held_outs[k], outs[k], out_sems.at[k]) for k in range(4)]
    local_kernel(heads, scale, recv, rest, w_t, *held_outs[:4], moves)
    for copy in copies + moves:
        copy.wait()


def write_sums(heads, scale, sums, w, table, head):
    cols = w.shape[0]
    high, low = split(sums[:, :cols])
    table[...] = (nn(high, w) + nn(low, w)) * scale
    both = sums[0:1] + sums[1:2]
    at = cols - heads
    rows = []
    for k in (1, 0, 2):
        lo = at + k * heads
        rows.append(both[:, lo : lo + heads] + both[:, lo + 3 * heads : lo + 4 * heads])
    head[...] = jnp.concatenate(rows, axis=0) * scale


def local_kernel(heads, scale, recv, rest, w_t, value, inputs, table, head, moves=()):
    levels = recv.shape[0]
    model_d = w_t.shape[1]
    cols = w_t.shape[0]
    dates = value.shape[1]
    w = w_t[...]
    ext_rows = []
    for z in range(levels):
        rows = recv[z].astype(F32)
        ext_rows.append(jnp.concatenate([rows[cols + 8 * b : cols + 8 * b + 8] for b in range(3)], axis=1))
        at = cols + 32
        values = jnp.concatenate([rows[at + 8 * b : at + 8 * b + 8] for b in range(model_d // LANES)], axis=1)
        for c in range(2):
            value[2 * z + c] = values[c * dates : (c + 1) * dates].astype(BF16)
    for move in moves[:1]:
        move.start()
    grads = nn(jnp.concatenate(ext_rows, axis=0).astype(BF16)[:, :cols], w)
    for p in range(2 * levels):
        inputs[p] = grads[p * dates : (p + 1) * dates].astype(BF16)
    for move in moves[1:2]:
        move.start()
    last = pltpu.roll(rest[0:8, :], 64, 1)
    sums = jnp.concatenate([rest[8:12, :], rest[12:16, :], last[0:4]], axis=1)
    sums = sums[0:2] + sums[2:4]
    write_sums(heads, scale, sums, w, table, head)
    for move in moves[2:]:
        move.start()


def gather_kernel(cols, half, scale, pos, own, other, out):
    tiles = own.shape[0]
    mine = bit_of(pos, 0) == 0
    for t in range(tiles):
        a = own[t].astype(F32)
        b = other[t].astype(F32)
        first = jnp.where(mine, a, b)[:cols, :half]
        second = jnp.where(mine, b, a)[:cols, :half]
        out[:, 2 * half * t : 2 * half * (t + 1)] = jnp.concatenate([first, second], axis=1) * scale


VMEM = pl.BlockSpec(memory_space=pltpu.VMEM)
SMEM = pl.BlockSpec(memory_space=pltpu.SMEM)
HBM = pl.BlockSpec(memory_space=pltpu.HBM)


def call(kernel, outs, ins, smem=0):
    return pl.pallas_call(
        kernel,
        out_shape=[jax.ShapeDtypeStruct(s, d) for s, d in outs],
        in_specs=[SMEM] * smem + [VMEM] * (len(ins) - smem),
        out_specs=[VMEM] * len(outs),
        compiler_params=pltpu.CompilerParams(vmem_limit_bytes=48 * 1024 * 1024),
    )(*ins)


def rows_block(rows):
    return [rows[:, b * LANES : (b + 1) * LANES] for b in range(rows.shape[1] // LANES)]


def block_rows(block, count):
    return jnp.concatenate([block[k : k + count] for k in range(0, block.shape[0], count)], axis=1)


def pack_sums(sums):
    high = sums.astype(BF16).astype(F32)
    return jnp.concatenate([high, sums - high], axis=0)


def unpack_sums(rows):
    return rows[:8] + rows[8:16]


def group_slab_kernel(dates, pos, recv, sel, rows_own, rows_high, rows_low, keep, keep_sums, rows_keep, give):
    peers = recv.shape[0]
    length = sel.shape[1] // peers
    count = keep.shape[0]
    first = bit_of(pos, 0) == 0
    tokens = recv[:, :length, :].reshape(peers * length, LANES)
    keys = recv[:, length : 2 * length, :].reshape(peers * length, LANES)
    reads = recv[:, 2 * length : 3 * length, :].reshape(peers * length, LANES)
    misc = [recv[t, 3 * length :, :] for t in range(peers)]
    raw_t = jnp.concatenate([m[:, :length] for m in misc], axis=1)
    part = jnp.concatenate([tn(keys, tokens), tn(reads, tokens), nn(raw_t, tokens)[: count - LANES]], axis=0)
    chosen = sel[...]
    head = sum(m.astype(F32) for m in misc)[8:10]
    sums = jnp.concatenate(
        [
            nn(chosen, keys)[0:2],
            nn(chosen, reads)[0:2],
            lane_pad(nt(chosen, raw_t)[0:2], LANES),
            head[0:1] + head[1:2],
            jnp.zeros((1, LANES), F32),
        ],
        axis=0,
    )
    upper, lower = part[:count], part[part.shape[0] - count :]
    keep[...] = jnp.where(first, upper, lower)
    keep_sums[...] = sums
    arrived = [rows[...].astype(F32) for rows in (rows_own, rows_high, rows_low)]
    kept, given = halves(arrived, dates, first)
    rows_keep[...] = kept.astype(BF16)
    give[...] = jnp.concatenate(
        [jnp.where(first, lower, upper), pack_sums(sums)] + rows_block(given), axis=0
    ).astype(BF16)


def group_join_kernel(dates, keep, keep_sums, rows_own, got, rows_keep, give):
    count = keep.shape[0]
    there = got[...].astype(F32)
    total = keep[...] + there[:count]
    sums = keep_sums[...] + unpack_sums(there[count : count + 16])
    mine = rows_own[...].astype(F32)
    theirs = block_rows(there[count + 16 :], mine.shape[0])
    stay = mine.shape[0] - dates
    rows_keep[...] = jnp.concatenate([mine[:stay], theirs[:stay]], axis=0).astype(BF16)
    given = jnp.concatenate([mine[stay:], theirs[stay:]], axis=0)
    give[...] = jnp.concatenate([total, pack_sums(sums)] + rows_block(given), axis=0).astype(BF16)


def group_total_kernel(own, got, send, rest):
    count = send.shape[1]
    total = (own[...].astype(F32) + got[...].astype(F32))[: count + 16]
    slab = total[:count].astype(BF16)
    for t in range(send.shape[0]):
        send[t] = slab
    rest[...] = unpack_sums(total[count:])


def store_rows(cols, scale, core, slabs, weight, held, sems):
    count = slabs.shape[1]
    base = cols - count
    for t in range(slabs.shape[0]):
        held[:, t * LANES : (t + 1) * LANES] = slabs[t].astype(F32) * scale
    at = pl.multiple_of(core * base, 8)
    main = pltpu.make_async_copy(held.at[:base], weight.at[pl.ds(at, base)], sems.at[0])
    last = pltpu.make_async_copy(held.at[base:], weight.at[2 * base :], sems.at[1])
    main.start()

    @pl.when(core == 1)
    def _():
        last.start()

    def wait():
        main.wait()

        @pl.when(core == 1)
        def _():
            last.wait()

    return wait


def other_rows_kernel(cols, scale, pos, slabs, weight_in, weight, held, sems):
    store_rows(cols, scale, 1 - bit_of(pos, 0), slabs, weight, held, sems)()


def final_kernel(heads, scale, pos, slabs, rows_own, got, rest, w_t, *refs):
    outs, (value, inputs, table, head), (held, sems, out_sems) = refs[:5], refs[5:9], refs[9:]
    model_d, cols, dates = w_t.shape[1], w_t.shape[0], value.shape[1]
    wait = store_rows(cols, scale, bit_of(pos, 0), slabs, outs[4], held, sems)
    moves = [
        pltpu.make_async_copy(source, outs[k], out_sems.at[k])
        for k, source in enumerate((value, inputs, table, head))
    ]
    w = w_t[...]
    rows_got = block_rows(got[...].astype(F32)[slabs.shape[1] + 16 :], 2 * dates)
    rows = jnp.concatenate([rows_own[...].astype(F32), rows_got], axis=0)
    masks = [0, 4, 2, 1, 5, 3, 6, 7]
    where_to = []
    for mask in masks:
        index = 0
        for bit in range(3):
            here = bit_of(pos, bit)
            index = index + 2**bit * (1 - here if mask >> bit & 1 else here)
        where_to.append(index)
    for k, pixel in enumerate(where_to):
        value[pixel] = rows[k * dates : (k + 1) * dates, :model_d].astype(BF16)
    moves[0].start()
    grads = nn(rows[:, model_d : model_d + EXT].astype(BF16)[:, :cols], w)
    for k, pixel in enumerate(where_to):
        inputs[pixel] = grads[k * dates : (k + 1) * dates].astype(BF16)
    moves[1].start()
    sums = jnp.concatenate([rest[0:2, :], rest[2:4, :], rest[4:6, :]], axis=1)[:, :cols]
    high, low = split(sums)
    table[...] = (nn(high, w) + nn(low, w)) * scale
    total = rest[6:7, :]
    head[...] = jnp.concatenate([total[:, k * heads : (k + 1) * heads] for k in (1, 0, 2)], axis=0) * scale
    for move in moves[2:]:
        move.start()
    wait()
    for move in moves:
        move.wait()


def finish_four_levels(series, w_t, date_s, heads, scale, pixel_dev, dates_dev, tiles, dates):
    length = series.shape[0]
    cols, model_d = w_t.shape
    peers = 2 * tiles
    wide = model_d + EXT
    count = (cols + 8) // 2
    half_rows = length // 2
    payload = count + 16 + half_rows * wide // LANES
    payload_high = count + 16 + half_rows // 2 * wide // LANES

    def groups(alternate):
        return [
            [t * dates + 4 * high + 2 * low + (c + alternate * t) % 2 for t in range(tiles) for low in range(2)]
            for high in range(2)
            for c in range(2)
        ]

    def across(bit):
        return [(i, i ^ 2**bit) for i in range(dates)]

    send_t, rows_own, give_low, give_high, sel = pl.pallas_call(
        functools.partial(group_series_kernel, heads, model_d, 2 * dates_dev),
        out_shape=[
            jax.ShapeDtypeStruct((peers, 3 * length + 16, LANES), BF16),
            jax.ShapeDtypeStruct((half_rows // 2, wide), BF16),
            jax.ShapeDtypeStruct((half_rows, wide), BF16),
            jax.ShapeDtypeStruct((half_rows // 2, wide), BF16),
            jax.ShapeDtypeStruct((16, peers * length), BF16),
        ],
        in_specs=[SMEM, VMEM, VMEM],
        out_specs=[HBM, VMEM, VMEM, VMEM, VMEM],
        scratch_shapes=[
            pltpu.VMEM((2 * length + 16, LANES), BF16),
            pltpu.SemaphoreType.DMA((2, peers)),
        ],
        compiler_params=pltpu.CompilerParams(vmem_limit_bytes=48 * 1024 * 1024),
    )(date_s, series, w_t)
    recv_t = lax.all_to_all(
        send_t, ("tile", "date"), split_axis=0, concat_axis=0, tiled=True, axis_index_groups=groups(1)
    )
    rows_low = lax.ppermute(give_low, "date", across(1))
    rows_high = lax.ppermute(give_high, "date", across(2))
    keep, keep_sums, rows_own, give = call(
        functools.partial(group_slab_kernel, dates_dev),
        [((count, LANES), F32), ((8, LANES), F32), ((half_rows, wide), BF16), ((payload, LANES), BF16)],
        [date_s, recv_t, sel, rows_own, rows_high, rows_low],
        1,
    )
    got = lax.ppermute(give, "date", across(0))
    rows_own, give = call(
        functools.partial(group_join_kernel, dates_dev),
        [((half_rows * 3 // 2, wide), BF16), ((payload_high, LANES), BF16)],
        [keep, keep_sums, rows_own, got],
    )
    got = lax.ppermute(give, "date", across(2))
    send_g, rest = call(
        group_total_kernel, [((peers, count, LANES), BF16), ((8, LANES), F32)], [give, got]
    )
    recv_g = lax.all_to_all(
        send_g, ("tile", "date"), split_axis=0, concat_axis=0, tiled=True, axis_index_groups=groups(0)
    )
    other_g = lax.ppermute(recv_g, "date", across(0))
    outs = [
        jax.ShapeDtypeStruct((pixel_dev, dates_dev, model_d), BF16),
        jax.ShapeDtypeStruct((pixel_dev, dates_dev, model_d), BF16),
        jax.ShapeDtypeStruct((2, model_d), F32),
        jax.ShapeDtypeStruct((3, heads), F32),
        jax.ShapeDtypeStruct((cols, model_d), F32),
    ]
    held = [pltpu.VMEM((count, model_d), F32), pltpu.SemaphoreType.DMA((2,))]
    limit = pltpu.CompilerParams(vmem_limit_bytes=48 * 1024 * 1024)
    value, inputs, table, head, weight_t = pl.pallas_call(
        functools.partial(final_kernel, heads, scale),
        out_shape=outs,
        in_specs=[SMEM] + [VMEM] * 5,
        out_specs=[HBM] * 5,
        scratch_shapes=[pltpu.VMEM(o.shape, o.dtype) for o in outs[:4]]
        + held
        + [pltpu.SemaphoreType.DMA((4,))],
        compiler_params=limit,
    )(date_s, recv_g, rows_own, got, rest, w_t)
    weight_t = pl.pallas_call(
        functools.partial(other_rows_kernel, cols, scale),
        out_shape=outs[4],
        in_specs=[SMEM, VMEM, HBM],
        out_specs=HBM,
        scratch_shapes=held,
        input_output_aliases={2: 0},
        compiler_params=limit,
    )(date_s, other_g, weight_t)
    return value, inputs, weight_t.T, table, head


def finish_any(series, w_t, date_s, heads, scale, pixel_dev, dates_dev, tiles, dates):
    length = series.shape[0]
    cols, model_d = w_t.shape
    levels = dates // 2
    slab = model_d // tiles
    half = slab // 2
    swap = [(i, i ^ 1) for i in range(dates)]
    planes = [[2 * z + c for z in range(levels)] for c in range(2)]
    rows_core = length // 2
    send_t, own, give_rows, sel = call(
        functools.partial(series_kernel, heads, model_d, 0, dates_dev),
        [
            ((tiles, length, EXT + slab), BF16),
            ((rows_core, model_d + EXT), BF16),
            ((rows_core, model_d + EXT), BF16),
            ((16, length), BF16),
        ],
        [date_s, series, w_t],
        1,
    )
    mixed = [
        [t * dates + 2 * z + (c + t) % 2 for t in range(tiles)] for z in range(levels) for c in range(2)
    ]
    recv_t = lax.all_to_all(
        send_t, ("tile", "date"), split_axis=0, concat_axis=0, tiled=True, axis_index_groups=mixed
    )
    rows_give = cols + 24 + rows_core * (model_d + EXT) // LANES
    keep, keep_sums, give = call(
        functools.partial(slab_kernel, cols),
        [((cols, LANES), F32), ((2, EXT), F32), ((rows_give, LANES), BF16)],
        [date_s, recv_t, sel, give_rows],
        1,
    )
    got = lax.ppermute(give, "date", swap)
    rows_z = cols + 32 + model_d // 16
    (send_z,) = call(
        functools.partial(join_kernel, cols, dates_dev),
        [((levels, rows_z, LANES), BF16)],
        [date_s, keep, keep_sums, got, own],
        1,
    )
    recv_z = lax.all_to_all(
        send_z, "date", split_axis=0, concat_axis=0, tiled=True, axis_index_groups=planes
    )
    send_g, rest = call(
        functools.partial(total_kernel, cols),
        [((tiles, cols, LANES), BF16), ((16, LANES), F32)],
        [recv_z],
    )
    recv_g = lax.all_to_all(send_g, "tile", split_axis=0, concat_axis=0, tiled=True)
    local_outs = [
        ((pixel_dev, dates_dev, model_d), BF16),
        ((pixel_dev, dates_dev, model_d), BF16),
        ((2, model_d), F32),
        ((3, heads), F32),
    ]
    other_g = lax.ppermute(recv_g, "date", swap)
    if half % LANES == 0:
        weight_shape = jax.ShapeDtypeStruct((cols, model_d), F32)
        held = [pltpu.VMEM((tiles, cols, half), F32), pltpu.SemaphoreType.DMA((tiles,))]
        limit = pltpu.CompilerParams(vmem_limit_bytes=48 * 1024 * 1024)
        value, inputs, table, head, weight_t = pl.pallas_call(
            functools.partial(local_weight_kernel, heads, scale, cols, half),
            out_shape=[jax.ShapeDtypeStruct(s, d) for s, d in local_outs] + [weight_shape],
            in_specs=[SMEM] + [VMEM] * 4,
            out_specs=[HBM] * 5,
            scratch_shapes=[pltpu.VMEM(s, d) for s, d in local_outs]
            + held
            + [pltpu.SemaphoreType.DMA((4,))],
            compiler_params=limit,
        )(date_s, recv_g, recv_z, rest, w_t)
        weight_t = pl.pallas_call(
            functools.partial(half_kernel, cols, scale, half),
            out_shape=weight_shape,
            in_specs=[SMEM, VMEM, HBM],
            out_specs=HBM,
            scratch_shapes=held,
            input_output_aliases={2: 0},
            compiler_params=limit,
        )(date_s, other_g, weight_t)
    else:
        value, inputs, table, head = call(
            functools.partial(local_kernel, heads, scale), local_outs, [recv_z, rest, w_t]
        )
        (weight_t,) = call(
            functools.partial(gather_kernel, cols, half, scale),
            [((cols, model_d), F32)],
            [date_s, recv_g, other_g],
            1,
        )
    return (
        value,
        inputs,
        weight_t.T,
        table,
        head,
    )


def on_device(
    layer_input,
    head_input,
    out_grad,
    sensor_ids,
    valid_mask,
    sensor_table,
    proj_weight,
    step_bias,
    decay_log,
    skip_gain,
):
    pixel_dev, dates_dev, model_d = layer_input.shape
    heads = step_bias.shape[0]
    tiles = lax.axis_size("tile")
    dates = lax.axis_size("date")
    assert pixel_dev == dates and dates % 2 == 0
    levels = dates // 2
    length = dates * dates_dev
    slab = model_d // tiles
    half = slab // 2
    date_s = lax.axis_index("date").astype(jnp.int32).reshape(1)
    w_t = proj_weight.T
    scale = 1.0 / math.sqrt(pixel_dev * dates_dev * tiles * dates)

    operands = [
        sensor_ids,
        valid_mask.T,
        sensor_table,
        step_bias[None],
        decay_log[None],
        skip_gain[None],
        layer_input,
        head_input,
        out_grad,
    ]
    packed = pl.pallas_call(
        pack_kernel,
        out_shape=jax.ShapeDtypeStruct((pixel_dev, dates_dev, 3 * model_d + LANES), BF16),
        in_specs=[SMEM] + [HBM] * 9,
        out_specs=VMEM,
        scratch_shapes=[
            pltpu.SMEM((dates_dev,), jnp.int32),
            pltpu.VMEM((dates_dev, pixel_dev), jnp.int32),
            pltpu.VMEM((2, model_d), F32),
            pltpu.VMEM((3, heads), F32),
            pltpu.VMEM((pixel_dev, dates_dev, model_d), BF16),
            pltpu.SemaphoreType.DMA((9,)),
        ],
        compiler_params=pltpu.CompilerParams(vmem_limit_bytes=16 * 1024 * 1024),
    )(date_s, *[pltpu.with_memory_space_constraint(operand, pltpu.HBM) for operand in operands])
    series = lax.all_to_all(packed, "date", split_axis=0, concat_axis=0, tiled=True).reshape(
        length, 3 * model_d + LANES
    )

    if levels == 4 and model_d == 2 * LANES * tiles:
        finish = finish_four_levels
    else:
        finish = finish_any
    return finish(series, w_t, date_s, heads, scale, pixel_dev, dates_dev, tiles, dates)


def solution(mesh):
    in_specs = (
        P("tile", "date", None),
        P("tile", "date", None),
        P("tile", "date", None),
        P("date"),
        P("tile", "date"),
        P(),
        P(),
        P(),
        P(),
        P(),
    )
    out_specs = (P("tile", "date", None), P("tile", "date", None), P(), P(), P())
    return jax.shard_map(
        on_device, mesh=mesh, in_specs=in_specs, out_specs=out_specs, check_vma=False
    )
```

```python
import functools
import math

import jax
import jax.numpy as jnp
from jax import lax
from jax.experimental import pallas as pl
from jax.experimental.pallas import tpu as pltpu
from jax.sharding import PartitionSpec as P

NEG_FILL = -1e30
HIGHEST_PREC = lax.Precision.HIGHEST
F32 = jnp.float32
BF16 = jnp.bfloat16
LANES = 128
EXT = 384


def nt(a, b, precision=None):
    return lax.dot_general(
        a, b, (((1,), (1,)), ((), ())), preferred_element_type=F32, precision=precision
    )


def nn(a, b, precision=None):
    return lax.dot_general(
        a, b, (((1,), (0,)), ((), ())), preferred_element_type=F32, precision=precision
    )


def tn(a, b):
    return lax.dot_general(a, b, (((0,), (0,)), ((), ())), preferred_element_type=F32)


def split(x):
    high = x.astype(BF16)
    return high, (x - high.astype(F32)).astype(BF16)


def bit_of(pos, bit):
    return lax.rem(lax.div(pos[0], 2**bit), 2)


def halves(arrays, span, first):
    kept, given = [], []
    for array in arrays:
        for at in range(0, array.shape[0], 2 * span):
            a, b = array[at : at + span], array[at + span : at + 2 * span]
            kept.append(jnp.where(first, a, b))
            given.append(jnp.where(first, b, a))
    return jnp.concatenate(kept, axis=0), jnp.concatenate(given, axis=0)


def series_terms(heads, model_d, recv, w_t):
    length = recv.shape[0]
    width_p = model_d // heads
    states = (w_t.shape[0] - heads) // 2
    mixed = recv[:, :model_d]
    aux = recv[:, 3 * model_d :].astype(F32)
    gate = aux[:, 0:1]
    ids = aux[:, 1:2]
    params = []
    for at in range(2, 2 + 9 * heads, 3 * heads):
        params.append(sum(aux[0:1, at + k * heads : at + (k + 1) * heads] for k in range(3)))
    bias, rate, skip = params[0], -jnp.exp(params[1]), params[2]
    projected = nt(mixed, w_t[...])
    keys = projected[:, :states].astype(BF16)
    reads = projected[:, states : 2 * states].astype(BF16)
    step_pre = projected[:, 2 * states :] + bias
    softplus = jnp.maximum(step_pre, 0.0) + jnp.log1p(jnp.exp(-jnp.abs(step_pre)))
    steps_b = (gate * softplus).astype(BF16)
    steps = steps_b.astype(F32)

    row = lax.broadcasted_iota(jnp.int32, (length, length), 0)
    col = lax.broadcasted_iota(jnp.int32, (length, length), 1)
    upper = col >= row
    upper_f = upper.astype(F32)
    eye = (col == row).astype(F32)
    lower_b = (row >= col).astype(BF16)
    head_row = lax.broadcasted_iota(jnp.int32, (heads, heads), 0)
    head_col = lax.broadcasted_iota(jnp.int32, (heads, heads), 1)
    eye_h = (head_row == head_col).astype(F32)
    rate_col = jnp.sum(eye_h * rate, axis=1, keepdims=True)
    log_col = nn(lower_b, steps_b) * rate
    steps_t = nt(eye_h.astype(BF16), steps_b).astype(BF16)
    log_row = nn(steps_t, upper.astype(BF16)) * rate_col
    scores_t = nt(keys, reads)

    pair_t = jnp.zeros((length, length), F32)
    mixes, weighted_cols, read_rows, skip_cols = [], [], [], []
    for h in range(heads):
        lo = model_d + h * width_p
        x_h = recv[:, lo : lo + width_p]
        g_h = recv[:, lo + model_d : lo + model_d + width_p]
        dt_h = steps[:, h : h + 1]
        gap = log_row[h : h + 1, :] - log_col[:, h : h + 1]
        decay = jnp.exp(jnp.where(upper, gap, NEG_FILL))
        cross = nt(x_h, g_h)
        mix = decay * scores_t
        pair_t = pair_t + decay * cross * dt_h
        both = mix * cross
        weighted = jnp.sum(both, axis=1, keepdims=True)
        weighted_cols.append(weighted)
        read_rows.append(jnp.sum(both * dt_h, axis=0, keepdims=True))
        skip_cols.append(jnp.sum(cross * eye, axis=1, keepdims=True))
        mixes.append((mix.astype(BF16), g_h, dt_h, skip[:, h : h + 1]))

    weighted = jnp.concatenate(weighted_cols, axis=1)
    read_sum = jnp.concatenate(read_rows, axis=0)
    skip_terms = jnp.concatenate(skip_cols, axis=1)
    later = nt(upper_f, read_sum, HIGHEST_PREC) - nn(upper_f, steps * weighted, HIGHEST_PREC)
    step_grad = (weighted + rate * later).astype(BF16).astype(F32)
    decay_terms = steps * later * rate
    pair_b = pair_t.astype(BF16)
    grad_keys = nn(pair_b, reads)
    grad_reads = tn(pair_b, keys)
    raw = step_grad * gate * jax.nn.sigmoid(step_pre)
    terms = jnp.concatenate(
        [raw, decay_terms, skip_terms, jnp.zeros((length, LANES - 3 * heads), F32)], axis=1
    )
    ids_row = jnp.sum(eye * ids, axis=0, keepdims=True)
    return mixes, grad_keys, grad_reads, raw, terms, ids_row, eye_h


def value_columns(mixes):
    return [nn(mix, g_h) * dt_h + skip_h * g_h.astype(F32) for mix, g_h, dt_h, skip_h in mixes]


def sensor_rows(ids_row):
    zeros = jnp.zeros((14, ids_row.shape[1]), F32)
    return jnp.concatenate([1.0 - ids_row, ids_row, zeros], axis=0).astype(BF16)


def series_kernel(heads, model_d, bit, span, pos, recv, w_t, send, own, give, sel):
    tiles, _, width = send.shape
    slab = width - EXT
    mixes, grad_keys, grad_reads, _, terms, ids_row, _ = series_terms(heads, model_d, recv, w_t)
    high = terms.astype(BF16).astype(F32)
    tail = high + pltpu.roll(terms - high, 3 * heads, 1)
    ext_f = jnp.concatenate([grad_keys, grad_reads, tail], axis=1)
    ext = ext_f.astype(BF16)
    back = jnp.concatenate(value_columns(mixes) + [ext_f], axis=1)
    kept, given = halves([back], span, bit_of(pos, bit) == 0)
    own[...] = kept.astype(BF16)
    give[...] = given.astype(BF16)
    for t in range(tiles):
        send[t, :, :EXT] = ext
        send[t, :, EXT:] = recv[:, t * slab : (t + 1) * slab]
    sel[...] = sensor_rows(ids_row)


def group_series_kernel(heads, model_d, dates, pos, recv, w_t, send, own, give, sel):
    peers, length = send.shape[0], recv.shape[0]
    mixes, grad_keys, grad_reads, raw, terms, ids_row, eye_h = series_terms(heads, model_d, recv, w_t)
    raw_t = nt(eye_h.astype(BF16), raw.astype(BF16))
    total = jnp.sum(terms, axis=0, keepdims=True)
    high = total.astype(BF16).astype(F32)
    misc = jnp.concatenate(
        [lane_pad(raw_t, LANES), high, total - high, jnp.zeros((6, LANES), F32)], axis=0
    )
    grads = jnp.concatenate([grad_keys, grad_reads, misc], axis=0).astype(BF16)
    for t in range(peers):
        send[t, :length] = recv[:, t * LANES : (t + 1) * LANES]
        send[t, length:] = grads
    back = jnp.concatenate(value_columns(mixes) + [grad_keys, grad_reads, lane_pad(raw, LANES)], axis=1)
    kept, given = halves([back], dates, bit_of(pos, 0) == 0)
    own[...] = kept.astype(BF16)
    give[...] = given.astype(BF16)
    sel[...] = jnp.concatenate([sensor_rows(ids_row)] * peers, axis=1)


def pack_kernel(core, ids_in, mask_in, table_in, bias_in, decay_in, skip_in, layer, values, cotangent, out, ids, mask_t, table, params, layer_v, sems):
    pixels, dates, model_d = layer.shape
    small = [
        pltpu.make_async_copy(ids_in, ids, sems.at[0]),
        pltpu.make_async_copy(mask_in, mask_t, sems.at[1]),
        pltpu.make_async_copy(table_in, table, sems.at[2]),
        pltpu.make_async_copy(layer, layer_v, sems.at[3]),
        pltpu.make_async_copy(bias_in, params.at[0:1], sems.at[6]),
        pltpu.make_async_copy(decay_in, params.at[1:2], sems.at[7]),
        pltpu.make_async_copy(skip_in, params.at[2:3], sems.at[8]),
    ]
    large = [
        pltpu.make_async_copy(values, out.at[:, :, model_d : 2 * model_d], sems.at[4]),
        pltpu.make_async_copy(cotangent, out.at[:, :, 2 * model_d : 3 * model_d], sems.at[5]),
    ]
    for copy in small[3:4] + large + small[:3] + small[4:]:
        copy.start()
    for copy in small:
        copy.wait()
    rows = [jnp.where(ids[i] == 1, table[1:2, :], table[0:1, :]) for i in range(dates)]
    embed = jnp.concatenate(rows, axis=0)
    row = lax.broadcasted_iota(jnp.int32, (dates, LANES), 0)
    lane = lax.broadcasted_iota(jnp.int32, (dates, LANES), 1)
    second = jnp.zeros((dates, LANES), F32)
    for i in range(dates):
        second = jnp.where((row == i) & (lane == 1), (ids[i] == 1).astype(F32), second)
    gate = mask_t[...].astype(F32)
    at = 2
    for k in range(3):
        rest = params[k : k + 1, :]
        for _ in range(3):
            term = rest.astype(BF16).astype(F32)
            rest = rest - term
            term = jnp.concatenate([jnp.zeros((1, at), F32), term, jnp.zeros((1, LANES - at - term.shape[1]), F32)], axis=1)
            second = second + term
            at = at + params.shape[1]
    for p in range(pixels):
        out[p, :, 3 * model_d :] = jnp.where(lane == 0, gate[:, p : p + 1], second).astype(BF16)
        out[p, :, :model_d] = (layer_v[p].astype(F32) + embed).astype(BF16)
    for copy in large:
        copy.wait()


def lane_pad(x, width):
    if x.shape[1] == width:
        return x
    return jnp.concatenate([x, jnp.zeros((x.shape[0], width - x.shape[1]), x.dtype)], axis=1)


def sum_rows(sums):
    high = sums.astype(BF16).astype(F32)
    low = (sums - high).astype(BF16).astype(F32)
    rows = jnp.concatenate([high, low, jnp.zeros((4, EXT), F32)], axis=0)
    return [rows[:, b * LANES : (b + 1) * LANES] for b in range(EXT // LANES)]


def rows_sum(block):
    rows = jnp.concatenate([block[8 * b : 8 * b + 8, :] for b in range(EXT // LANES)], axis=1)
    return rows[0:2] + rows[2:4]


def slab_kernel(cols, pos, recv, sel, rows, keep, keep_sums, give):
    tiles, length, width = recv.shape
    slab = width - EXT
    half = slab // 2
    ext = recv[:, :, :EXT].reshape(tiles * length, EXT)
    tokens = recv[:, :, EXT:].reshape(tiles * length, slab)
    part = tn(ext, tokens)[:cols]
    sums = jnp.zeros((16, EXT), F32)
    for t in range(tiles):
        sums = sums + nn(sel[...], recv[t, :, :EXT])
    sums = sums[0:2]
    mine = bit_of(pos, 0) == 0
    first = lane_pad(part[:, :half], LANES)
    second = lane_pad(part[:, half:], LANES)
    keep[...] = jnp.where(mine, first, second)
    keep_sums[...] = sums
    other = jnp.where(mine, second, first)
    blocks = [rows[:, b * LANES : (b + 1) * LANES].astype(F32) for b in range(rows.shape[1] // LANES)]
    give[...] = jnp.concatenate([other] + sum_rows(sums) + blocks, axis=0).astype(BF16)


def join_kernel(cols, dates, pos, keep, keep_sums, got, own, send):
    levels = send.shape[0]
    first = bit_of(pos, 0) == 0
    model_d = own.shape[1] - EXT
    total = keep[...] + got[:cols, :].astype(F32)
    sums = sum_rows(keep_sums[...] + rows_sum(got[cols : cols + 24, :].astype(F32)))
    pair_sums = jnp.concatenate([sums[0][:4], sums[1][:4]], axis=0)
    mine, count = own[...].astype(F32), own.shape[0]
    tall = got[cols + 24 :, :].astype(F32)
    theirs = jnp.concatenate([tall[k : k + count] for k in range(0, tall.shape[0], count)], axis=1)
    firsts, seconds = jnp.where(first, mine, theirs), jnp.where(first, theirs, mine)
    lane = lax.broadcasted_iota(jnp.int32, (8, LANES), 1)
    last = pltpu.roll(sums[2], 64, 1)
    for z in range(levels):
        at = z * dates
        rows = jnp.concatenate([firsts[at : at + dates], seconds[at : at + dates]], axis=0)
        ext = [rows[:, model_d + b * LANES : model_d + (b + 1) * LANES] for b in range(EXT // LANES)]
        misc = jnp.where(lane < 64, ext[2], last)
        value = [rows[:, b * LANES : (b + 1) * LANES] for b in range(model_d // LANES)]
        send[z] = jnp.concatenate([total, ext[0], ext[1], misc, pair_sums] + value, axis=0).astype(BF16)


def total_kernel(cols, recv, send, rest):
    levels = recv.shape[0]
    total = recv[0].astype(F32)
    for z in range(1, levels):
        total = total + recv[z].astype(F32)
    slab = total[:cols].astype(BF16)
    for t in range(send.shape[0]):
        send[t] = slab
    rest[...] = total[cols + 16 : cols + 32]


def store_half(cols, scale, core, half, slabs, weight, held, sems):
    copies = []
    for t in range(slabs.shape[0]):
        held[t] = slabs[t].astype(F32)[:cols] * scale
        at = pl.multiple_of((2 * t + core) * half, half)
        copies.append(pltpu.make_async_copy(held.at[t], weight.at[:, pl.ds(at, half)], sems.at[t]))
        copies[-1].start()
    return copies


def half_kernel(cols, scale, half, pos, slabs, weight_in, weight, held, sems):
    for copy in store_half(cols, scale, 1 - bit_of(pos, 0), half, slabs, weight, held, sems):
        copy.wait()


def local_weight_kernel(heads, scale, cols, half, pos, slabs, recv, rest, w_t, *refs):
    outs, held_outs = refs[:5], refs[5:10]
    held, sems, out_sems = held_outs[4], refs[10], refs[11]
    copies = store_half(cols, scale, bit_of(pos, 0), half, slabs, outs[4], held, sems)
    moves = [pltpu.make_async_copy(held_outs[k], outs[k], out_sems.at[k]) for k in range(4)]
    local_kernel(heads, scale, recv, rest, w_t, *held_outs[:4], moves)
    for copy in copies + moves:
        copy.wait()


def write_sums(heads, scale, sums, w, table, head):
    cols = w.shape[0]
    high, low = split(sums[:, :cols])
    table[...] = (nn(high, w) + nn(low, w)) * scale
    both = sums[0:1] + sums[1:2]
    at = cols - heads
    rows = []
    for k in (1, 0, 2):
        lo = at + k * heads
        rows.append(both[:, lo : lo + heads] + both[:, lo + 3 * heads : lo + 4 * heads])
    head[...] = jnp.concatenate(rows, axis=0) * scale


def local_kernel(heads, scale, recv, rest, w_t, value, inputs, table, head, moves=()):
    levels = recv.shape[0]
    model_d = w_t.shape[1]
    cols = w_t.shape[0]
    dates = value.shape[1]
    w = w_t[...]
    ext_rows = []
    for z in range(levels):
        rows = recv[z].astype(F32)
        ext_rows.append(jnp.concatenate([rows[cols + 8 * b : cols + 8 * b + 8] for b in range(3)], axis=1))
        at = cols + 32
        values = jnp.concatenate([rows[at + 8 * b : at + 8 * b + 8] for b in range(model_d // LANES)], axis=1)
        for c in range(2):
            value[2 * z + c] = values[c * dates : (c + 1) * dates].astype(BF16)
    for move in moves[:1]:
        move.start()
    grads = nn(jnp.concatenate(ext_rows, axis=0).astype(BF16)[:, :cols], w)
    for p in range(2 * levels):
        inputs[p] = grads[p * dates : (p + 1) * dates].astype(BF16)
    for move in moves[1:2]:
        move.start()
    last = pltpu.roll(rest[0:8, :], 64, 1)
    sums = jnp.concatenate([rest[8:12, :], rest[12:16, :], last[0:4]], axis=1)
    sums = sums[0:2] + sums[2:4]
    write_sums(heads, scale, sums, w, table, head)
    for move in moves[2:]:
        move.start()


def gather_kernel(cols, half, scale, pos, own, other, out):
    tiles = own.shape[0]
    mine = bit_of(pos, 0) == 0
    for t in range(tiles):
        a = own[t].astype(F32)
        b = other[t].astype(F32)
        first = jnp.where(mine, a, b)[:cols, :half]
        second = jnp.where(mine, b, a)[:cols, :half]
        out[:, 2 * half * t : 2 * half * (t + 1)] = jnp.concatenate([first, second], axis=1) * scale


VMEM = pl.BlockSpec(memory_space=pltpu.VMEM)
SMEM = pl.BlockSpec(memory_space=pltpu.SMEM)
HBM = pl.BlockSpec(memory_space=pltpu.HBM)


def call(kernel, outs, ins, smem=0):
    return pl.pallas_call(
        kernel,
        out_shape=[jax.ShapeDtypeStruct(s, d) for s, d in outs],
        in_specs=[SMEM] * smem + [VMEM] * (len(ins) - smem),
        out_specs=[VMEM] * len(outs),
        compiler_params=pltpu.CompilerParams(vmem_limit_bytes=48 * 1024 * 1024),
    )(*ins)


def rows_block(rows):
    return [rows[:, b * LANES : (b + 1) * LANES] for b in range(rows.shape[1] // LANES)]


def block_rows(block, count):
    return jnp.concatenate([block[k : k + count] for k in range(0, block.shape[0], count)], axis=1)


def pack_sums(sums):
    high = sums.astype(BF16).astype(F32)
    return jnp.concatenate([high, sums - high], axis=0)


def unpack_sums(rows):
    return rows[:8] + rows[8:16]


def group_slab_kernel(pos, recv, sel, rows, keep, keep_sums, give):
    peers = recv.shape[0]
    length = sel.shape[1] // peers
    count = keep.shape[0]
    first = bit_of(pos, 0) == 0
    tokens = recv[:, :length, :].reshape(peers * length, LANES)
    keys = recv[:, length : 2 * length, :].reshape(peers * length, LANES)
    reads = recv[:, 2 * length : 3 * length, :].reshape(peers * length, LANES)
    misc = [recv[t, 3 * length :, :] for t in range(peers)]
    raw_t = jnp.concatenate([m[:, :length] for m in misc], axis=1)
    part = jnp.concatenate([tn(keys, tokens), tn(reads, tokens), nn(raw_t, tokens)[: count - LANES]], axis=0)
    chosen = sel[...]
    head = sum(m.astype(F32) for m in misc)[8:10]
    sums = jnp.concatenate(
        [
            nn(chosen, keys)[0:2],
            nn(chosen, reads)[0:2],
            lane_pad(nt(chosen, raw_t)[0:2], LANES),
            head[0:1] + head[1:2],
            jnp.zeros((1, LANES), F32),
        ],
        axis=0,
    )
    upper, lower = part[:count], part[part.shape[0] - count :]
    keep[...] = jnp.where(first, upper, lower)
    keep_sums[...] = sums
    give[...] = jnp.concatenate(
        [jnp.where(first, lower, upper), pack_sums(sums)] + rows_block(rows[...].astype(F32)), axis=0
    ).astype(BF16)


def group_join_kernel(dates, pos, keep, keep_sums, rows_own, got, rows_keep, give, give_low, give_both):
    count = keep.shape[0]
    there = got[...].astype(F32)
    total = keep[...] + there[:count]
    sums = keep_sums[...] + unpack_sums(there[count : count + 16])
    rows = [rows_own[...].astype(F32), block_rows(there[count + 16 :], rows_own.shape[0])]
    same_low, other_low = halves(rows, dates, bit_of(pos, 1) == 0)
    here, high = halves([same_low], dates, bit_of(pos, 2) == 0)
    low, both = halves([other_low], dates, bit_of(pos, 2) == 0)
    rows_keep[...] = here.astype(BF16)
    give_low[...] = low.astype(BF16)
    give_both[...] = both.astype(BF16)
    give[...] = jnp.concatenate([total, pack_sums(sums)] + rows_block(high), axis=0).astype(BF16)


def group_total_kernel(own, got, send, rest):
    count = send.shape[1]
    total = (own[...].astype(F32) + got[...].astype(F32))[: count + 16]
    slab = total[:count].astype(BF16)
    for t in range(send.shape[0]):
        send[t] = slab
    rest[...] = unpack_sums(total[count:])


def store_rows(cols, scale, core, slabs, weight, held, sems):
    count = slabs.shape[1]
    base = cols - count
    for t in range(slabs.shape[0]):
        held[:, t * LANES : (t + 1) * LANES] = slabs[t].astype(F32) * scale
    at = pl.multiple_of(core * base, 8)
    main = pltpu.make_async_copy(held.at[:base], weight.at[pl.ds(at, base)], sems.at[0])
    last = pltpu.make_async_copy(held.at[base:], weight.at[2 * base :], sems.at[1])
    main.start()

    @pl.when(core == 1)
    def _():
        last.start()

    def wait():
        main.wait()

        @pl.when(core == 1)
        def _():
            last.wait()

    return wait


def other_rows_kernel(cols, scale, pos, slabs, weight_in, weight, held, sems):
    store_rows(cols, scale, 1 - bit_of(pos, 0), slabs, weight, held, sems)()


def final_kernel(heads, scale, pos, slabs, rows_own, got, low, both, rest, w_t, *refs):
    outs, (value, inputs, table, head), (held, sems, out_sems) = refs[:5], refs[5:9], refs[9:]
    model_d, cols, dates = w_t.shape[1], w_t.shape[0], value.shape[1]
    wait = store_rows(cols, scale, bit_of(pos, 0), slabs, outs[4], held, sems)
    moves = [
        pltpu.make_async_copy(source, outs[k], out_sems.at[k])
        for k, source in enumerate((value, inputs, table, head))
    ]
    w = w_t[...]
    rows_got = block_rows(got[...].astype(F32)[slabs.shape[1] + 16 :], 2 * dates)
    rows = jnp.concatenate(
        [rows_own[...].astype(F32), rows_got, low[...].astype(F32), both[...].astype(F32)], axis=0
    )
    masks = [0, 1, 4, 5, 2, 3, 6, 7]
    where_to = []
    for mask in masks:
        index = 0
        for bit in range(3):
            here = bit_of(pos, bit)
            index = index + 2**bit * (1 - here if mask >> bit & 1 else here)
        where_to.append(index)
    for k, pixel in enumerate(where_to):
        value[pixel] = rows[k * dates : (k + 1) * dates, :model_d].astype(BF16)
    moves[0].start()
    grads = nn(rows[:, model_d : model_d + EXT].astype(BF16)[:, :cols], w)
    for k, pixel in enumerate(where_to):
        inputs[pixel] = grads[k * dates : (k + 1) * dates].astype(BF16)
    moves[1].start()
    sums = jnp.concatenate([rest[0:2, :], rest[2:4, :], rest[4:6, :]], axis=1)[:, :cols]
    high, low = split(sums)
    table[...] = (nn(high, w) + nn(low, w)) * scale
    total = rest[6:7, :]
    head[...] = jnp.concatenate([total[:, k * heads : (k + 1) * heads] for k in (1, 0, 2)], axis=0) * scale
    for move in moves[2:]:
        move.start()
    wait()
    for move in moves:
        move.wait()


def finish_four_levels(series, w_t, date_s, heads, scale, pixel_dev, dates_dev, tiles, dates):
    length = series.shape[0]
    cols, model_d = w_t.shape
    peers = 2 * tiles
    wide = model_d + EXT
    count = (cols + 8) // 2
    half_rows = length // 2
    payload = count + 16 + half_rows * wide // LANES
    payload_high = count + 16 + 2 * dates_dev * wide // LANES

    def groups(alternate):
        return [
            [t * dates + 4 * high + 2 * low + (c + alternate * t) % 2 for t in range(tiles) for low in range(2)]
            for high in range(2)
            for c in range(2)
        ]

    def across(bit):
        return [(i, i ^ 2**bit) for i in range(dates)]

    send_t, rows_own, rows_give, sel = call(
        functools.partial(group_series_kernel, heads, model_d, dates_dev),
        [
            ((peers, 3 * length + 16, LANES), BF16),
            ((half_rows, wide), BF16),
            ((half_rows, wide), BF16),
            ((16, peers * length), BF16),
        ],
        [date_s, series, w_t],
        1,
    )
    recv_t = lax.all_to_all(
        send_t, ("tile", "date"), split_axis=0, concat_axis=0, tiled=True, axis_index_groups=groups(1)
    )
    keep, keep_sums, give = call(
        group_slab_kernel,
        [((count, LANES), F32), ((8, LANES), F32), ((payload, LANES), BF16)],
        [date_s, recv_t, sel, rows_give],
        1,
    )
    got = lax.ppermute(give, "date", across(0))
    rows_own, give, give_low, give_both = call(
        functools.partial(group_join_kernel, dates_dev),
        [
            ((2 * dates_dev, wide), BF16),
            ((payload_high, LANES), BF16),
            ((2 * dates_dev, wide), BF16),
            ((2 * dates_dev, wide), BF16),
        ],
        [date_s, keep, keep_sums, rows_own, got],
        1,
    )
    got = lax.ppermute(give, "date", across(2))
    rows_both = lax.ppermute(give_both, "date", [(i, i ^ 6) for i in range(dates)])
    rows_low = lax.ppermute(give_low, "date", across(1))
    got, rows_both, rows_low = lax.optimization_barrier((got, rows_both, rows_low))
    send_g, rest = call(
        group_total_kernel, [((peers, count, LANES), BF16), ((8, LANES), F32)], [give, got]
    )
    recv_g = lax.all_to_all(
        send_g, ("tile", "date"), split_axis=0, concat_axis=0, tiled=True, axis_index_groups=groups(0)
    )
    other_g = lax.ppermute(recv_g, "date", across(0))
    outs = [
        jax.ShapeDtypeStruct((pixel_dev, dates_dev, model_d), BF16),
        jax.ShapeDtypeStruct((pixel_dev, dates_dev, model_d), BF16),
        jax.ShapeDtypeStruct((2, model_d), F32),
        jax.ShapeDtypeStruct((3, heads), F32),
        jax.ShapeDtypeStruct((cols, model_d), F32),
    ]
    held = [pltpu.VMEM((count, model_d), F32), pltpu.SemaphoreType.DMA((2,))]
    limit = pltpu.CompilerParams(vmem_limit_bytes=48 * 1024 * 1024)
    value, inputs, table, head, weight_t = pl.pallas_call(
        functools.partial(final_kernel, heads, scale),
        out_shape=outs,
        in_specs=[SMEM] + [VMEM] * 7,
        out_specs=[HBM] * 5,
        scratch_shapes=[pltpu.VMEM(o.shape, o.dtype) for o in outs[:4]]
        + held
        + [pltpu.SemaphoreType.DMA((4,))],
        compiler_params=limit,
    )(date_s, recv_g, rows_own, got, rows_low, rows_both, rest, w_t)
    weight_t = pl.pallas_call(
        functools.partial(other_rows_kernel, cols, scale),
        out_shape=outs[4],
        in_specs=[SMEM, VMEM, HBM],
        out_specs=HBM,
        scratch_shapes=held,
        input_output_aliases={2: 0},
        compiler_params=limit,
    )(date_s, other_g, weight_t)
    return value, inputs, weight_t.T, table, head


def finish_any(series, w_t, date_s, heads, scale, pixel_dev, dates_dev, tiles, dates):
    length = series.shape[0]
    cols, model_d = w_t.shape
    levels = dates // 2
    slab = model_d // tiles
    half = slab // 2
    swap = [(i, i ^ 1) for i in range(dates)]
    planes = [[2 * z + c for z in range(levels)] for c in range(2)]
    rows_core = length // 2
    send_t, own, give_rows, sel = call(
        functools.partial(series_kernel, heads, model_d, 0, dates_dev),
        [
            ((tiles, length, EXT + slab), BF16),
            ((rows_core, model_d + EXT), BF16),
            ((rows_core, model_d + EXT), BF16),
            ((16, length), BF16),
        ],
        [date_s, series, w_t],
        1,
    )
    mixed = [
        [t * dates + 2 * z + (c + t) % 2 for t in range(tiles)] for z in range(levels) for c in range(2)
    ]
    recv_t = lax.all_to_all(
        send_t, ("tile", "date"), split_axis=0, concat_axis=0, tiled=True, axis_index_groups=mixed
    )
    rows_give = cols + 24 + rows_core * (model_d + EXT) // LANES
    keep, keep_sums, give = call(
        functools.partial(slab_kernel, cols),
        [((cols, LANES), F32), ((2, EXT), F32), ((rows_give, LANES), BF16)],
        [date_s, recv_t, sel, give_rows],
        1,
    )
    got = lax.ppermute(give, "date", swap)
    rows_z = cols + 32 + model_d // 16
    (send_z,) = call(
        functools.partial(join_kernel, cols, dates_dev),
        [((levels, rows_z, LANES), BF16)],
        [date_s, keep, keep_sums, got, own],
        1,
    )
    recv_z = lax.all_to_all(
        send_z, "date", split_axis=0, concat_axis=0, tiled=True, axis_index_groups=planes
    )
    send_g, rest = call(
        functools.partial(total_kernel, cols),
        [((tiles, cols, LANES), BF16), ((16, LANES), F32)],
        [recv_z],
    )
    recv_g = lax.all_to_all(send_g, "tile", split_axis=0, concat_axis=0, tiled=True)
    local_outs = [
        ((pixel_dev, dates_dev, model_d), BF16),
        ((pixel_dev, dates_dev, model_d), BF16),
        ((2, model_d), F32),
        ((3, heads), F32),
    ]
    other_g = lax.ppermute(recv_g, "date", swap)
    if half % LANES == 0:
        weight_shape = jax.ShapeDtypeStruct((cols, model_d), F32)
        held = [pltpu.VMEM((tiles, cols, half), F32), pltpu.SemaphoreType.DMA((tiles,))]
        limit = pltpu.CompilerParams(vmem_limit_bytes=48 * 1024 * 1024)
        value, inputs, table, head, weight_t = pl.pallas_call(
            functools.partial(local_weight_kernel, heads, scale, cols, half),
            out_shape=[jax.ShapeDtypeStruct(s, d) for s, d in local_outs] + [weight_shape],
            in_specs=[SMEM] + [VMEM] * 4,
            out_specs=[HBM] * 5,
            scratch_shapes=[pltpu.VMEM(s, d) for s, d in local_outs]
            + held
            + [pltpu.SemaphoreType.DMA((4,))],
            compiler_params=limit,
        )(date_s, recv_g, recv_z, rest, w_t)
        weight_t = pl.pallas_call(
            functools.partial(half_kernel, cols, scale, half),
            out_shape=weight_shape,
            in_specs=[SMEM, VMEM, HBM],
            out_specs=HBM,
            scratch_shapes=held,
            input_output_aliases={2: 0},
            compiler_params=limit,
        )(date_s, other_g, weight_t)
    else:
        value, inputs, table, head = call(
            functools.partial(local_kernel, heads, scale), local_outs, [recv_z, rest, w_t]
        )
        (weight_t,) = call(
            functools.partial(gather_kernel, cols, half, scale),
            [((cols, model_d), F32)],
            [date_s, recv_g, other_g],
            1,
        )
    return (
        value,
        inputs,
        weight_t.T,
        table,
        head,
    )


def on_device(
    layer_input,
    head_input,
    out_grad,
    sensor_ids,
    valid_mask,
    sensor_table,
    proj_weight,
    step_bias,
    decay_log,
    skip_gain,
):
    pixel_dev, dates_dev, model_d = layer_input.shape
    heads = step_bias.shape[0]
    tiles = lax.axis_size("tile")
    dates = lax.axis_size("date")
    assert pixel_dev == dates and dates % 2 == 0
    levels = dates // 2
    length = dates * dates_dev
    slab = model_d // tiles
    half = slab // 2
    date_s = lax.axis_index("date").astype(jnp.int32).reshape(1)
    w_t = proj_weight.T
    scale = 1.0 / math.sqrt(pixel_dev * dates_dev * tiles * dates)

    operands = [
        sensor_ids,
        valid_mask.T,
        sensor_table,
        step_bias[None],
        decay_log[None],
        skip_gain[None],
        layer_input,
        head_input,
        out_grad,
    ]
    packed = pl.pallas_call(
        pack_kernel,
        out_shape=jax.ShapeDtypeStruct((pixel_dev, dates_dev, 3 * model_d + LANES), BF16),
        in_specs=[SMEM] + [HBM] * 9,
        out_specs=VMEM,
        scratch_shapes=[
            pltpu.SMEM((dates_dev,), jnp.int32),
            pltpu.VMEM((dates_dev, pixel_dev), jnp.int32),
            pltpu.VMEM((2, model_d), F32),
            pltpu.VMEM((3, heads), F32),
            pltpu.VMEM((pixel_dev, dates_dev, model_d), BF16),
            pltpu.SemaphoreType.DMA((9,)),
        ],
        compiler_params=pltpu.CompilerParams(vmem_limit_bytes=16 * 1024 * 1024),
    )(date_s, *[pltpu.with_memory_space_constraint(operand, pltpu.HBM) for operand in operands])
    series = lax.all_to_all(packed, "date", split_axis=0, concat_axis=0, tiled=True).reshape(
        length, 3 * model_d + LANES
    )

    if levels == 4 and model_d == 2 * LANES * tiles:
        finish = finish_four_levels
    else:
        finish = finish_any
    return finish(series, w_t, date_s, heads, scale, pixel_dev, dates_dev, tiles, dates)


def solution(mesh):
    in_specs = (
        P("tile", "date", None),
        P("tile", "date", None),
        P("tile", "date", None),
        P("date"),
        P("tile", "date"),
        P(),
        P(),
        P(),
        P(),
        P(),
    )
    out_specs = (P("tile", "date", None), P("tile", "date", None), P(), P(), P())
    return jax.shard_map(
        on_device, mesh=mesh, in_specs=in_specs, out_specs=out_specs, check_vma=False
    )
```

```python
import functools
import math

import jax
import jax.numpy as jnp
from jax import lax
from jax.experimental import pallas as pl
from jax.experimental.pallas import tpu as pltpu
from jax.sharding import PartitionSpec as P

NEG_FILL = -1e30
HIGHEST_PREC = lax.Precision.HIGHEST
F32 = jnp.float32
BF16 = jnp.bfloat16
LANES = 128
EXT = 384


def nt(a, b, precision=None):
    return lax.dot_general(
        a, b, (((1,), (1,)), ((), ())), preferred_element_type=F32, precision=precision
    )


def nn(a, b, precision=None):
    return lax.dot_general(
        a, b, (((1,), (0,)), ((), ())), preferred_element_type=F32, precision=precision
    )


def tn(a, b):
    return lax.dot_general(a, b, (((0,), (0,)), ((), ())), preferred_element_type=F32)


def split(x):
    high = x.astype(BF16)
    return high, (x - high.astype(F32)).astype(BF16)


def bit_of(pos, bit):
    return lax.rem(lax.div(pos[0], 2**bit), 2)


def halves(arrays, span, first):
    kept, given = [], []
    for array in arrays:
        for at in range(0, array.shape[0], 2 * span):
            a, b = array[at : at + span], array[at + span : at + 2 * span]
            kept.append(jnp.where(first, a, b))
            given.append(jnp.where(first, b, a))
    return jnp.concatenate(kept, axis=0), jnp.concatenate(given, axis=0)


def series_terms(heads, model_d, recv, w_t):
    length = recv.shape[0]
    width_p = model_d // heads
    states = (w_t.shape[0] - heads) // 2
    mixed = recv[:, :model_d]
    aux = recv[:, 3 * model_d :].astype(F32)
    gate = aux[:, 0:1]
    ids = aux[:, 1:2]
    params = []
    for at in range(2, 2 + 9 * heads, 3 * heads):
        params.append(sum(aux[0:1, at + k * heads : at + (k + 1) * heads] for k in range(3)))
    bias, rate, skip = params[0], -jnp.exp(params[1]), params[2]
    projected = nt(mixed, w_t[...])
    keys = projected[:, :states].astype(BF16)
    reads = projected[:, states : 2 * states].astype(BF16)
    step_pre = projected[:, 2 * states :] + bias
    softplus = jnp.maximum(step_pre, 0.0) + jnp.log1p(jnp.exp(-jnp.abs(step_pre)))
    steps_b = (gate * softplus).astype(BF16)
    steps = steps_b.astype(F32)

    row = lax.broadcasted_iota(jnp.int32, (length, length), 0)
    col = lax.broadcasted_iota(jnp.int32, (length, length), 1)
    upper = col >= row
    upper_f = upper.astype(F32)
    eye = (col == row).astype(F32)
    lower_b = (row >= col).astype(BF16)
    head_row = lax.broadcasted_iota(jnp.int32, (heads, heads), 0)
    head_col = lax.broadcasted_iota(jnp.int32, (heads, heads), 1)
    eye_h = (head_row == head_col).astype(F32)
    rate_col = jnp.sum(eye_h * rate, axis=1, keepdims=True)
    log_col = nn(lower_b, steps_b) * rate
    steps_t = nt(eye_h.astype(BF16), steps_b).astype(BF16)
    log_row = nn(steps_t, upper.astype(BF16)) * rate_col
    scores_t = nt(keys, reads)

    pair_t = jnp.zeros((length, length), F32)
    mixes, weighted_cols, read_rows, skip_cols = [], [], [], []
    for h in range(heads):
        lo = model_d + h * width_p
        x_h = recv[:, lo : lo + width_p]
        g_h = recv[:, lo + model_d : lo + model_d + width_p]
        dt_h = steps[:, h : h + 1]
        gap = log_row[h : h + 1, :] - log_col[:, h : h + 1]
        decay = jnp.exp(jnp.where(upper, gap, NEG_FILL))
        cross = nt(x_h, g_h)
        mix = decay * scores_t
        pair_t = pair_t + decay * cross * dt_h
        both = mix * cross
        weighted = jnp.sum(both, axis=1, keepdims=True)
        weighted_cols.append(weighted)
        read_rows.append(jnp.sum(both * dt_h, axis=0, keepdims=True))
        skip_cols.append(jnp.sum(cross * eye, axis=1, keepdims=True))
        mixes.append((mix.astype(BF16), g_h, dt_h, skip[:, h : h + 1]))

    weighted = jnp.concatenate(weighted_cols, axis=1)
    read_sum = jnp.concatenate(read_rows, axis=0)
    skip_terms = jnp.concatenate(skip_cols, axis=1)
    later = nt(upper_f, read_sum, HIGHEST_PREC) - nn(upper_f, steps * weighted, HIGHEST_PREC)
    step_grad = (weighted + rate * later).astype(BF16).astype(F32)
    decay_terms = steps * later * rate
    pair_b = pair_t.astype(BF16)
    grad_keys = nn(pair_b, reads)
    grad_reads = tn(pair_b, keys)
    raw = step_grad * gate * jax.nn.sigmoid(step_pre)
    terms = jnp.concatenate(
        [raw, decay_terms, skip_terms, jnp.zeros((length, LANES - 3 * heads), F32)], axis=1
    )
    ids_row = jnp.sum(eye * ids, axis=0, keepdims=True)
    return mixes, grad_keys, grad_reads, raw, terms, ids_row, eye_h


def value_columns(mixes):
    return [nn(mix, g_h) * dt_h + skip_h * g_h.astype(F32) for mix, g_h, dt_h, skip_h in mixes]


def sensor_rows(ids_row):
    zeros = jnp.zeros((14, ids_row.shape[1]), F32)
    return jnp.concatenate([1.0 - ids_row, ids_row, zeros], axis=0).astype(BF16)


def series_kernel(heads, model_d, bit, span, pos, recv, w_t, send, own, give, sel):
    tiles, _, width = send.shape
    slab = width - EXT
    mixes, grad_keys, grad_reads, _, terms, ids_row, _ = series_terms(heads, model_d, recv, w_t)
    high = terms.astype(BF16).astype(F32)
    tail = high + pltpu.roll(terms - high, 3 * heads, 1)
    ext_f = jnp.concatenate([grad_keys, grad_reads, tail], axis=1)
    ext = ext_f.astype(BF16)
    back = jnp.concatenate(value_columns(mixes) + [ext_f], axis=1)
    kept, given = halves([back], span, bit_of(pos, bit) == 0)
    own[...] = kept.astype(BF16)
    give[...] = given.astype(BF16)
    for t in range(tiles):
        send[t, :, :EXT] = ext
        send[t, :, EXT:] = recv[:, t * slab : (t + 1) * slab]
    sel[...] = sensor_rows(ids_row)


def direct_series_kernel(heads, model_d, dates, pos, tile, recv, w_t, *refs):
    sends, (own, give, sel) = refs[:-3], refs[-3:]
    length = recv.shape[0]
    slab = 2 * LANES
    mixes, grad_keys, grad_reads, raw, terms, ids_row, eye_h = series_terms(heads, model_d, recv, w_t)
    raw_t = nt(eye_h.astype(BF16), raw.astype(BF16))
    total = jnp.sum(terms, axis=0, keepdims=True)
    high = total.astype(BF16).astype(F32)
    misc = jnp.concatenate(
        [lane_pad(raw_t, LANES), high, total - high, jnp.zeros((6, LANES), F32)], axis=0
    )
    grads = jnp.concatenate([grad_keys, grad_reads, misc], axis=0).astype(BF16)
    for k, send in enumerate(sends):
        for block in range(2):
            at = pl.multiple_of((tile[0] ^ k) * slab + block * LANES, LANES)
            send[block * length : (block + 1) * length] = recv[:, pl.ds(at, LANES)]
        send[2 * length :] = grads
    back = jnp.concatenate(value_columns(mixes) + [grad_keys, grad_reads, lane_pad(raw, LANES)], axis=1)
    kept, given = halves([back], dates, bit_of(pos, 0) == 0)
    own[...] = kept.astype(BF16)
    give[...] = given.astype(BF16)
    sel[...] = sensor_rows(ids_row)


def pack_kernel(pos, tile, ids_in, mask_in, table_in, bias_in, decay_in, skip_in, layer, values, cotangent, out, ids, mask_t, table, params, layer_v, sems):
    pixels, dates, model_d = layer.shape
    small = [
        pltpu.make_async_copy(ids_in, ids, sems.at[0]),
        pltpu.make_async_copy(mask_in, mask_t, sems.at[1]),
        pltpu.make_async_copy(table_in, table, sems.at[2]),
        pltpu.make_async_copy(layer, layer_v, sems.at[3]),
        pltpu.make_async_copy(bias_in, params.at[0:1], sems.at[6]),
        pltpu.make_async_copy(decay_in, params.at[1:2], sems.at[7]),
        pltpu.make_async_copy(skip_in, params.at[2:3], sems.at[8]),
    ]
    large = [
        pltpu.make_async_copy(values, out.at[:, :, model_d : 2 * model_d], sems.at[4]),
        pltpu.make_async_copy(cotangent, out.at[:, :, 2 * model_d : 3 * model_d], sems.at[5]),
    ]
    for copy in small[3:4] + large + small[:3] + small[4:]:
        copy.start()
    for copy in small:
        copy.wait()
    rows = [jnp.where(ids[i] == 1, table[1:2, :], table[0:1, :]) for i in range(dates)]
    embed = jnp.concatenate(rows, axis=0)
    row = lax.broadcasted_iota(jnp.int32, (dates, LANES), 0)
    lane = lax.broadcasted_iota(jnp.int32, (dates, LANES), 1)
    second = jnp.zeros((dates, LANES), F32)
    for i in range(dates):
        second = jnp.where((row == i) & (lane == 1), (ids[i] == 1).astype(F32), second)
    gate = mask_t[...].astype(F32)
    at = 2
    for k in range(3):
        rest = params[k : k + 1, :]
        for _ in range(3):
            term = rest.astype(BF16).astype(F32)
            rest = rest - term
            term = jnp.concatenate([jnp.zeros((1, at), F32), term, jnp.zeros((1, LANES - at - term.shape[1]), F32)], axis=1)
            second = second + term
            at = at + params.shape[1]
    for p in range(pixels):
        out[p, :, 3 * model_d :] = jnp.where(lane == 0, gate[:, p : p + 1], second).astype(BF16)
        out[p, :, :model_d] = (layer_v[p].astype(F32) + embed).astype(BF16)
    for copy in large:
        copy.wait()


def lane_pad(x, width):
    if x.shape[1] == width:
        return x
    return jnp.concatenate([x, jnp.zeros((x.shape[0], width - x.shape[1]), x.dtype)], axis=1)


def sum_rows(sums):
    high = sums.astype(BF16).astype(F32)
    low = (sums - high).astype(BF16).astype(F32)
    rows = jnp.concatenate([high, low, jnp.zeros((4, EXT), F32)], axis=0)
    return [rows[:, b * LANES : (b + 1) * LANES] for b in range(EXT // LANES)]


def rows_sum(block):
    rows = jnp.concatenate([block[8 * b : 8 * b + 8, :] for b in range(EXT // LANES)], axis=1)
    return rows[0:2] + rows[2:4]


def slab_kernel(cols, pos, recv, sel, rows, keep, keep_sums, give):
    tiles, length, width = recv.shape
    slab = width - EXT
    half = slab // 2
    ext = recv[:, :, :EXT].reshape(tiles * length, EXT)
    tokens = recv[:, :, EXT:].reshape(tiles * length, slab)
    part = tn(ext, tokens)[:cols]
    sums = jnp.zeros((16, EXT), F32)
    for t in range(tiles):
        sums = sums + nn(sel[...], recv[t, :, :EXT])
    sums = sums[0:2]
    mine = bit_of(pos, 0) == 0
    first = lane_pad(part[:, :half], LANES)
    second = lane_pad(part[:, half:], LANES)
    keep[...] = jnp.where(mine, first, second)
    keep_sums[...] = sums
    other = jnp.where(mine, second, first)
    blocks = [rows[:, b * LANES : (b + 1) * LANES].astype(F32) for b in range(rows.shape[1] // LANES)]
    give[...] = jnp.concatenate([other] + sum_rows(sums) + blocks, axis=0).astype(BF16)


def join_kernel(cols, dates, pos, keep, keep_sums, got, own, send):
    levels = send.shape[0]
    first = bit_of(pos, 0) == 0
    model_d = own.shape[1] - EXT
    total = keep[...] + got[:cols, :].astype(F32)
    sums = sum_rows(keep_sums[...] + rows_sum(got[cols : cols + 24, :].astype(F32)))
    pair_sums = jnp.concatenate([sums[0][:4], sums[1][:4]], axis=0)
    mine, count = own[...].astype(F32), own.shape[0]
    tall = got[cols + 24 :, :].astype(F32)
    theirs = jnp.concatenate([tall[k : k + count] for k in range(0, tall.shape[0], count)], axis=1)
    firsts, seconds = jnp.where(first, mine, theirs), jnp.where(first, theirs, mine)
    lane = lax.broadcasted_iota(jnp.int32, (8, LANES), 1)
    last = pltpu.roll(sums[2], 64, 1)
    for z in range(levels):
        at = z * dates
        rows = jnp.concatenate([firsts[at : at + dates], seconds[at : at + dates]], axis=0)
        ext = [rows[:, model_d + b * LANES : model_d + (b + 1) * LANES] for b in range(EXT // LANES)]
        misc = jnp.where(lane < 64, ext[2], last)
        value = [rows[:, b * LANES : (b + 1) * LANES] for b in range(model_d // LANES)]
        send[z] = jnp.concatenate([total, ext[0], ext[1], misc, pair_sums] + value, axis=0).astype(BF16)


def total_kernel(cols, recv, send, rest):
    levels = recv.shape[0]
    total = recv[0].astype(F32)
    for z in range(1, levels):
        total = total + recv[z].astype(F32)
    slab = total[:cols].astype(BF16)
    for t in range(send.shape[0]):
        send[t] = slab
    rest[...] = total[cols + 16 : cols + 32]


def store_half(cols, scale, core, half, slabs, weight, held, sems):
    copies = []
    for t in range(slabs.shape[0]):
        held[t] = slabs[t].astype(F32)[:cols] * scale
        at = pl.multiple_of((2 * t + core) * half, half)
        copies.append(pltpu.make_async_copy(held.at[t], weight.at[:, pl.ds(at, half)], sems.at[t]))
        copies[-1].start()
    return copies


def half_kernel(cols, scale, half, pos, slabs, weight_in, weight, held, sems):
    for copy in store_half(cols, scale, 1 - bit_of(pos, 0), half, slabs, weight, held, sems):
        copy.wait()


def local_weight_kernel(heads, scale, cols, half, pos, slabs, recv, rest, w_t, *refs):
    outs, held_outs = refs[:5], refs[5:10]
    held, sems, out_sems = held_outs[4], refs[10], refs[11]
    copies = store_half(cols, scale, bit_of(pos, 0), half, slabs, outs[4], held, sems)
    moves = [pltpu.make_async_copy(held_outs[k], outs[k], out_sems.at[k]) for k in range(4)]
    local_kernel(heads, scale, recv, rest, w_t, *held_outs[:4], moves)
    for copy in copies + moves:
        copy.wait()


def write_sums(heads, scale, sums, w, table, head):
    cols = w.shape[0]
    high, low = split(sums[:, :cols])
    table[...] = (nn(high, w) + nn(low, w)) * scale
    both = sums[0:1] + sums[1:2]
    at = cols - heads
    rows = []
    for k in (1, 0, 2):
        lo = at + k * heads
        rows.append(both[:, lo : lo + heads] + both[:, lo + 3 * heads : lo + 4 * heads])
    head[...] = jnp.concatenate(rows, axis=0) * scale


def local_kernel(heads, scale, recv, rest, w_t, value, inputs, table, head, moves=()):
    levels = recv.shape[0]
    model_d = w_t.shape[1]
    cols = w_t.shape[0]
    dates = value.shape[1]
    w = w_t[...]
    ext_rows = []
    for z in range(levels):
        rows = recv[z].astype(F32)
        ext_rows.append(jnp.concatenate([rows[cols + 8 * b : cols + 8 * b + 8] for b in range(3)], axis=1))
        at = cols + 32
        values = jnp.concatenate([rows[at + 8 * b : at + 8 * b + 8] for b in range(model_d // LANES)], axis=1)
        for c in range(2):
            value[2 * z + c] = values[c * dates : (c + 1) * dates].astype(BF16)
    for move in moves[:1]:
        move.start()
    grads = nn(jnp.concatenate(ext_rows, axis=0).astype(BF16)[:, :cols], w)
    for p in range(2 * levels):
        inputs[p] = grads[p * dates : (p + 1) * dates].astype(BF16)
    for move in moves[1:2]:
        move.start()
    last = pltpu.roll(rest[0:8, :], 64, 1)
    sums = jnp.concatenate([rest[8:12, :], rest[12:16, :], last[0:4]], axis=1)
    sums = sums[0:2] + sums[2:4]
    write_sums(heads, scale, sums, w, table, head)
    for move in moves[2:]:
        move.start()


def gather_kernel(cols, half, scale, pos, own, other, out):
    tiles = own.shape[0]
    mine = bit_of(pos, 0) == 0
    for t in range(tiles):
        a = own[t].astype(F32)
        b = other[t].astype(F32)
        first = jnp.where(mine, a, b)[:cols, :half]
        second = jnp.where(mine, b, a)[:cols, :half]
        out[:, 2 * half * t : 2 * half * (t + 1)] = jnp.concatenate([first, second], axis=1) * scale


VMEM = pl.BlockSpec(memory_space=pltpu.VMEM)
SMEM = pl.BlockSpec(memory_space=pltpu.SMEM)
HBM = pl.BlockSpec(memory_space=pltpu.HBM)


def call(kernel, outs, ins, smem=0):
    return pl.pallas_call(
        kernel,
        out_shape=[jax.ShapeDtypeStruct(s, d) for s, d in outs],
        in_specs=[SMEM] * smem + [VMEM] * (len(ins) - smem),
        out_specs=[VMEM] * len(outs),
        compiler_params=pltpu.CompilerParams(vmem_limit_bytes=48 * 1024 * 1024),
    )(*ins)


def rows_block(rows):
    return [rows[:, b * LANES : (b + 1) * LANES] for b in range(rows.shape[1] // LANES)]


def block_rows(block, count):
    return jnp.concatenate([block[k : k + count] for k in range(0, block.shape[0], count)], axis=1)


def pack_sums(sums):
    high = sums.astype(BF16).astype(F32)
    return jnp.concatenate([high, sums - high], axis=0)


def unpack_sums(rows):
    return rows[:8] + rows[8:16]


def pair_sum(parts):
    return (parts[0] + parts[1]) + (parts[2] + parts[3])


def direct_slab_kernel(pos, *refs):
    parts, (sel, rows, keep, keep_sums, give) = refs[:4], refs[4:]
    cols = keep.shape[0]
    length = sel.shape[1]
    first = bit_of(pos, 0) == 0
    chosen = sel[...]
    tokens, keys, reads, raw_t, sums = [], [], [], [], []
    for part in parts:
        tokens.append(jnp.concatenate([part[:length], part[length : 2 * length]], axis=1))
        keys.append(part[2 * length : 3 * length])
        reads.append(part[3 * length : 4 * length])
        misc = part[4 * length :]
        raw_t.append(misc[:, :length])
        head = misc.astype(F32)[8:10]
        sums.append(
            jnp.concatenate(
                [
                    nn(chosen, keys[-1])[0:2],
                    nn(chosen, reads[-1])[0:2],
                    lane_pad(nt(chosen, raw_t[-1])[0:2], LANES),
                    head[0:1] + head[1:2],
                    jnp.zeros((1, LANES), F32),
                ],
                axis=0,
            )
        )
    tokens = jnp.concatenate(tokens, axis=0)
    slab = jnp.concatenate(
        [
            tn(jnp.concatenate(keys, axis=0), tokens),
            tn(jnp.concatenate(reads, axis=0), tokens),
            nn(jnp.concatenate(raw_t, axis=1), tokens)[: cols - 2 * LANES],
        ],
        axis=0,
    )
    left, right = slab[:, :LANES], slab[:, LANES:]
    keep[...] = jnp.where(first, left, right)
    packed = pack_sums(pair_sum(sums))
    keep_sums[...] = unpack_sums(packed)
    give[...] = jnp.concatenate(
        [jnp.where(first, right, left), packed] + rows_block(rows[...].astype(F32)), axis=0
    ).astype(BF16)


def direct_join_kernel(dates, pos, keep, keep_sums, rows_own, got, rows_keep, own, low, high, both):
    cols = keep.shape[0]
    there = got[...].astype(F32)
    total = keep[...] + there[:cols]
    sums = keep_sums[...] + unpack_sums(there[cols : cols + 16])
    rows = [rows_own[...].astype(F32), block_rows(there[cols + 16 :], rows_own.shape[0])]
    same_low, other_low = halves(rows, dates, bit_of(pos, 1) == 0)
    here, high_rows = halves([same_low], dates, bit_of(pos, 2) == 0)
    low_rows, both_rows = halves([other_low], dates, bit_of(pos, 2) == 0)
    rows_keep[...] = here.astype(BF16)
    common = jnp.concatenate([total, pack_sums(sums)], axis=0).astype(BF16)
    own[...] = common
    for send, part in ((low, low_rows), (high, high_rows), (both, both_rows)):
        send[...] = jnp.concatenate([common] + rows_block(part.astype(BF16)), axis=0)


def direct_total_kernel(own, low, high, both, send, rest):
    cols = send.shape[0]
    total = pair_sum([part[...].astype(F32)[: cols + 16] for part in (own, low, high, both)])
    send[...] = total[:cols].astype(BF16)
    rest[...] = unpack_sums(total[cols:])


def store_slabs(scale, tile, core, slabs, weight, held, sems):
    copies = []
    for k, slab in enumerate(slabs):
        held[k] = slab.astype(F32) * scale
        at = pl.multiple_of((2 * (tile ^ k) + core) * LANES, LANES)
        copies.append(pltpu.make_async_copy(held.at[k], weight.at[:, pl.ds(at, LANES)], sems.at[k]))
        copies[-1].start()
    return copies


def other_slabs_kernel(scale, pos, tile, slabs, weight_in, weight, held, sems):
    parts = [slabs[k] for k in range(slabs.shape[0])]
    for copy in store_slabs(scale, tile[0], 1 - bit_of(pos, 0), parts, weight, held, sems):
        copy.wait()


def final_kernel(heads, scale, pos, tile, slabs, rows_own, low, high, both, rest, w_t, *refs):
    outs, (value, inputs, table, head), (held, sems, out_sems) = refs[:5], refs[5:9], refs[9:]
    model_d, cols, dates = w_t.shape[1], w_t.shape[0], value.shape[1]
    parts = [slabs[k] for k in range(slabs.shape[0])]
    copies = store_slabs(scale, tile[0], bit_of(pos, 0), parts, outs[4], held, sems)
    moves = [
        pltpu.make_async_copy(source, outs[k], out_sems.at[k])
        for k, source in enumerate((value, inputs, table, head))
    ]
    w = w_t[...]
    rows = [rows_own[...].astype(F32)]
    for part in (low, high, both):
        rows.append(block_rows(part[...].astype(F32)[cols + 16 :], 2 * dates))
    rows = jnp.concatenate(rows, axis=0)
    masks = [0, 1, 2, 3, 4, 5, 6, 7]
    for k, mask in enumerate(masks):
        value[pos[0] ^ mask] = rows[k * dates : (k + 1) * dates, :model_d].astype(BF16)
    moves[0].start()
    grads = nn(rows[:, model_d : model_d + EXT].astype(BF16)[:, :cols], w)
    for k, mask in enumerate(masks):
        inputs[pos[0] ^ mask] = grads[k * dates : (k + 1) * dates].astype(BF16)
    moves[1].start()
    sums = jnp.concatenate([rest[0:2, :], rest[2:4, :], rest[4:6, :]], axis=1)[:, :cols]
    parts_high, parts_low = split(sums)
    table[...] = (nn(parts_high, w) + nn(parts_low, w)) * scale
    total = rest[6:7, :]
    head[...] = jnp.concatenate([total[:, k * heads : (k + 1) * heads] for k in (1, 0, 2)], axis=0) * scale
    for move in moves[2:]:
        move.start()
    for copy in copies + moves:
        copy.wait()


def finish_direct(series, w_t, date_s, tile_s, heads, scale, pixel_dev, dates_dev, tiles, dates):
    length = series.shape[0]
    cols, model_d = w_t.shape
    wide = model_d + EXT
    half_rows = length // 2
    payload = cols + 16 + half_rows * wide // LANES
    payload_z = cols + 16 + 2 * dates_dev * wide // LANES
    axes = ("tile", "date")

    def across(mask):
        return [(i, i ^ mask) for i in range(tiles * dates)]

    *sends, rows_own, rows_give, sel = call(
        functools.partial(direct_series_kernel, heads, model_d, dates_dev),
        [((4 * length + 16, LANES), BF16)] * tiles
        + [((half_rows, wide), BF16), ((half_rows, wide), BF16), ((16, length), BF16)],
        [date_s, tile_s, series, w_t],
        2,
    )
    parts = {k: lax.ppermute(sends[k], axes, across(dates * k + k % 2)) for k in (3, 2, 1)}
    keep, keep_sums, give = call(
        direct_slab_kernel,
        [((cols, LANES), F32), ((8, LANES), F32), ((payload, LANES), BF16)],
        [date_s, sends[0], parts[1], parts[2], parts[3], sel, rows_give],
        1,
    )
    got = lax.ppermute(give, axes, across(1))
    rows_own, own, *levels = call(
        functools.partial(direct_join_kernel, dates_dev),
        [((2 * dates_dev, wide), BF16), ((cols + 16, LANES), BF16)] + [((payload_z, LANES), BF16)] * 3,
        [date_s, keep, keep_sums, rows_own, got],
        1,
    )
    arrived = {k: lax.ppermute(levels[k - 1], axes, across(2 * k)) for k in (3, 2, 1)}
    low, high, both = (arrived[k] for k in (1, 2, 3))
    slab, rest = call(
        direct_total_kernel, [((cols, LANES), BF16), ((8, LANES), F32)], [own, low, high, both]
    )
    gathered = {k: lax.ppermute(slab, axes, across(dates * k)) for k in (3, 2, 1)}
    slabs = jnp.stack([slab] + [gathered[k] for k in (1, 2, 3)])
    other_slabs = lax.ppermute(slabs, axes, across(1))
    outs = [
        jax.ShapeDtypeStruct((pixel_dev, dates_dev, model_d), BF16),
        jax.ShapeDtypeStruct((pixel_dev, dates_dev, model_d), BF16),
        jax.ShapeDtypeStruct((2, model_d), F32),
        jax.ShapeDtypeStruct((3, heads), F32),
        jax.ShapeDtypeStruct((cols, model_d), F32),
    ]
    held = [pltpu.VMEM((tiles, cols, LANES), F32), pltpu.SemaphoreType.DMA((tiles,))]
    limit = pltpu.CompilerParams(vmem_limit_bytes=48 * 1024 * 1024)
    value, inputs, table, head, weight_t = pl.pallas_call(
        functools.partial(final_kernel, heads, scale),
        out_shape=outs,
        in_specs=[SMEM] * 2 + [VMEM] * 7,
        out_specs=[HBM] * 5,
        scratch_shapes=[pltpu.VMEM(o.shape, o.dtype) for o in outs[:4]]
        + held
        + [pltpu.SemaphoreType.DMA((4,))],
        compiler_params=limit,
    )(date_s, tile_s, slabs, rows_own, low, high, both, rest, w_t)
    weight_t = pl.pallas_call(
        functools.partial(other_slabs_kernel, scale),
        out_shape=outs[4],
        in_specs=[SMEM, SMEM, VMEM, HBM],
        out_specs=HBM,
        scratch_shapes=held,
        input_output_aliases={3: 0},
        compiler_params=limit,
    )(date_s, tile_s, other_slabs, weight_t)
    return value, inputs, weight_t.T, table, head


def finish_any(series, w_t, date_s, tile_s, heads, scale, pixel_dev, dates_dev, tiles, dates):
    length = series.shape[0]
    cols, model_d = w_t.shape
    levels = dates // 2
    slab = model_d // tiles
    half = slab // 2
    swap = [(i, i ^ 1) for i in range(dates)]
    planes = [[2 * z + c for z in range(levels)] for c in range(2)]
    rows_core = length // 2
    send_t, own, give_rows, sel = call(
        functools.partial(series_kernel, heads, model_d, 0, dates_dev),
        [
            ((tiles, length, EXT + slab), BF16),
            ((rows_core, model_d + EXT), BF16),
            ((rows_core, model_d + EXT), BF16),
            ((16, length), BF16),
        ],
        [date_s, series, w_t],
        1,
    )
    mixed = [
        [t * dates + 2 * z + (c + t) % 2 for t in range(tiles)] for z in range(levels) for c in range(2)
    ]
    recv_t = lax.all_to_all(
        send_t, ("tile", "date"), split_axis=0, concat_axis=0, tiled=True, axis_index_groups=mixed
    )
    rows_give = cols + 24 + rows_core * (model_d + EXT) // LANES
    keep, keep_sums, give = call(
        functools.partial(slab_kernel, cols),
        [((cols, LANES), F32), ((2, EXT), F32), ((rows_give, LANES), BF16)],
        [date_s, recv_t, sel, give_rows],
        1,
    )
    got = lax.ppermute(give, "date", swap)
    rows_z = cols + 32 + model_d // 16
    (send_z,) = call(
        functools.partial(join_kernel, cols, dates_dev),
        [((levels, rows_z, LANES), BF16)],
        [date_s, keep, keep_sums, got, own],
        1,
    )
    recv_z = lax.all_to_all(
        send_z, "date", split_axis=0, concat_axis=0, tiled=True, axis_index_groups=planes
    )
    send_g, rest = call(
        functools.partial(total_kernel, cols),
        [((tiles, cols, LANES), BF16), ((16, LANES), F32)],
        [recv_z],
    )
    recv_g = lax.all_to_all(send_g, "tile", split_axis=0, concat_axis=0, tiled=True)
    local_outs = [
        ((pixel_dev, dates_dev, model_d), BF16),
        ((pixel_dev, dates_dev, model_d), BF16),
        ((2, model_d), F32),
        ((3, heads), F32),
    ]
    other_g = lax.ppermute(recv_g, "date", swap)
    if half % LANES == 0:
        weight_shape = jax.ShapeDtypeStruct((cols, model_d), F32)
        held = [pltpu.VMEM((tiles, cols, half), F32), pltpu.SemaphoreType.DMA((tiles,))]
        limit = pltpu.CompilerParams(vmem_limit_bytes=48 * 1024 * 1024)
        value, inputs, table, head, weight_t = pl.pallas_call(
            functools.partial(local_weight_kernel, heads, scale, cols, half),
            out_shape=[jax.ShapeDtypeStruct(s, d) for s, d in local_outs] + [weight_shape],
            in_specs=[SMEM] + [VMEM] * 4,
            out_specs=[HBM] * 5,
            scratch_shapes=[pltpu.VMEM(s, d) for s, d in local_outs]
            + held
            + [pltpu.SemaphoreType.DMA((4,))],
            compiler_params=limit,
        )(date_s, recv_g, recv_z, rest, w_t)
        weight_t = pl.pallas_call(
            functools.partial(half_kernel, cols, scale, half),
            out_shape=weight_shape,
            in_specs=[SMEM, VMEM, HBM],
            out_specs=HBM,
            scratch_shapes=held,
            input_output_aliases={2: 0},
            compiler_params=limit,
        )(date_s, other_g, weight_t)
    else:
        value, inputs, table, head = call(
            functools.partial(local_kernel, heads, scale), local_outs, [recv_z, rest, w_t]
        )
        (weight_t,) = call(
            functools.partial(gather_kernel, cols, half, scale),
            [((cols, model_d), F32)],
            [date_s, recv_g, other_g],
            1,
        )
    return (
        value,
        inputs,
        weight_t.T,
        table,
        head,
    )


def on_device(
    layer_input,
    head_input,
    out_grad,
    sensor_ids,
    valid_mask,
    sensor_table,
    proj_weight,
    step_bias,
    decay_log,
    skip_gain,
):
    pixel_dev, dates_dev, model_d = layer_input.shape
    heads = step_bias.shape[0]
    tiles = lax.axis_size("tile")
    dates = lax.axis_size("date")
    assert pixel_dev == dates and dates % 2 == 0
    levels = dates // 2
    length = dates * dates_dev
    slab = model_d // tiles
    half = slab // 2
    date_s = lax.axis_index("date").astype(jnp.int32).reshape(1)
    tile_s = lax.axis_index("tile").astype(jnp.int32).reshape(1)
    w_t = proj_weight.T
    scale = 1.0 / math.sqrt(pixel_dev * dates_dev * tiles * dates)

    operands = [
        sensor_ids,
        valid_mask.T,
        sensor_table,
        step_bias[None],
        decay_log[None],
        skip_gain[None],
        layer_input,
        head_input,
        out_grad,
    ]
    packed = pl.pallas_call(
        pack_kernel,
        out_shape=jax.ShapeDtypeStruct((pixel_dev, dates_dev, 3 * model_d + LANES), BF16),
        in_specs=[SMEM] * 2 + [HBM] * 9,
        out_specs=VMEM,
        scratch_shapes=[
            pltpu.SMEM((dates_dev,), jnp.int32),
            pltpu.VMEM((dates_dev, pixel_dev), jnp.int32),
            pltpu.VMEM((2, model_d), F32),
            pltpu.VMEM((3, heads), F32),
            pltpu.VMEM((pixel_dev, dates_dev, model_d), BF16),
            pltpu.SemaphoreType.DMA((9,)),
        ],
        compiler_params=pltpu.CompilerParams(vmem_limit_bytes=16 * 1024 * 1024),
    )(date_s, tile_s, *[pltpu.with_memory_space_constraint(operand, pltpu.HBM) for operand in operands])
    series = lax.all_to_all(packed, "date", split_axis=0, concat_axis=0, tiled=True).reshape(
        length, 3 * model_d + LANES
    )

    if levels == 4 and tiles == 4 and model_d == 2 * LANES * tiles:
        finish = finish_direct
    else:
        finish = finish_any
    return finish(series, w_t, date_s, tile_s, heads, scale, pixel_dev, dates_dev, tiles, dates)


def solution(mesh):
    in_specs = (
        P("tile", "date", None),
        P("tile", "date", None),
        P("tile", "date", None),
        P("date"),
        P("tile", "date"),
        P(),
        P(),
        P(),
        P(),
        P(),
    )
    out_specs = (P("tile", "date", None), P("tile", "date", None), P(), P(), P())
    return jax.shard_map(
        on_device, mesh=mesh, in_specs=in_specs, out_specs=out_specs, check_vma=False
    )
```

```python
import functools
import math

import jax
import jax.numpy as jnp
from jax import lax
from jax.experimental import pallas as pl
from jax.experimental.pallas import tpu as pltpu
from jax.sharding import PartitionSpec as P

NEG_FILL = -1e30
HIGHEST_PREC = lax.Precision.HIGHEST
F32 = jnp.float32
BF16 = jnp.bfloat16
LANES = 128
EXT = 384


def nt(a, b, precision=None):
    return lax.dot_general(
        a, b, (((1,), (1,)), ((), ())), preferred_element_type=F32, precision=precision
    )


def nn(a, b, precision=None):
    return lax.dot_general(
        a, b, (((1,), (0,)), ((), ())), preferred_element_type=F32, precision=precision
    )


def tn(a, b):
    return lax.dot_general(a, b, (((0,), (0,)), ((), ())), preferred_element_type=F32)


def split(x):
    high = x.astype(BF16)
    return high, (x - high.astype(F32)).astype(BF16)


def bit_of(pos, bit):
    return lax.rem(lax.div(pos[0], 2**bit), 2)


def halves(arrays, span, first):
    kept, given = [], []
    for array in arrays:
        for at in range(0, array.shape[0], 2 * span):
            a, b = array[at : at + span], array[at + span : at + 2 * span]
            kept.append(jnp.where(first, a, b))
            given.append(jnp.where(first, b, a))
    return jnp.concatenate(kept, axis=0), jnp.concatenate(given, axis=0)


def series_terms(heads, model_d, recv, w_t, order=0):
    length = recv.shape[0]
    width_p = model_d // heads
    states = (w_t.shape[0] - heads) // 2
    mixed = recv[:, :model_d]
    aux = recv[:, 3 * model_d :].astype(F32)
    gate = aux[:, 0:1]
    ids = aux[:, 1:2]
    params = []
    for at in range(2, 2 + 9 * heads, 3 * heads):
        params.append(sum(aux[0:1, at + k * heads : at + (k + 1) * heads] for k in range(3)))
    bias, rate, skip = params[0], -jnp.exp(params[1]), params[2]
    projected = nt(mixed, w_t[...])
    keys = projected[:, :states].astype(BF16)
    reads = projected[:, states : 2 * states].astype(BF16)
    step_pre = projected[:, 2 * states :] + bias
    softplus = jnp.maximum(step_pre, 0.0) + jnp.log1p(jnp.exp(-jnp.abs(step_pre)))
    steps_b = (gate * softplus).astype(BF16)
    steps = steps_b.astype(F32)

    row = lax.broadcasted_iota(jnp.int32, (length, length), 0)
    col = lax.broadcasted_iota(jnp.int32, (length, length), 1)
    upper = (col ^ order) >= (row ^ order)
    upper_f = upper.astype(F32)
    eye = (col == row).astype(F32)
    lower_b = ((row ^ order) >= (col ^ order)).astype(BF16)
    head_row = lax.broadcasted_iota(jnp.int32, (heads, heads), 0)
    head_col = lax.broadcasted_iota(jnp.int32, (heads, heads), 1)
    eye_h = (head_row == head_col).astype(F32)
    rate_col = jnp.sum(eye_h * rate, axis=1, keepdims=True)
    log_col = nn(lower_b, steps_b) * rate
    steps_t = nt(eye_h.astype(BF16), steps_b).astype(BF16)
    log_row = nn(steps_t, upper.astype(BF16)) * rate_col
    scores_t = nt(keys, reads)

    pair_t = jnp.zeros((length, length), F32)
    mixes, weighted_cols, read_rows, skip_cols = [], [], [], []
    for h in range(heads):
        lo = model_d + h * width_p
        x_h = recv[:, lo : lo + width_p]
        g_h = recv[:, lo + model_d : lo + model_d + width_p]
        dt_h = steps[:, h : h + 1]
        gap = log_row[h : h + 1, :] - log_col[:, h : h + 1]
        decay = jnp.exp(jnp.where(upper, gap, NEG_FILL))
        cross = nt(x_h, g_h)
        mix = decay * scores_t
        pair_t = pair_t + decay * cross * dt_h
        both = mix * cross
        weighted = jnp.sum(both, axis=1, keepdims=True)
        weighted_cols.append(weighted)
        read_rows.append(jnp.sum(both * dt_h, axis=0, keepdims=True))
        skip_cols.append(jnp.sum(cross * eye, axis=1, keepdims=True))
        mixes.append((mix.astype(BF16), g_h, dt_h, skip[:, h : h + 1]))

    weighted = jnp.concatenate(weighted_cols, axis=1)
    read_sum = jnp.concatenate(read_rows, axis=0)
    skip_terms = jnp.concatenate(skip_cols, axis=1)
    later = nt(upper_f, read_sum, HIGHEST_PREC) - nn(upper_f, steps * weighted, HIGHEST_PREC)
    step_grad = (weighted + rate * later).astype(BF16).astype(F32)
    decay_terms = steps * later * rate
    pair_b = pair_t.astype(BF16)
    grad_keys = nn(pair_b, reads)
    grad_reads = tn(pair_b, keys)
    raw = step_grad * gate * jax.nn.sigmoid(step_pre)
    terms = jnp.concatenate(
        [raw, decay_terms, skip_terms, jnp.zeros((length, LANES - 3 * heads), F32)], axis=1
    )
    ids_row = jnp.sum(eye * ids, axis=0, keepdims=True)
    return mixes, grad_keys, grad_reads, raw, terms, ids_row, eye_h


def value_columns(mixes):
    return [nn(mix, g_h) * dt_h + skip_h * g_h.astype(F32) for mix, g_h, dt_h, skip_h in mixes]


def sensor_rows(ids_row):
    zeros = jnp.zeros((14, ids_row.shape[1]), F32)
    return jnp.concatenate([1.0 - ids_row, ids_row, zeros], axis=0).astype(BF16)


def series_kernel(heads, model_d, bit, span, pos, recv, w_t, send, own, give, sel):
    tiles, _, width = send.shape
    slab = width - EXT
    mixes, grad_keys, grad_reads, _, terms, ids_row, _ = series_terms(heads, model_d, recv, w_t)
    high = terms.astype(BF16).astype(F32)
    tail = high + pltpu.roll(terms - high, 3 * heads, 1)
    ext_f = jnp.concatenate([grad_keys, grad_reads, tail], axis=1)
    ext = ext_f.astype(BF16)
    back = jnp.concatenate(value_columns(mixes) + [ext_f], axis=1)
    kept, given = halves([back], span, bit_of(pos, bit) == 0)
    own[...] = kept.astype(BF16)
    give[...] = given.astype(BF16)
    for t in range(tiles):
        send[t, :, :EXT] = ext
        send[t, :, EXT:] = recv[:, t * slab : (t + 1) * slab]
    sel[...] = sensor_rows(ids_row)


def direct_series_kernel(heads, model_d, dates, pos, tile, *refs):
    levels, w_t, sends, (own, give, sel, recv) = refs[:4], refs[4], refs[5:-4], refs[-4:]
    length = recv.shape[0]
    slab = 2 * LANES
    recv[...] = jnp.concatenate([level[...].astype(F32) for level in levels], axis=0).astype(BF16)
    order = lax.div(pos[0], 2) * (2 * dates)
    mixes, grad_keys, grad_reads, raw, terms, ids_row, eye_h = series_terms(heads, model_d, recv, w_t, order)
    raw_t = nt(eye_h.astype(BF16), raw.astype(BF16))
    total = jnp.sum(terms, axis=0, keepdims=True)
    high = total.astype(BF16).astype(F32)
    misc = jnp.concatenate(
        [lane_pad(raw_t, LANES), high, total - high, jnp.zeros((6, LANES), F32)], axis=0
    )
    grads = jnp.concatenate([grad_keys, grad_reads, misc], axis=0).astype(BF16)
    for k, send in enumerate(sends):
        for block in range(2):
            at = pl.multiple_of((tile[0] ^ k) * slab + block * LANES, LANES)
            send[block * length : (block + 1) * length] = recv[:, pl.ds(at, LANES)]
        send[2 * length :] = grads
    back = jnp.concatenate(value_columns(mixes) + [grad_keys, grad_reads, lane_pad(raw, LANES)], axis=1)
    kept, given = halves([back], dates, bit_of(pos, 0) == 0)
    own[...] = kept.astype(BF16)
    give[...] = given.astype(BF16)
    sel[...] = sensor_rows(ids_row)


def shared_rows(dates, ids, table, params):
    rows = [jnp.where(ids[i] == 1, table[1:2, :], table[0:1, :]) for i in range(dates)]
    embed = jnp.concatenate(rows, axis=0)
    row = lax.broadcasted_iota(jnp.int32, (dates, LANES), 0)
    lane = lax.broadcasted_iota(jnp.int32, (dates, LANES), 1)
    second = jnp.zeros((dates, LANES), F32)
    for i in range(dates):
        second = jnp.where((row == i) & (lane == 1), (ids[i] == 1).astype(F32), second)
    at = 2
    for k in range(3):
        rest = params[k : k + 1, :]
        for _ in range(3):
            term = rest.astype(BF16).astype(F32)
            rest = rest - term
            term = jnp.concatenate([jnp.zeros((1, at), F32), term, jnp.zeros((1, LANES - at - term.shape[1]), F32)], axis=1)
            second = second + term
            at = at + params.shape[1]
    return embed, second


def pack_kernel(pos, tile, ids_in, mask_in, table_in, bias_in, decay_in, skip_in, layer, values, cotangent, out, ids, mask_t, table, params, layer_v, sems):
    pixels, dates, model_d = layer.shape
    small = [
        pltpu.make_async_copy(ids_in, ids, sems.at[0]),
        pltpu.make_async_copy(mask_in, mask_t, sems.at[1]),
        pltpu.make_async_copy(table_in, table, sems.at[2]),
        pltpu.make_async_copy(layer, layer_v, sems.at[3]),
        pltpu.make_async_copy(bias_in, params.at[0:1], sems.at[6]),
        pltpu.make_async_copy(decay_in, params.at[1:2], sems.at[7]),
        pltpu.make_async_copy(skip_in, params.at[2:3], sems.at[8]),
    ]
    large = [
        pltpu.make_async_copy(values, out.at[:, :, model_d : 2 * model_d], sems.at[4]),
        pltpu.make_async_copy(cotangent, out.at[:, :, 2 * model_d : 3 * model_d], sems.at[5]),
    ]
    for copy in small[3:4] + large + small[:3] + small[4:]:
        copy.start()
    for copy in small:
        copy.wait()
    embed, second = shared_rows(dates, ids, table, params)
    lane = lax.broadcasted_iota(jnp.int32, (dates, LANES), 1)
    gate = mask_t[...].astype(F32)
    for p in range(pixels):
        out[p, :, 3 * model_d :] = jnp.where(lane == 0, gate[:, p : p + 1], second).astype(BF16)
        out[p, :, :model_d] = (layer_v[p].astype(F32) + embed).astype(BF16)
    for copy in large:
        copy.wait()


def direct_pack_kernel(
    pos, w_in, ids_in, mask_in, table_in, bias_in, decay_in, skip_in, layer, values, cotangent, keep, give, w_t, *scratch
):
    ids, mask_t, table, params, layer_v, sems = scratch
    levels, _, dates, model_d = layer.shape
    core = bit_of(pos, 0)
    small = [
        pltpu.make_async_copy(ids_in, ids, sems.at[0]),
        pltpu.make_async_copy(mask_in, mask_t, sems.at[1]),
        pltpu.make_async_copy(table_in, table, sems.at[2]),
        pltpu.make_async_copy(bias_in, params.at[0:1], sems.at[3]),
        pltpu.make_async_copy(decay_in, params.at[1:2], sems.at[4]),
        pltpu.make_async_copy(skip_in, params.at[2:3], sems.at[5]),
        pltpu.make_async_copy(layer, layer_v, sems.at[6]),
    ]
    large = [pltpu.make_async_copy(w_in, w_t, sems.at[11])]
    for k, array in enumerate((values, cotangent)):
        to = slice((k + 1) * model_d, (k + 2) * model_d)
        large.append(pltpu.make_async_copy(array.at[:, core], keep.at[:, :, to], sems.at[7 + k]))
        large.append(pltpu.make_async_copy(array.at[:, 1 - core], give.at[:, :, to], sems.at[9 + k]))
    for copy in small[-1:] + large[1:] + small[:-1] + large[:1]:
        copy.start()
    for copy in small:
        copy.wait()
    embed, extra = shared_rows(dates, ids, table, params)
    lane = lax.broadcasted_iota(jnp.int32, (dates, LANES), 1)
    gate = mask_t[...].astype(F32)
    first = core == 0
    for level in range(levels):
        gates = [gate[:, 2 * level + c : 2 * level + c + 1] for c in range(2)]
        mixed = [layer_v[level, c].astype(F32) + embed for c in range(2)]
        for out, mine in ((keep, first), (give, jnp.logical_not(first))):
            chosen = jnp.where(mine, gates[0], gates[1])
            out[level, :, 3 * model_d :] = jnp.where(lane == 0, chosen, extra).astype(BF16)
            out[level, :, :model_d] = jnp.where(mine, mixed[0], mixed[1]).astype(BF16)
    for copy in large:
        copy.wait()


def level_rows_kernel(pos, keep, got, *outs):
    first = bit_of(pos, 0) == 0
    level = lax.div(pos[0], 2)
    for k, out in enumerate(outs):
        mine, theirs = keep[level ^ k].astype(F32), got[level ^ k].astype(F32)
        out[...] = jnp.concatenate(
            [jnp.where(first, mine, theirs), jnp.where(first, theirs, mine)], axis=0
        ).astype(BF16)


def lane_pad(x, width):
    if x.shape[1] == width:
        return x
    return jnp.concatenate([x, jnp.zeros((x.shape[0], width - x.shape[1]), x.dtype)], axis=1)


def sum_rows(sums):
    high = sums.astype(BF16).astype(F32)
    low = (sums - high).astype(BF16).astype(F32)
    rows = jnp.concatenate([high, low, jnp.zeros((4, EXT), F32)], axis=0)
    return [rows[:, b * LANES : (b + 1) * LANES] for b in range(EXT // LANES)]


def rows_sum(block):
    rows = jnp.concatenate([block[8 * b : 8 * b + 8, :] for b in range(EXT // LANES)], axis=1)
    return rows[0:2] + rows[2:4]


def slab_kernel(cols, pos, recv, sel, rows, keep, keep_sums, give):
    tiles, length, width = recv.shape
    slab = width - EXT
    half = slab // 2
    ext = recv[:, :, :EXT].reshape(tiles * length, EXT)
    tokens = recv[:, :, EXT:].reshape(tiles * length, slab)
    part = tn(ext, tokens)[:cols]
    sums = jnp.zeros((16, EXT), F32)
    for t in range(tiles):
        sums = sums + nn(sel[...], recv[t, :, :EXT])
    sums = sums[0:2]
    mine = bit_of(pos, 0) == 0
    first = lane_pad(part[:, :half], LANES)
    second = lane_pad(part[:, half:], LANES)
    keep[...] = jnp.where(mine, first, second)
    keep_sums[...] = sums
    other = jnp.where(mine, second, first)
    blocks = [rows[:, b * LANES : (b + 1) * LANES].astype(F32) for b in range(rows.shape[1] // LANES)]
    give[...] = jnp.concatenate([other] + sum_rows(sums) + blocks, axis=0).astype(BF16)


def join_kernel(cols, dates, pos, keep, keep_sums, got, own, send):
    levels = send.shape[0]
    first = bit_of(pos, 0) == 0
    model_d = own.shape[1] - EXT
    total = keep[...] + got[:cols, :].astype(F32)
    sums = sum_rows(keep_sums[...] + rows_sum(got[cols : cols + 24, :].astype(F32)))
    pair_sums = jnp.concatenate([sums[0][:4], sums[1][:4]], axis=0)
    mine, count = own[...].astype(F32), own.shape[0]
    tall = got[cols + 24 :, :].astype(F32)
    theirs = jnp.concatenate([tall[k : k + count] for k in range(0, tall.shape[0], count)], axis=1)
    firsts, seconds = jnp.where(first, mine, theirs), jnp.where(first, theirs, mine)
    lane = lax.broadcasted_iota(jnp.int32, (8, LANES), 1)
    last = pltpu.roll(sums[2], 64, 1)
    for z in range(levels):
        at = z * dates
        rows = jnp.concatenate([firsts[at : at + dates], seconds[at : at + dates]], axis=0)
        ext = [rows[:, model_d + b * LANES : model_d + (b + 1) * LANES] for b in range(EXT // LANES)]
        misc = jnp.where(lane < 64, ext[2], last)
        value = [rows[:, b * LANES : (b + 1) * LANES] for b in range(model_d // LANES)]
        send[z] = jnp.concatenate([total, ext[0], ext[1], misc, pair_sums] + value, axis=0).astype(BF16)


def total_kernel(cols, recv, send, rest):
    levels = recv.shape[0]
    total = recv[0].astype(F32)
    for z in range(1, levels):
        total = total + recv[z].astype(F32)
    slab = total[:cols].astype(BF16)
    for t in range(send.shape[0]):
        send[t] = slab
    rest[...] = total[cols + 16 : cols + 32]


def store_half(cols, scale, core, half, slabs, weight, held, sems):
    copies = []
    for t in range(slabs.shape[0]):
        held[t] = slabs[t].astype(F32)[:cols] * scale
        at = pl.multiple_of((2 * t + core) * half, half)
        copies.append(pltpu.make_async_copy(held.at[t], weight.at[:, pl.ds(at, half)], sems.at[t]))
        copies[-1].start()
    return copies


def half_kernel(cols, scale, half, pos, slabs, weight_in, weight, held, sems):
    for copy in store_half(cols, scale, 1 - bit_of(pos, 0), half, slabs, weight, held, sems):
        copy.wait()


def local_weight_kernel(heads, scale, cols, half, pos, slabs, recv, rest, w_t, *refs):
    outs, held_outs = refs[:5], refs[5:10]
    held, sems, out_sems = held_outs[4], refs[10], refs[11]
    copies = store_half(cols, scale, bit_of(pos, 0), half, slabs, outs[4], held, sems)
    moves = [pltpu.make_async_copy(held_outs[k], outs[k], out_sems.at[k]) for k in range(4)]
    local_kernel(heads, scale, recv, rest, w_t, *held_outs[:4], moves)
    for copy in copies + moves:
        copy.wait()


def write_sums(heads, scale, sums, w, table, head):
    cols = w.shape[0]
    high, low = split(sums[:, :cols])
    table[...] = (nn(high, w) + nn(low, w)) * scale
    both = sums[0:1] + sums[1:2]
    at = cols - heads
    rows = []
    for k in (1, 0, 2):
        lo = at + k * heads
        rows.append(both[:, lo : lo + heads] + both[:, lo + 3 * heads : lo + 4 * heads])
    head[...] = jnp.concatenate(rows, axis=0) * scale


def local_kernel(heads, scale, recv, rest, w_t, value, inputs, table, head, moves=()):
    levels = recv.shape[0]
    model_d = w_t.shape[1]
    cols = w_t.shape[0]
    dates = value.shape[1]
    w = w_t[...]
    ext_rows = []
    for z in range(levels):
        rows = recv[z].astype(F32)
        ext_rows.append(jnp.concatenate([rows[cols + 8 * b : cols + 8 * b + 8] for b in range(3)], axis=1))
        at = cols + 32
        values = jnp.concatenate([rows[at + 8 * b : at + 8 * b + 8] for b in range(model_d // LANES)], axis=1)
        for c in range(2):
            value[2 * z + c] = values[c * dates : (c + 1) * dates].astype(BF16)
    for move in moves[:1]:
        move.start()
    grads = nn(jnp.concatenate(ext_rows, axis=0).astype(BF16)[:, :cols], w)
    for p in range(2 * levels):
        inputs[p] = grads[p * dates : (p + 1) * dates].astype(BF16)
    for move in moves[1:2]:
        move.start()
    last = pltpu.roll(rest[0:8, :], 64, 1)
    sums = jnp.concatenate([rest[8:12, :], rest[12:16, :], last[0:4]], axis=1)
    sums = sums[0:2] + sums[2:4]
    write_sums(heads, scale, sums, w, table, head)
    for move in moves[2:]:
        move.start()


def gather_kernel(cols, half, scale, pos, own, other, out):
    tiles = own.shape[0]
    mine = bit_of(pos, 0) == 0
    for t in range(tiles):
        a = own[t].astype(F32)
        b = other[t].astype(F32)
        first = jnp.where(mine, a, b)[:cols, :half]
        second = jnp.where(mine, b, a)[:cols, :half]
        out[:, 2 * half * t : 2 * half * (t + 1)] = jnp.concatenate([first, second], axis=1) * scale


VMEM = pl.BlockSpec(memory_space=pltpu.VMEM)
SMEM = pl.BlockSpec(memory_space=pltpu.SMEM)
HBM = pl.BlockSpec(memory_space=pltpu.HBM)


def call(kernel, outs, ins, smem=0, scratch=()):
    return pl.pallas_call(
        kernel,
        out_shape=[jax.ShapeDtypeStruct(s, d) for s, d in outs],
        in_specs=[SMEM] * smem + [VMEM] * (len(ins) - smem),
        out_specs=[VMEM] * len(outs),
        scratch_shapes=list(scratch),
        compiler_params=pltpu.CompilerParams(vmem_limit_bytes=48 * 1024 * 1024),
    )(*ins)


def rows_block(rows):
    return [rows[:, b * LANES : (b + 1) * LANES] for b in range(rows.shape[1] // LANES)]


def block_rows(block, count):
    return jnp.concatenate([block[k : k + count] for k in range(0, block.shape[0], count)], axis=1)


def pack_sums(sums):
    high = sums.astype(BF16).astype(F32)
    return jnp.concatenate([high, sums - high], axis=0)


def unpack_sums(rows):
    return rows[:8] + rows[8:16]


def pair_sum(parts):
    return (parts[0] + parts[1]) + (parts[2] + parts[3])


def direct_slab_kernel(pos, *refs):
    parts, (sel, rows, keep, keep_sums, give) = refs[:4], refs[4:]
    cols = keep.shape[0]
    length = sel.shape[1]
    first = bit_of(pos, 0) == 0
    chosen = sel[...]
    tokens, keys, reads, raw_t, sums = [], [], [], [], []
    for part in parts:
        tokens.append(jnp.concatenate([part[:length], part[length : 2 * length]], axis=1))
        keys.append(part[2 * length : 3 * length])
        reads.append(part[3 * length : 4 * length])
        misc = part[4 * length :]
        raw_t.append(misc[:, :length])
        head = misc.astype(F32)[8:10]
        sums.append(
            jnp.concatenate(
                [
                    nn(chosen, keys[-1])[0:2],
                    nn(chosen, reads[-1])[0:2],
                    lane_pad(nt(chosen, raw_t[-1])[0:2], LANES),
                    head[0:1] + head[1:2],
                    jnp.zeros((1, LANES), F32),
                ],
                axis=0,
            )
        )
    tokens = jnp.concatenate(tokens, axis=0)
    slab = jnp.concatenate(
        [
            tn(jnp.concatenate(keys, axis=0), tokens),
            tn(jnp.concatenate(reads, axis=0), tokens),
            nn(jnp.concatenate(raw_t, axis=1), tokens)[: cols - 2 * LANES],
        ],
        axis=0,
    )
    left, right = slab[:, :LANES], slab[:, LANES:]
    keep[...] = jnp.where(first, left, right)
    packed = pack_sums(pair_sum(sums))
    keep_sums[...] = unpack_sums(packed)
    give[...] = jnp.concatenate(
        [jnp.where(first, right, left), packed] + rows_block(rows[...].astype(F32)), axis=0
    ).astype(BF16)


def direct_join_kernel(dates, keep, keep_sums, rows_own, got, rows_keep, own, low, high, both):
    cols = keep.shape[0]
    there = got[...].astype(F32)
    total = keep[...] + there[:cols]
    sums = keep_sums[...] + unpack_sums(there[cols : cols + 16])
    rows = [rows_own[...].astype(F32), block_rows(there[cols + 16 :], rows_own.shape[0])]
    here, low_rows, high_rows, both_rows = (
        jnp.concatenate([part[k * dates : (k + 1) * dates] for part in rows], axis=0) for k in range(4)
    )
    rows_keep[...] = here.astype(BF16)
    common = jnp.concatenate([total, pack_sums(sums)], axis=0).astype(BF16)
    own[...] = common
    for send, part in ((low, low_rows), (high, high_rows), (both, both_rows)):
        send[...] = jnp.concatenate([common] + rows_block(part.astype(BF16)), axis=0)


def direct_total_kernel(own, low, high, both, send, rest):
    cols = send.shape[0]
    total = pair_sum([part[...].astype(F32)[: cols + 16] for part in (own, low, high, both)])
    send[...] = total[:cols].astype(BF16)
    rest[...] = unpack_sums(total[cols:])


def store_slabs(scale, tile, core, slabs, weight, held, sems):
    copies = []
    for k, slab in enumerate(slabs):
        held[k] = slab.astype(F32) * scale
        at = pl.multiple_of((2 * (tile ^ k) + core) * LANES, LANES)
        copies.append(pltpu.make_async_copy(held.at[k], weight.at[:, pl.ds(at, LANES)], sems.at[k]))
        copies[-1].start()
    return copies


def other_slabs_kernel(scale, pos, tile, slabs, weight_in, weight, held, sems):
    parts = [slabs[k] for k in range(slabs.shape[0])]
    for copy in store_slabs(scale, tile[0], 1 - bit_of(pos, 0), parts, weight, held, sems):
        copy.wait()


def final_kernel(heads, scale, pos, tile, slabs, rows_own, low, high, both, rest, w_t, *refs):
    outs, (value, inputs, table, head), (held, sems, out_sems) = refs[:5], refs[5:9], refs[9:]
    model_d, cols, dates = w_t.shape[1], w_t.shape[0], value.shape[1]
    parts = [slabs[k] for k in range(slabs.shape[0])]
    copies = store_slabs(scale, tile[0], bit_of(pos, 0), parts, outs[4], held, sems)
    moves = [
        pltpu.make_async_copy(source, outs[k], out_sems.at[k])
        for k, source in enumerate((value, inputs, table, head))
    ]
    w = w_t[...]
    rows = [rows_own[...].astype(F32)]
    for part in (low, high, both):
        rows.append(block_rows(part[...].astype(F32)[cols + 16 :], 2 * dates))
    rows = jnp.concatenate(rows, axis=0)
    masks = [0, 1, 2, 3, 4, 5, 6, 7]
    for k, mask in enumerate(masks):
        value[pos[0] ^ mask] = rows[k * dates : (k + 1) * dates, :model_d].astype(BF16)
    moves[0].start()
    grads = nn(rows[:, model_d : model_d + EXT].astype(BF16)[:, :cols], w)
    for k, mask in enumerate(masks):
        inputs[pos[0] ^ mask] = grads[k * dates : (k + 1) * dates].astype(BF16)
    moves[1].start()
    sums = jnp.concatenate([rest[0:2, :], rest[2:4, :], rest[4:6, :]], axis=1)[:, :cols]
    parts_high, parts_low = split(sums)
    table[...] = (nn(parts_high, w) + nn(parts_low, w)) * scale
    total = rest[6:7, :]
    head[...] = jnp.concatenate([total[:, k * heads : (k + 1) * heads] for k in (1, 0, 2)], axis=0) * scale
    for move in moves[2:]:
        move.start()
    for copy in copies + moves:
        copy.wait()


def direct_series(operands, w_t, date_s, dates_dev, model_d, axes, across):
    *small, layer, values, cotangent = operands
    arrays = [a.reshape(4, 2, dates_dev, model_d) for a in (layer, values, cotangent)]
    packed = jax.ShapeDtypeStruct((4, dates_dev, 3 * model_d + LANES), BF16)
    heads = small[-1].shape[1]
    keep, give, w_t = pl.pallas_call(
        direct_pack_kernel,
        out_shape=[packed, packed, jax.ShapeDtypeStruct(w_t.shape, w_t.dtype)],
        in_specs=[SMEM] + [HBM] * 10,
        out_specs=[VMEM] * 3,
        scratch_shapes=[
            pltpu.SMEM((dates_dev,), jnp.int32),
            pltpu.VMEM((dates_dev, 8), jnp.int32),
            pltpu.VMEM((2, model_d), F32),
            pltpu.VMEM((3, heads), F32),
            pltpu.VMEM((4, 2, dates_dev, model_d), BF16),
            pltpu.SemaphoreType.DMA((12,)),
        ],
        compiler_params=pltpu.CompilerParams(vmem_limit_bytes=16 * 1024 * 1024),
    )(date_s, *[pltpu.with_memory_space_constraint(operand, pltpu.HBM) for operand in [w_t] + small + arrays])
    got = lax.ppermute(give, axes, across(1))
    levels = call(
        level_rows_kernel, [((2 * dates_dev, 3 * model_d + LANES), BF16)] * 4, [date_s, keep, got], 1
    )
    arrived = {k: lax.ppermute(levels[k], axes, across(2 * k)) for k in (3, 2, 1)}
    return [levels[0]] + [arrived[k] for k in (1, 2, 3)], w_t


def finish_direct(operands, w_t, date_s, tile_s, heads, scale, pixel_dev, dates_dev, tiles, dates):
    length = dates * dates_dev
    cols, model_d = w_t.shape
    wide = model_d + EXT
    half_rows = length // 2
    payload = cols + 16 + half_rows * wide // LANES
    payload_z = cols + 16 + 2 * dates_dev * wide // LANES
    axes = ("tile", "date")

    def across(mask):
        return [(i, i ^ mask) for i in range(tiles * dates)]

    series, w_t = direct_series(operands, w_t, date_s, dates_dev, model_d, axes, across)
    *sends, rows_own, rows_give, sel = call(
        functools.partial(direct_series_kernel, heads, model_d, dates_dev),
        [((4 * length + 16, LANES), BF16)] * tiles
        + [((half_rows, wide), BF16), ((half_rows, wide), BF16), ((16, length), BF16)],
        [date_s, tile_s, *series, w_t],
        2,
        [pltpu.VMEM((length, 3 * model_d + LANES), BF16)],
    )
    parts = {k: lax.ppermute(sends[k], axes, across(dates * k + k % 2)) for k in (3, 2, 1)}
    keep, keep_sums, give = call(
        direct_slab_kernel,
        [((cols, LANES), F32), ((8, LANES), F32), ((payload, LANES), BF16)],
        [date_s, sends[0], parts[1], parts[2], parts[3], sel, rows_give],
        1,
    )
    got = lax.ppermute(give, axes, across(1))
    rows_own, own, *levels = call(
        functools.partial(direct_join_kernel, dates_dev),
        [((2 * dates_dev, wide), BF16), ((cols + 16, LANES), BF16)] + [((payload_z, LANES), BF16)] * 3,
        [keep, keep_sums, rows_own, got],
    )
    arrived = {k: lax.ppermute(levels[k - 1], axes, across(2 * k)) for k in (3, 2, 1)}
    low, high, both = (arrived[k] for k in (1, 2, 3))
    slab, rest = call(
        direct_total_kernel, [((cols, LANES), BF16), ((8, LANES), F32)], [own, low, high, both]
    )
    gathered = {k: lax.ppermute(slab, axes, across(dates * k)) for k in (3, 2, 1)}
    slabs = jnp.stack([slab] + [gathered[k] for k in (1, 2, 3)])
    other_slabs = lax.ppermute(slabs, axes, across(1))
    outs = [
        jax.ShapeDtypeStruct((pixel_dev, dates_dev, model_d), BF16),
        jax.ShapeDtypeStruct((pixel_dev, dates_dev, model_d), BF16),
        jax.ShapeDtypeStruct((2, model_d), F32),
        jax.ShapeDtypeStruct((3, heads), F32),
        jax.ShapeDtypeStruct((cols, model_d), F32),
    ]
    held = [pltpu.VMEM((tiles, cols, LANES), F32), pltpu.SemaphoreType.DMA((tiles,))]
    limit = pltpu.CompilerParams(vmem_limit_bytes=48 * 1024 * 1024)
    value, inputs, table, head, weight_t = pl.pallas_call(
        functools.partial(final_kernel, heads, scale),
        out_shape=outs,
        in_specs=[SMEM] * 2 + [VMEM] * 7,
        out_specs=[HBM] * 5,
        scratch_shapes=[pltpu.VMEM(o.shape, o.dtype) for o in outs[:4]]
        + held
        + [pltpu.SemaphoreType.DMA((4,))],
        compiler_params=limit,
    )(date_s, tile_s, slabs, rows_own, low, high, both, rest, w_t)
    weight_t = pl.pallas_call(
        functools.partial(other_slabs_kernel, scale),
        out_shape=outs[4],
        in_specs=[SMEM, SMEM, VMEM, HBM],
        out_specs=HBM,
        scratch_shapes=held,
        input_output_aliases={3: 0},
        compiler_params=limit,
    )(date_s, tile_s, other_slabs, weight_t)
    return value, inputs, weight_t.T, table, head


def finish_any(series, w_t, date_s, tile_s, heads, scale, pixel_dev, dates_dev, tiles, dates):
    length = series.shape[0]
    cols, model_d = w_t.shape
    levels = dates // 2
    slab = model_d // tiles
    half = slab // 2
    swap = [(i, i ^ 1) for i in range(dates)]
    planes = [[2 * z + c for z in range(levels)] for c in range(2)]
    rows_core = length // 2
    send_t, own, give_rows, sel = call(
        functools.partial(series_kernel, heads, model_d, 0, dates_dev),
        [
            ((tiles, length, EXT + slab), BF16),
            ((rows_core, model_d + EXT), BF16),
            ((rows_core, model_d + EXT), BF16),
            ((16, length), BF16),
        ],
        [date_s, series, w_t],
        1,
    )
    mixed = [
        [t * dates + 2 * z + (c + t) % 2 for t in range(tiles)] for z in range(levels) for c in range(2)
    ]
    recv_t = lax.all_to_all(
        send_t, ("tile", "date"), split_axis=0, concat_axis=0, tiled=True, axis_index_groups=mixed
    )
    rows_give = cols + 24 + rows_core * (model_d + EXT) // LANES
    keep, keep_sums, give = call(
        functools.partial(slab_kernel, cols),
        [((cols, LANES), F32), ((2, EXT), F32), ((rows_give, LANES), BF16)],
        [date_s, recv_t, sel, give_rows],
        1,
    )
    got = lax.ppermute(give, "date", swap)
    rows_z = cols + 32 + model_d // 16
    (send_z,) = call(
        functools.partial(join_kernel, cols, dates_dev),
        [((levels, rows_z, LANES), BF16)],
        [date_s, keep, keep_sums, got, own],
        1,
    )
    recv_z = lax.all_to_all(
        send_z, "date", split_axis=0, concat_axis=0, tiled=True, axis_index_groups=planes
    )
    send_g, rest = call(
        functools.partial(total_kernel, cols),
        [((tiles, cols, LANES), BF16), ((16, LANES), F32)],
        [recv_z],
    )
    recv_g = lax.all_to_all(send_g, "tile", split_axis=0, concat_axis=0, tiled=True)
    local_outs = [
        ((pixel_dev, dates_dev, model_d), BF16),
        ((pixel_dev, dates_dev, model_d), BF16),
        ((2, model_d), F32),
        ((3, heads), F32),
    ]
    other_g = lax.ppermute(recv_g, "date", swap)
    if half % LANES == 0:
        weight_shape = jax.ShapeDtypeStruct((cols, model_d), F32)
        held = [pltpu.VMEM((tiles, cols, half), F32), pltpu.SemaphoreType.DMA((tiles,))]
        limit = pltpu.CompilerParams(vmem_limit_bytes=48 * 1024 * 1024)
        value, inputs, table, head, weight_t = pl.pallas_call(
            functools.partial(local_weight_kernel, heads, scale, cols, half),
            out_shape=[jax.ShapeDtypeStruct(s, d) for s, d in local_outs] + [weight_shape],
            in_specs=[SMEM] + [VMEM] * 4,
            out_specs=[HBM] * 5,
            scratch_shapes=[pltpu.VMEM(s, d) for s, d in local_outs]
            + held
            + [pltpu.SemaphoreType.DMA((4,))],
            compiler_params=limit,
        )(date_s, recv_g, recv_z, rest, w_t)
        weight_t = pl.pallas_call(
            functools.partial(half_kernel, cols, scale, half),
            out_shape=weight_shape,
            in_specs=[SMEM, VMEM, HBM],
            out_specs=HBM,
            scratch_shapes=held,
            input_output_aliases={2: 0},
            compiler_params=limit,
        )(date_s, other_g, weight_t)
    else:
        value, inputs, table, head = call(
            functools.partial(local_kernel, heads, scale), local_outs, [recv_z, rest, w_t]
        )
        (weight_t,) = call(
            functools.partial(gather_kernel, cols, half, scale),
            [((cols, model_d), F32)],
            [date_s, recv_g, other_g],
            1,
        )
    return (
        value,
        inputs,
        weight_t.T,
        table,
        head,
    )


def on_device(
    layer_input,
    head_input,
    out_grad,
    sensor_ids,
    valid_mask,
    sensor_table,
    proj_weight,
    step_bias,
    decay_log,
    skip_gain,
):
    pixel_dev, dates_dev, model_d = layer_input.shape
    heads = step_bias.shape[0]
    tiles = lax.axis_size("tile")
    dates = lax.axis_size("date")
    assert pixel_dev == dates and dates % 2 == 0
    levels = dates // 2
    length = dates * dates_dev
    slab = model_d // tiles
    half = slab // 2
    date_s = lax.axis_index("date").astype(jnp.int32).reshape(1)
    tile_s = lax.axis_index("tile").astype(jnp.int32).reshape(1)
    w_t = proj_weight.T
    scale = 1.0 / math.sqrt(pixel_dev * dates_dev * tiles * dates)

    operands = [
        sensor_ids,
        valid_mask.T,
        sensor_table,
        step_bias[None],
        decay_log[None],
        skip_gain[None],
        layer_input,
        head_input,
        out_grad,
    ]
    if levels == 4 and tiles == 4 and model_d == 2 * LANES * tiles:
        return finish_direct(operands, w_t, date_s, tile_s, heads, scale, pixel_dev, dates_dev, tiles, dates)
    packed = pl.pallas_call(
        pack_kernel,
        out_shape=jax.ShapeDtypeStruct((pixel_dev, dates_dev, 3 * model_d + LANES), BF16),
        in_specs=[SMEM] * 2 + [HBM] * 9,
        out_specs=VMEM,
        scratch_shapes=[
            pltpu.SMEM((dates_dev,), jnp.int32),
            pltpu.VMEM((dates_dev, pixel_dev), jnp.int32),
            pltpu.VMEM((2, model_d), F32),
            pltpu.VMEM((3, heads), F32),
            pltpu.VMEM((pixel_dev, dates_dev, model_d), BF16),
            pltpu.SemaphoreType.DMA((9,)),
        ],
        compiler_params=pltpu.CompilerParams(vmem_limit_bytes=16 * 1024 * 1024),
    )(date_s, tile_s, *[pltpu.with_memory_space_constraint(operand, pltpu.HBM) for operand in operands])
    series = lax.all_to_all(packed, "date", split_axis=0, concat_axis=0, tiled=True).reshape(
        length, 3 * model_d + LANES
    )

    return finish_any(series, w_t, date_s, tile_s, heads, scale, pixel_dev, dates_dev, tiles, dates)


def solution(mesh):
    in_specs = (
        P("tile", "date", None),
        P("tile", "date", None),
        P("tile", "date", None),
        P("date"),
        P("tile", "date"),
        P(),
        P(),
        P(),
        P(),
        P(),
    )
    out_specs = (P("tile", "date", None), P("tile", "date", None), P(), P(), P())
    return jax.shard_map(
        on_device, mesh=mesh, in_specs=in_specs, out_specs=out_specs, check_vma=False
    )
```

```python
import functools
import math

import jax
import jax.numpy as jnp
from jax import lax
from jax.experimental import pallas as pl
from jax.experimental.pallas import tpu as pltpu
from jax.sharding import PartitionSpec as P

NEG_FILL = -1e30
HIGHEST_PREC = lax.Precision.HIGHEST
F32 = jnp.float32
BF16 = jnp.bfloat16
LANES = 128
EXT = 384


def nt(a, b, precision=None):
    return lax.dot_general(
        a, b, (((1,), (1,)), ((), ())), preferred_element_type=F32, precision=precision
    )


def nn(a, b, precision=None):
    return lax.dot_general(
        a, b, (((1,), (0,)), ((), ())), preferred_element_type=F32, precision=precision
    )


def tn(a, b):
    return lax.dot_general(a, b, (((0,), (0,)), ((), ())), preferred_element_type=F32)


def split(x):
    high = x.astype(BF16)
    return high, (x - high.astype(F32)).astype(BF16)


def bit_of(pos, bit):
    return lax.rem(lax.div(pos[0], 2**bit), 2)


def halves(arrays, span, first):
    kept, given = [], []
    for array in arrays:
        for at in range(0, array.shape[0], 2 * span):
            a, b = array[at : at + span], array[at + span : at + 2 * span]
            kept.append(jnp.where(first, a, b))
            given.append(jnp.where(first, b, a))
    return jnp.concatenate(kept, axis=0), jnp.concatenate(given, axis=0)


def series_terms(heads, model_d, recv, w_t, order=0):
    length = recv.shape[0]
    width_p = model_d // heads
    states = (w_t.shape[0] - heads) // 2
    mixed = recv[:, :model_d]
    aux = recv[:, 3 * model_d :].astype(F32)
    gate = aux[:, 0:1]
    ids = aux[:, 1:2]
    params = []
    for at in range(2, 2 + 9 * heads, 3 * heads):
        params.append(sum(aux[0:1, at + k * heads : at + (k + 1) * heads] for k in range(3)))
    bias, rate, skip = params[0], -jnp.exp(params[1]), params[2]
    projected = nt(mixed, w_t[...])
    keys = projected[:, :states].astype(BF16)
    reads = projected[:, states : 2 * states].astype(BF16)
    step_pre = projected[:, 2 * states :] + bias
    softplus = jnp.maximum(step_pre, 0.0) + jnp.log1p(jnp.exp(-jnp.abs(step_pre)))
    steps_b = (gate * softplus).astype(BF16)
    steps = steps_b.astype(F32)

    row = lax.broadcasted_iota(jnp.int32, (length, length), 0)
    col = lax.broadcasted_iota(jnp.int32, (length, length), 1)
    upper = (col ^ order) >= (row ^ order)
    upper_f = upper.astype(F32)
    eye = (col == row).astype(F32)
    lower_b = ((row ^ order) >= (col ^ order)).astype(BF16)
    head_row = lax.broadcasted_iota(jnp.int32, (heads, heads), 0)
    head_col = lax.broadcasted_iota(jnp.int32, (heads, heads), 1)
    eye_h = (head_row == head_col).astype(F32)
    rate_col = jnp.sum(eye_h * rate, axis=1, keepdims=True)
    log_col = nn(lower_b, steps_b) * rate
    steps_t = nt(eye_h.astype(BF16), steps_b).astype(BF16)
    log_row = nn(steps_t, upper.astype(BF16)) * rate_col
    scores_t = nt(keys, reads)

    pair_t = jnp.zeros((length, length), F32)
    mixes, weighted_cols, read_rows, skip_cols = [], [], [], []
    for h in range(heads):
        lo = model_d + h * width_p
        x_h = recv[:, lo : lo + width_p]
        g_h = recv[:, lo + model_d : lo + model_d + width_p]
        dt_h = steps[:, h : h + 1]
        gap = log_row[h : h + 1, :] - log_col[:, h : h + 1]
        decay = jnp.exp(jnp.where(upper, gap, NEG_FILL))
        cross = nt(x_h, g_h)
        mix = decay * scores_t
        pair_t = pair_t + decay * cross * dt_h
        both = mix * cross
        weighted = jnp.sum(both, axis=1, keepdims=True)
        weighted_cols.append(weighted)
        read_rows.append(jnp.sum(both * dt_h, axis=0, keepdims=True))
        skip_cols.append(jnp.sum(cross * eye, axis=1, keepdims=True))
        mixes.append((mix.astype(BF16), g_h, dt_h, skip[:, h : h + 1]))

    weighted = jnp.concatenate(weighted_cols, axis=1)
    read_sum = jnp.concatenate(read_rows, axis=0)
    skip_terms = jnp.concatenate(skip_cols, axis=1)
    later = nt(upper_f, read_sum, HIGHEST_PREC) - nn(upper_f, steps * weighted, HIGHEST_PREC)
    step_grad = (weighted + rate * later).astype(BF16).astype(F32)
    decay_terms = steps * later * rate
    pair_b = pair_t.astype(BF16)
    grad_keys = nn(pair_b, reads)
    grad_reads = tn(pair_b, keys)
    raw = step_grad * gate * jax.nn.sigmoid(step_pre)
    terms = jnp.concatenate(
        [raw, decay_terms, skip_terms, jnp.zeros((length, LANES - 3 * heads), F32)], axis=1
    )
    ids_row = jnp.sum(eye * ids, axis=0, keepdims=True)
    return mixes, grad_keys, grad_reads, raw, terms, ids_row, eye_h


def value_columns(mixes):
    return [nn(mix, g_h) * dt_h + skip_h * g_h.astype(F32) for mix, g_h, dt_h, skip_h in mixes]


def sensor_rows(ids_row):
    zeros = jnp.zeros((14, ids_row.shape[1]), F32)
    return jnp.concatenate([1.0 - ids_row, ids_row, zeros], axis=0).astype(BF16)


def series_kernel(heads, model_d, bit, span, pos, recv, w_t, send, own, give, sel):
    tiles, _, width = send.shape
    slab = width - EXT
    mixes, grad_keys, grad_reads, _, terms, ids_row, _ = series_terms(heads, model_d, recv, w_t)
    high = terms.astype(BF16).astype(F32)
    tail = high + pltpu.roll(terms - high, 3 * heads, 1)
    ext_f = jnp.concatenate([grad_keys, grad_reads, tail], axis=1)
    ext = ext_f.astype(BF16)
    back = jnp.concatenate(value_columns(mixes) + [ext_f], axis=1)
    kept, given = halves([back], span, bit_of(pos, bit) == 0)
    own[...] = kept.astype(BF16)
    give[...] = given.astype(BF16)
    for t in range(tiles):
        send[t, :, :EXT] = ext
        send[t, :, EXT:] = recv[:, t * slab : (t + 1) * slab]
    sel[...] = sensor_rows(ids_row)


def direct_series_kernel(heads, model_d, dates, pos, tile, *refs):
    levels, w_t, sends, (own, give, sel, recv) = refs[:4], refs[4], refs[5:-4], refs[-4:]
    levels = tuple(levels[k] for k in (0, 2, 1, 3))
    length = recv.shape[0]
    slab = 2 * LANES
    recv[...] = jnp.concatenate([level[...].astype(F32) for level in levels], axis=0).astype(BF16)
    order = lax.div(pos[0], 2) * (2 * dates)
    mixes, grad_keys, grad_reads, raw, terms, ids_row, eye_h = series_terms(heads, model_d, recv, w_t, order)
    raw_t = nt(eye_h.astype(BF16), raw.astype(BF16))
    total = jnp.sum(terms, axis=0, keepdims=True)
    high = total.astype(BF16).astype(F32)
    misc = jnp.concatenate(
        [lane_pad(raw_t, LANES), high, total - high, jnp.zeros((6, LANES), F32)], axis=0
    )
    grads = jnp.concatenate([grad_keys, grad_reads, misc], axis=0).astype(BF16)
    for k, send in enumerate(sends):
        for block in range(2):
            at = pl.multiple_of((tile[0] ^ k) * slab + block * LANES, LANES)
            send[block * length : (block + 1) * length] = recv[:, pl.ds(at, LANES)]
        send[2 * length :] = grads
    back = jnp.concatenate(value_columns(mixes) + [grad_keys, grad_reads, lane_pad(raw, LANES)], axis=1)
    kept, given = halves([back], dates, bit_of(pos, 0) == 0)
    own[...] = kept.astype(BF16)
    give[...] = given.astype(BF16)
    sel[...] = sensor_rows(ids_row)


def shared_rows(dates, ids, table, params):
    rows = [jnp.where(ids[i] == 1, table[1:2, :], table[0:1, :]) for i in range(dates)]
    embed = jnp.concatenate(rows, axis=0)
    row = lax.broadcasted_iota(jnp.int32, (dates, LANES), 0)
    lane = lax.broadcasted_iota(jnp.int32, (dates, LANES), 1)
    second = jnp.zeros((dates, LANES), F32)
    for i in range(dates):
        second = jnp.where((row == i) & (lane == 1), (ids[i] == 1).astype(F32), second)
    at = 2
    for k in range(3):
        rest = params[k : k + 1, :]
        for _ in range(3):
            term = rest.astype(BF16).astype(F32)
            rest = rest - term
            term = jnp.concatenate([jnp.zeros((1, at), F32), term, jnp.zeros((1, LANES - at - term.shape[1]), F32)], axis=1)
            second = second + term
            at = at + params.shape[1]
    return embed, second


def pack_kernel(pos, tile, ids_in, mask_in, table_in, bias_in, decay_in, skip_in, layer, values, cotangent, out, ids, mask_t, table, params, layer_v, sems):
    pixels, dates, model_d = layer.shape
    small = [
        pltpu.make_async_copy(ids_in, ids, sems.at[0]),
        pltpu.make_async_copy(mask_in, mask_t, sems.at[1]),
        pltpu.make_async_copy(table_in, table, sems.at[2]),
        pltpu.make_async_copy(layer, layer_v, sems.at[3]),
        pltpu.make_async_copy(bias_in, params.at[0:1], sems.at[6]),
        pltpu.make_async_copy(decay_in, params.at[1:2], sems.at[7]),
        pltpu.make_async_copy(skip_in, params.at[2:3], sems.at[8]),
    ]
    large = [
        pltpu.make_async_copy(values, out.at[:, :, model_d : 2 * model_d], sems.at[4]),
        pltpu.make_async_copy(cotangent, out.at[:, :, 2 * model_d : 3 * model_d], sems.at[5]),
    ]
    for copy in small[3:4] + large + small[:3] + small[4:]:
        copy.start()
    for copy in small:
        copy.wait()
    embed, second = shared_rows(dates, ids, table, params)
    lane = lax.broadcasted_iota(jnp.int32, (dates, LANES), 1)
    gate = mask_t[...].astype(F32)
    for p in range(pixels):
        out[p, :, 3 * model_d :] = jnp.where(lane == 0, gate[:, p : p + 1], second).astype(BF16)
        out[p, :, :model_d] = (layer_v[p].astype(F32) + embed).astype(BF16)
    for copy in large:
        copy.wait()


def direct_pack_kernel(
    pos, w_in, ids_in, mask_in, table_in, bias_in, decay_in, skip_in, layer, values, cotangent, keep, give, w_t, *scratch
):
    ids, mask_t, table, params, layer_v, sems = scratch
    levels, _, dates, model_d = layer.shape
    core = bit_of(pos, 0)
    small = [
        pltpu.make_async_copy(ids_in, ids, sems.at[0]),
        pltpu.make_async_copy(mask_in, mask_t, sems.at[1]),
        pltpu.make_async_copy(table_in, table, sems.at[2]),
        pltpu.make_async_copy(bias_in, params.at[0:1], sems.at[3]),
        pltpu.make_async_copy(decay_in, params.at[1:2], sems.at[4]),
        pltpu.make_async_copy(skip_in, params.at[2:3], sems.at[5]),
        pltpu.make_async_copy(layer, layer_v, sems.at[6]),
    ]
    large = [pltpu.make_async_copy(w_in, w_t, sems.at[11])]
    for k, array in enumerate((values, cotangent)):
        to = slice((k + 1) * model_d, (k + 2) * model_d)
        large.append(pltpu.make_async_copy(array.at[:, core], keep.at[:, :, to], sems.at[7 + k]))
        large.append(pltpu.make_async_copy(array.at[:, 1 - core], give.at[:, :, to], sems.at[9 + k]))
    for copy in small[-1:] + large[1:] + small[:-1] + large[:1]:
        copy.start()
    for copy in small:
        copy.wait()
    embed, extra = shared_rows(dates, ids, table, params)
    lane = lax.broadcasted_iota(jnp.int32, (dates, LANES), 1)
    gate = mask_t[...].astype(F32)
    first = core == 0
    for level in range(levels):
        gates = [gate[:, 2 * level + c : 2 * level + c + 1] for c in range(2)]
        mixed = [layer_v[level, c].astype(F32) + embed for c in range(2)]
        for out, mine in ((keep, first), (give, jnp.logical_not(first))):
            chosen = jnp.where(mine, gates[0], gates[1])
            out[level, :, 3 * model_d :] = jnp.where(lane == 0, chosen, extra).astype(BF16)
            out[level, :, :model_d] = jnp.where(mine, mixed[0], mixed[1]).astype(BF16)
    for copy in large:
        copy.wait()


def level_rows_kernel(pos, keep, got, *outs):
    first = bit_of(pos, 0) == 0
    level = lax.div(pos[0], 2)
    for k, out in enumerate(outs):
        mine, theirs = keep[level ^ k].astype(F32), got[level ^ k].astype(F32)
        out[...] = jnp.concatenate(
            [jnp.where(first, mine, theirs), jnp.where(first, theirs, mine)], axis=0
        ).astype(BF16)


def lane_pad(x, width):
    if x.shape[1] == width:
        return x
    return jnp.concatenate([x, jnp.zeros((x.shape[0], width - x.shape[1]), x.dtype)], axis=1)


def sum_rows(sums):
    high = sums.astype(BF16).astype(F32)
    low = (sums - high).astype(BF16).astype(F32)
    rows = jnp.concatenate([high, low, jnp.zeros((4, EXT), F32)], axis=0)
    return [rows[:, b * LANES : (b + 1) * LANES] for b in range(EXT // LANES)]


def rows_sum(block):
    rows = jnp.concatenate([block[8 * b : 8 * b + 8, :] for b in range(EXT // LANES)], axis=1)
    return rows[0:2] + rows[2:4]


def slab_kernel(cols, pos, recv, sel, rows, keep, keep_sums, give):
    tiles, length, width = recv.shape
    slab = width - EXT
    half = slab // 2
    ext = recv[:, :, :EXT].reshape(tiles * length, EXT)
    tokens = recv[:, :, EXT:].reshape(tiles * length, slab)
    part = tn(ext, tokens)[:cols]
    sums = jnp.zeros((16, EXT), F32)
    for t in range(tiles):
        sums = sums + nn(sel[...], recv[t, :, :EXT])
    sums = sums[0:2]
    mine = bit_of(pos, 0) == 0
    first = lane_pad(part[:, :half], LANES)
    second = lane_pad(part[:, half:], LANES)
    keep[...] = jnp.where(mine, first, second)
    keep_sums[...] = sums
    other = jnp.where(mine, second, first)
    blocks = [rows[:, b * LANES : (b + 1) * LANES].astype(F32) for b in range(rows.shape[1] // LANES)]
    give[...] = jnp.concatenate([other] + sum_rows(sums) + blocks, axis=0).astype(BF16)


def join_kernel(cols, dates, pos, keep, keep_sums, got, own, send):
    levels = send.shape[0]
    first = bit_of(pos, 0) == 0
    model_d = own.shape[1] - EXT
    total = keep[...] + got[:cols, :].astype(F32)
    sums = sum_rows(keep_sums[...] + rows_sum(got[cols : cols + 24, :].astype(F32)))
    pair_sums = jnp.concatenate([sums[0][:4], sums[1][:4]], axis=0)
    mine, count = own[...].astype(F32), own.shape[0]
    tall = got[cols + 24 :, :].astype(F32)
    theirs = jnp.concatenate([tall[k : k + count] for k in range(0, tall.shape[0], count)], axis=1)
    firsts, seconds = jnp.where(first, mine, theirs), jnp.where(first, theirs, mine)
    lane = lax.broadcasted_iota(jnp.int32, (8, LANES), 1)
    last = pltpu.roll(sums[2], 64, 1)
    for z in range(levels):
        at = z * dates
        rows = jnp.concatenate([firsts[at : at + dates], seconds[at : at + dates]], axis=0)
        ext = [rows[:, model_d + b * LANES : model_d + (b + 1) * LANES] for b in range(EXT // LANES)]
        misc = jnp.where(lane < 64, ext[2], last)
        value = [rows[:, b * LANES : (b + 1) * LANES] for b in range(model_d // LANES)]
        send[z] = jnp.concatenate([total, ext[0], ext[1], misc, pair_sums] + value, axis=0).astype(BF16)


def total_kernel(cols, recv, send, rest):
    levels = recv.shape[0]
    total = recv[0].astype(F32)
    for z in range(1, levels):
        total = total + recv[z].astype(F32)
    slab = total[:cols].astype(BF16)
    for t in range(send.shape[0]):
        send[t] = slab
    rest[...] = total[cols + 16 : cols + 32]


def store_half(cols, scale, core, half, slabs, weight, held, sems):
    copies = []
    for t in range(slabs.shape[0]):
        held[t] = slabs[t].astype(F32)[:cols] * scale
        at = pl.multiple_of((2 * t + core) * half, half)
        copies.append(pltpu.make_async_copy(held.at[t], weight.at[:, pl.ds(at, half)], sems.at[t]))
        copies[-1].start()
    return copies


def half_kernel(cols, scale, half, pos, slabs, weight_in, weight, held, sems):
    for copy in store_half(cols, scale, 1 - bit_of(pos, 0), half, slabs, weight, held, sems):
        copy.wait()


def local_weight_kernel(heads, scale, cols, half, pos, slabs, recv, rest, w_t, *refs):
    outs, held_outs = refs[:5], refs[5:10]
    held, sems, out_sems = held_outs[4], refs[10], refs[11]
    copies = store_half(cols, scale, bit_of(pos, 0), half, slabs, outs[4], held, sems)
    moves = [pltpu.make_async_copy(held_outs[k], outs[k], out_sems.at[k]) for k in range(4)]
    local_kernel(heads, scale, recv, rest, w_t, *held_outs[:4], moves)
    for copy in copies + moves:
        copy.wait()


def write_sums(heads, scale, sums, w, table, head):
    cols = w.shape[0]
    high, low = split(sums[:, :cols])
    table[...] = (nn(high, w) + nn(low, w)) * scale
    both = sums[0:1] + sums[1:2]
    at = cols - heads
    rows = []
    for k in (1, 0, 2):
        lo = at + k * heads
        rows.append(both[:, lo : lo + heads] + both[:, lo + 3 * heads : lo + 4 * heads])
    head[...] = jnp.concatenate(rows, axis=0) * scale


def local_kernel(heads, scale, recv, rest, w_t, value, inputs, table, head, moves=()):
    levels = recv.shape[0]
    model_d = w_t.shape[1]
    cols = w_t.shape[0]
    dates = value.shape[1]
    w = w_t[...]
    ext_rows = []
    for z in range(levels):
        rows = recv[z].astype(F32)
        ext_rows.append(jnp.concatenate([rows[cols + 8 * b : cols + 8 * b + 8] for b in range(3)], axis=1))
        at = cols + 32
        values = jnp.concatenate([rows[at + 8 * b : at + 8 * b + 8] for b in range(model_d // LANES)], axis=1)
        for c in range(2):
            value[2 * z + c] = values[c * dates : (c + 1) * dates].astype(BF16)
    for move in moves[:1]:
        move.start()
    grads = nn(jnp.concatenate(ext_rows, axis=0).astype(BF16)[:, :cols], w)
    for p in range(2 * levels):
        inputs[p] = grads[p * dates : (p + 1) * dates].astype(BF16)
    for move in moves[1:2]:
        move.start()
    last = pltpu.roll(rest[0:8, :], 64, 1)
    sums = jnp.concatenate([rest[8:12, :], rest[12:16, :], last[0:4]], axis=1)
    sums = sums[0:2] + sums[2:4]
    write_sums(heads, scale, sums, w, table, head)
    for move in moves[2:]:
        move.start()


def gather_kernel(cols, half, scale, pos, own, other, out):
    tiles = own.shape[0]
    mine = bit_of(pos, 0) == 0
    for t in range(tiles):
        a = own[t].astype(F32)
        b = other[t].astype(F32)
        first = jnp.where(mine, a, b)[:cols, :half]
        second = jnp.where(mine, b, a)[:cols, :half]
        out[:, 2 * half * t : 2 * half * (t + 1)] = jnp.concatenate([first, second], axis=1) * scale


VMEM = pl.BlockSpec(memory_space=pltpu.VMEM)
SMEM = pl.BlockSpec(memory_space=pltpu.SMEM)
HBM = pl.BlockSpec(memory_space=pltpu.HBM)


def call(kernel, outs, ins, smem=0, scratch=()):
    return pl.pallas_call(
        kernel,
        out_shape=[jax.ShapeDtypeStruct(s, d) for s, d in outs],
        in_specs=[SMEM] * smem + [VMEM] * (len(ins) - smem),
        out_specs=[VMEM] * len(outs),
        scratch_shapes=list(scratch),
        compiler_params=pltpu.CompilerParams(vmem_limit_bytes=48 * 1024 * 1024),
    )(*ins)


def rows_block(rows):
    return [rows[:, b * LANES : (b + 1) * LANES] for b in range(rows.shape[1] // LANES)]


def block_rows(block, count):
    return jnp.concatenate([block[k : k + count] for k in range(0, block.shape[0], count)], axis=1)


def pack_sums(sums):
    high = sums.astype(BF16).astype(F32)
    return jnp.concatenate([high, sums - high], axis=0)


def unpack_sums(rows):
    return rows[:8] + rows[8:16]


def pair_sum(parts):
    return (parts[0] + parts[1]) + (parts[2] + parts[3])


def direct_slab_kernel(pos, *refs):
    parts, (sel, rows, keep, keep_sums, give) = refs[:4], refs[4:]
    parts = (parts[0], parts[3], parts[2], parts[1])
    cols = keep.shape[0]
    length = sel.shape[1]
    first = bit_of(pos, 0) == 0
    chosen = sel[...]
    tokens, keys, reads, raw_t, sums = [], [], [], [], []
    for part in parts:
        tokens.append(jnp.concatenate([part[:length], part[length : 2 * length]], axis=1))
        keys.append(part[2 * length : 3 * length])
        reads.append(part[3 * length : 4 * length])
        misc = part[4 * length :]
        raw_t.append(misc[:, :length])
        head = misc.astype(F32)[8:10]
        sums.append(
            jnp.concatenate(
                [
                    nn(chosen, keys[-1])[0:2],
                    nn(chosen, reads[-1])[0:2],
                    lane_pad(nt(chosen, raw_t[-1])[0:2], LANES),
                    head[0:1] + head[1:2],
                    jnp.zeros((1, LANES), F32),
                ],
                axis=0,
            )
        )
    tokens = jnp.concatenate(tokens, axis=0)
    slab = jnp.concatenate(
        [
            tn(jnp.concatenate(keys, axis=0), tokens),
            tn(jnp.concatenate(reads, axis=0), tokens),
            nn(jnp.concatenate(raw_t, axis=1), tokens)[: cols - 2 * LANES],
        ],
        axis=0,
    )
    left, right = slab[:, :LANES], slab[:, LANES:]
    keep[...] = jnp.where(first, left, right)
    packed = pack_sums(pair_sum(sums))
    keep_sums[...] = unpack_sums(packed)
    give[...] = jnp.concatenate(
        [jnp.where(first, right, left), packed] + rows_block(rows[...].astype(F32)), axis=0
    ).astype(BF16)


def direct_join_kernel(dates, keep, keep_sums, rows_own, got, rows_keep, own, low, high, both):
    cols = keep.shape[0]
    there = got[...].astype(F32)
    total = keep[...] + there[:cols]
    sums = keep_sums[...] + unpack_sums(there[cols : cols + 16])
    rows = [rows_own[...].astype(F32), block_rows(there[cols + 16 :], rows_own.shape[0])]
    here, low_rows, high_rows, both_rows = (
        jnp.concatenate([part[k * dates : (k + 1) * dates] for part in rows], axis=0) for k in range(4)
    )
    rows_keep[...] = here.astype(BF16)
    common = jnp.concatenate([total, pack_sums(sums)], axis=0).astype(BF16)
    own[...] = common
    for send, part in ((low, low_rows), (high, high_rows), (both, both_rows)):
        send[...] = jnp.concatenate([common] + rows_block(part.astype(BF16)), axis=0)


def direct_total_kernel(own, low, both, high, send, rest):
    cols = send.shape[0]
    total = pair_sum([part[...].astype(F32)[: cols + 16] for part in (own, low, high, both)])
    send[...] = total[:cols].astype(BF16)
    rest[...] = unpack_sums(total[cols:])


def store_slabs(scale, tile, core, slabs, weight, held, sems):
    copies = []
    for k, slab in enumerate(slabs):
        held[k] = slab.astype(F32) * scale
        at = pl.multiple_of((2 * (tile ^ k) + core) * LANES, LANES)
        copies.append(pltpu.make_async_copy(held.at[k], weight.at[:, pl.ds(at, LANES)], sems.at[k]))
        copies[-1].start()
    return copies


def other_slabs_kernel(scale, pos, tile, slabs, weight_in, weight, held, sems):
    parts = [slabs[k] for k in range(slabs.shape[0])]
    for copy in store_slabs(scale, tile[0], 1 - bit_of(pos, 0), parts, weight, held, sems):
        copy.wait()


def final_kernel(heads, scale, pos, tile, slabs, rows_own, low, high, both, rest, w_t, *refs):
    outs, (value, inputs, table, head), (held, sems, out_sems) = refs[:5], refs[5:9], refs[9:]
    model_d, cols, dates = w_t.shape[1], w_t.shape[0], value.shape[1]
    parts = [slabs[k] for k in range(slabs.shape[0])]
    copies = store_slabs(scale, tile[0], bit_of(pos, 0), parts, outs[4], held, sems)
    moves = [
        pltpu.make_async_copy(source, outs[k], out_sems.at[k])
        for k, source in enumerate((value, inputs, table, head))
    ]
    w = w_t[...]
    rows = [rows_own[...].astype(F32)]
    for part in (low, high, both):
        rows.append(block_rows(part[...].astype(F32)[cols + 16 :], 2 * dates))
    rows = jnp.concatenate(rows, axis=0)
    masks = [0, 1, 2, 3, 4, 5, 6, 7]
    for k, mask in enumerate(masks):
        value[pos[0] ^ mask] = rows[k * dates : (k + 1) * dates, :model_d].astype(BF16)
    moves[0].start()
    grads = nn(rows[:, model_d : model_d + EXT].astype(BF16)[:, :cols], w)
    for k, mask in enumerate(masks):
        inputs[pos[0] ^ mask] = grads[k * dates : (k + 1) * dates].astype(BF16)
    moves[1].start()
    sums = jnp.concatenate([rest[0:2, :], rest[2:4, :], rest[4:6, :]], axis=1)[:, :cols]
    parts_high, parts_low = split(sums)
    table[...] = (nn(parts_high, w) + nn(parts_low, w)) * scale
    total = rest[6:7, :]
    head[...] = jnp.concatenate([total[:, k * heads : (k + 1) * heads] for k in (1, 0, 2)], axis=0) * scale
    for move in moves[2:]:
        move.start()
    for copy in copies + moves:
        copy.wait()


def direct_series(operands, w_t, date_s, dates_dev, model_d, axes, across):
    *small, layer, values, cotangent = operands
    arrays = [a.reshape(4, 2, dates_dev, model_d) for a in (layer, values, cotangent)]
    packed = jax.ShapeDtypeStruct((4, dates_dev, 3 * model_d + LANES), BF16)
    heads = small[-1].shape[1]
    keep, give, w_t = pl.pallas_call(
        direct_pack_kernel,
        out_shape=[packed, packed, jax.ShapeDtypeStruct(w_t.shape, w_t.dtype)],
        in_specs=[SMEM] + [HBM] * 10,
        out_specs=[VMEM] * 3,
        scratch_shapes=[
            pltpu.SMEM((dates_dev,), jnp.int32),
            pltpu.VMEM((dates_dev, 8), jnp.int32),
            pltpu.VMEM((2, model_d), F32),
            pltpu.VMEM((3, heads), F32),
            pltpu.VMEM((4, 2, dates_dev, model_d), BF16),
            pltpu.SemaphoreType.DMA((12,)),
        ],
        compiler_params=pltpu.CompilerParams(vmem_limit_bytes=16 * 1024 * 1024),
    )(date_s, *[pltpu.with_memory_space_constraint(operand, pltpu.HBM) for operand in [w_t] + small + arrays])
    got = lax.ppermute(give, axes, across(1))
    levels = call(
        level_rows_kernel, [((2 * dates_dev, 3 * model_d + LANES), BF16)] * 4, [date_s, keep, got], 1
    )
    arrived = {k: lax.ppermute(levels[k], axes, across(2 * k)) for k in (3, 2, 1)}
    return [levels[0]] + [arrived[k] for k in (2, 1, 3)], w_t


def finish_direct(operands, w_t, date_s, tile_s, heads, scale, pixel_dev, dates_dev, tiles, dates):
    length = dates * dates_dev
    cols, model_d = w_t.shape
    wide = model_d + EXT
    half_rows = length // 2
    payload = cols + 16 + half_rows * wide // LANES
    payload_z = cols + 16 + 2 * dates_dev * wide // LANES
    axes = ("tile", "date")

    def across(mask):
        return [(i, i ^ mask) for i in range(tiles * dates)]

    series, w_t = direct_series(operands, w_t, date_s, dates_dev, model_d, axes, across)
    *sends, rows_own, rows_give, sel = call(
        functools.partial(direct_series_kernel, heads, model_d, dates_dev),
        [((4 * length + 16, LANES), BF16)] * tiles
        + [((half_rows, wide), BF16), ((half_rows, wide), BF16), ((16, length), BF16)],
        [date_s, tile_s, *series, w_t],
        2,
        [pltpu.VMEM((length, 3 * model_d + LANES), BF16)],
    )
    parts = {k: lax.ppermute(sends[k], axes, across(dates * k + k % 2)) for k in (3, 2, 1)}
    keep, keep_sums, give = call(
        direct_slab_kernel,
        [((cols, LANES), F32), ((8, LANES), F32), ((payload, LANES), BF16)],
        [date_s, sends[0], parts[3], parts[2], parts[1], sel, rows_give],
        1,
    )
    got = lax.ppermute(give, axes, across(1))
    rows_own, own, *levels = call(
        functools.partial(direct_join_kernel, dates_dev),
        [((2 * dates_dev, wide), BF16), ((cols + 16, LANES), BF16)] + [((payload_z, LANES), BF16)] * 3,
        [keep, keep_sums, rows_own, got],
    )
    arrived = {k: lax.ppermute(levels[k - 1], axes, across(2 * k)) for k in (3, 2, 1)}
    low, high, both = (arrived[k] for k in (1, 2, 3))
    slab, rest = call(
        direct_total_kernel, [((cols, LANES), BF16), ((8, LANES), F32)], [own, low, both, high]
    )
    gathered = {k: lax.ppermute(slab, axes, across(dates * k)) for k in (3, 2, 1)}
    slabs = jnp.stack([slab] + [gathered[k] for k in (1, 2, 3)])
    other_slabs = lax.ppermute(slabs, axes, across(1))
    outs = [
        jax.ShapeDtypeStruct((pixel_dev, dates_dev, model_d), BF16),
        jax.ShapeDtypeStruct((pixel_dev, dates_dev, model_d), BF16),
        jax.ShapeDtypeStruct((2, model_d), F32),
        jax.ShapeDtypeStruct((3, heads), F32),
        jax.ShapeDtypeStruct((cols, model_d), F32),
    ]
    held = [pltpu.VMEM((tiles, cols, LANES), F32), pltpu.SemaphoreType.DMA((tiles,))]
    limit = pltpu.CompilerParams(vmem_limit_bytes=48 * 1024 * 1024)
    value, inputs, table, head, weight_t = pl.pallas_call(
        functools.partial(final_kernel, heads, scale),
        out_shape=outs,
        in_specs=[SMEM] * 2 + [VMEM] * 7,
        out_specs=[HBM] * 5,
        scratch_shapes=[pltpu.VMEM(o.shape, o.dtype) for o in outs[:4]]
        + held
        + [pltpu.SemaphoreType.DMA((4,))],
        compiler_params=limit,
    )(date_s, tile_s, slabs, rows_own, low, high, both, rest, w_t)
    weight_t = pl.pallas_call(
        functools.partial(other_slabs_kernel, scale),
        out_shape=outs[4],
        in_specs=[SMEM, SMEM, VMEM, HBM],
        out_specs=HBM,
        scratch_shapes=held,
        input_output_aliases={3: 0},
        compiler_params=limit,
    )(date_s, tile_s, other_slabs, weight_t)
    return value, inputs, weight_t.T, table, head


def finish_any(series, w_t, date_s, tile_s, heads, scale, pixel_dev, dates_dev, tiles, dates):
    length = series.shape[0]
    cols, model_d = w_t.shape
    levels = dates // 2
    slab = model_d // tiles
    half = slab // 2
    swap = [(i, i ^ 1) for i in range(dates)]
    planes = [[2 * z + c for z in range(levels)] for c in range(2)]
    rows_core = length // 2
    send_t, own, give_rows, sel = call(
        functools.partial(series_kernel, heads, model_d, 0, dates_dev),
        [
            ((tiles, length, EXT + slab), BF16),
            ((rows_core, model_d + EXT), BF16),
            ((rows_core, model_d + EXT), BF16),
            ((16, length), BF16),
        ],
        [date_s, series, w_t],
        1,
    )
    mixed = [
        [t * dates + 2 * z + (c + t) % 2 for t in range(tiles)] for z in range(levels) for c in range(2)
    ]
    recv_t = lax.all_to_all(
        send_t, ("tile", "date"), split_axis=0, concat_axis=0, tiled=True, axis_index_groups=mixed
    )
    rows_give = cols + 24 + rows_core * (model_d + EXT) // LANES
    keep, keep_sums, give = call(
        functools.partial(slab_kernel, cols),
        [((cols, LANES), F32), ((2, EXT), F32), ((rows_give, LANES), BF16)],
        [date_s, recv_t, sel, give_rows],
        1,
    )
    got = lax.ppermute(give, "date", swap)
    rows_z = cols + 32 + model_d // 16
    (send_z,) = call(
        functools.partial(join_kernel, cols, dates_dev),
        [((levels, rows_z, LANES), BF16)],
        [date_s, keep, keep_sums, got, own],
        1,
    )
    recv_z = lax.all_to_all(
        send_z, "date", split_axis=0, concat_axis=0, tiled=True, axis_index_groups=planes
    )
    send_g, rest = call(
        functools.partial(total_kernel, cols),
        [((tiles, cols, LANES), BF16), ((16, LANES), F32)],
        [recv_z],
    )
    recv_g = lax.all_to_all(send_g, "tile", split_axis=0, concat_axis=0, tiled=True)
    local_outs = [
        ((pixel_dev, dates_dev, model_d), BF16),
        ((pixel_dev, dates_dev, model_d), BF16),
        ((2, model_d), F32),
        ((3, heads), F32),
    ]
    other_g = lax.ppermute(recv_g, "date", swap)
    if half % LANES == 0:
        weight_shape = jax.ShapeDtypeStruct((cols, model_d), F32)
        held = [pltpu.VMEM((tiles, cols, half), F32), pltpu.SemaphoreType.DMA((tiles,))]
        limit = pltpu.CompilerParams(vmem_limit_bytes=48 * 1024 * 1024)
        value, inputs, table, head, weight_t = pl.pallas_call(
            functools.partial(local_weight_kernel, heads, scale, cols, half),
            out_shape=[jax.ShapeDtypeStruct(s, d) for s, d in local_outs] + [weight_shape],
            in_specs=[SMEM] + [VMEM] * 4,
            out_specs=[HBM] * 5,
            scratch_shapes=[pltpu.VMEM(s, d) for s, d in local_outs]
            + held
            + [pltpu.SemaphoreType.DMA((4,))],
            compiler_params=limit,
        )(date_s, recv_g, recv_z, rest, w_t)
        weight_t = pl.pallas_call(
            functools.partial(half_kernel, cols, scale, half),
            out_shape=weight_shape,
            in_specs=[SMEM, VMEM, HBM],
            out_specs=HBM,
            scratch_shapes=held,
            input_output_aliases={2: 0},
            compiler_params=limit,
        )(date_s, other_g, weight_t)
    else:
        value, inputs, table, head = call(
            functools.partial(local_kernel, heads, scale), local_outs, [recv_z, rest, w_t]
        )
        (weight_t,) = call(
            functools.partial(gather_kernel, cols, half, scale),
            [((cols, model_d), F32)],
            [date_s, recv_g, other_g],
            1,
        )
    return (
        value,
        inputs,
        weight_t.T,
        table,
        head,
    )


def on_device(
    layer_input,
    head_input,
    out_grad,
    sensor_ids,
    valid_mask,
    sensor_table,
    proj_weight,
    step_bias,
    decay_log,
    skip_gain,
):
    pixel_dev, dates_dev, model_d = layer_input.shape
    heads = step_bias.shape[0]
    tiles = lax.axis_size("tile")
    dates = lax.axis_size("date")
    assert pixel_dev == dates and dates % 2 == 0
    levels = dates // 2
    length = dates * dates_dev
    slab = model_d // tiles
    half = slab // 2
    date_s = lax.axis_index("date").astype(jnp.int32).reshape(1)
    tile_s = lax.axis_index("tile").astype(jnp.int32).reshape(1)
    w_t = proj_weight.T
    scale = 1.0 / math.sqrt(pixel_dev * dates_dev * tiles * dates)

    operands = [
        sensor_ids,
        valid_mask.T,
        sensor_table,
        step_bias[None],
        decay_log[None],
        skip_gain[None],
        layer_input,
        head_input,
        out_grad,
    ]
    if levels == 4 and tiles == 4 and model_d == 2 * LANES * tiles:
        return finish_direct(operands, w_t, date_s, tile_s, heads, scale, pixel_dev, dates_dev, tiles, dates)
    packed = pl.pallas_call(
        pack_kernel,
        out_shape=jax.ShapeDtypeStruct((pixel_dev, dates_dev, 3 * model_d + LANES), BF16),
        in_specs=[SMEM] * 2 + [HBM] * 9,
        out_specs=VMEM,
        scratch_shapes=[
            pltpu.SMEM((dates_dev,), jnp.int32),
            pltpu.VMEM((dates_dev, pixel_dev), jnp.int32),
            pltpu.VMEM((2, model_d), F32),
            pltpu.VMEM((3, heads), F32),
            pltpu.VMEM((pixel_dev, dates_dev, model_d), BF16),
            pltpu.SemaphoreType.DMA((9,)),
        ],
        compiler_params=pltpu.CompilerParams(vmem_limit_bytes=16 * 1024 * 1024),
    )(date_s, tile_s, *[pltpu.with_memory_space_constraint(operand, pltpu.HBM) for operand in operands])
    series = lax.all_to_all(packed, "date", split_axis=0, concat_axis=0, tiled=True).reshape(
        length, 3 * model_d + LANES
    )

    return finish_any(series, w_t, date_s, tile_s, heads, scale, pixel_dev, dates_dev, tiles, dates)


def solution(mesh):
    in_specs = (
        P("tile", "date", None),
        P("tile", "date", None),
        P("tile", "date", None),
        P("date"),
        P("tile", "date"),
        P(),
        P(),
        P(),
        P(),
        P(),
    )
    out_specs = (P("tile", "date", None), P("tile", "date", None), P(), P(), P())
    return jax.shard_map(
        on_device, mesh=mesh, in_specs=in_specs, out_specs=out_specs, check_vma=False
    )
```

```python
import functools
import math

import jax
import jax.numpy as jnp
from jax import lax
from jax.experimental import pallas as pl
from jax.experimental.pallas import tpu as pltpu
from jax.sharding import PartitionSpec as P

NEG_FILL = -1e30
HIGHEST_PREC = lax.Precision.HIGHEST
F32 = jnp.float32
BF16 = jnp.bfloat16
LANES = 128
TILE_ORDER = (0, 3, 2, 1)
EXT = 384


def nt(a, b, precision=None):
    return lax.dot_general(
        a, b, (((1,), (1,)), ((), ())), preferred_element_type=F32, precision=precision
    )


def nn(a, b, precision=None):
    return lax.dot_general(
        a, b, (((1,), (0,)), ((), ())), preferred_element_type=F32, precision=precision
    )


def tn(a, b):
    return lax.dot_general(a, b, (((0,), (0,)), ((), ())), preferred_element_type=F32)


def split(x):
    high = x.astype(BF16)
    return high, (x - high.astype(F32)).astype(BF16)


def bit_of(pos, bit):
    return lax.rem(lax.div(pos[0], 2**bit), 2)


def halves(arrays, span, first):
    kept, given = [], []
    for array in arrays:
        for at in range(0, array.shape[0], 2 * span):
            a, b = array[at : at + span], array[at + span : at + 2 * span]
            kept.append(jnp.where(first, a, b))
            given.append(jnp.where(first, b, a))
    return jnp.concatenate(kept, axis=0), jnp.concatenate(given, axis=0)


def series_terms(heads, model_d, recv, w_t, order=0):
    length = recv.shape[0]
    width_p = model_d // heads
    states = (w_t.shape[0] - heads) // 2
    mixed = recv[:, :model_d]
    aux = recv[:, 3 * model_d :].astype(F32)
    gate = aux[:, 0:1]
    ids = aux[:, 1:2]
    params = []
    for at in range(2, 2 + 9 * heads, 3 * heads):
        params.append(sum(aux[0:1, at + k * heads : at + (k + 1) * heads] for k in range(3)))
    bias, rate, skip = params[0], -jnp.exp(params[1]), params[2]
    projected = nt(mixed, w_t[...])
    keys = projected[:, :states].astype(BF16)
    reads = projected[:, states : 2 * states].astype(BF16)
    step_pre = projected[:, 2 * states :] + bias
    softplus = jnp.maximum(step_pre, 0.0) + jnp.log1p(jnp.exp(-jnp.abs(step_pre)))
    steps_b = (gate * softplus).astype(BF16)
    steps = steps_b.astype(F32)

    row = lax.broadcasted_iota(jnp.int32, (length, length), 0)
    col = lax.broadcasted_iota(jnp.int32, (length, length), 1)
    upper = (col ^ order) >= (row ^ order)
    upper_f = upper.astype(F32)
    eye = (col == row).astype(F32)
    lower_b = ((row ^ order) >= (col ^ order)).astype(BF16)
    head_row = lax.broadcasted_iota(jnp.int32, (heads, heads), 0)
    head_col = lax.broadcasted_iota(jnp.int32, (heads, heads), 1)
    eye_h = (head_row == head_col).astype(F32)
    rate_col = jnp.sum(eye_h * rate, axis=1, keepdims=True)
    log_col = nn(lower_b, steps_b) * rate
    steps_t = nt(eye_h.astype(BF16), steps_b).astype(BF16)
    log_row = nn(steps_t, upper.astype(BF16)) * rate_col
    scores_t = nt(keys, reads)

    pair_t = jnp.zeros((length, length), F32)
    mixes, weighted_cols, read_rows, skip_cols = [], [], [], []
    for h in range(heads):
        lo = model_d + h * width_p
        x_h = recv[:, lo : lo + width_p]
        g_h = recv[:, lo + model_d : lo + model_d + width_p]
        dt_h = steps[:, h : h + 1]
        gap = log_row[h : h + 1, :] - log_col[:, h : h + 1]
        decay = jnp.exp(jnp.where(upper, gap, NEG_FILL))
        cross = nt(x_h, g_h)
        mix = decay * scores_t
        pair_t = pair_t + decay * cross * dt_h
        both = mix * cross
        weighted = jnp.sum(both, axis=1, keepdims=True)
        weighted_cols.append(weighted)
        read_rows.append(jnp.sum(both * dt_h, axis=0, keepdims=True))
        skip_cols.append(jnp.sum(cross * eye, axis=1, keepdims=True))
        mixes.append((mix.astype(BF16), g_h, dt_h, skip[:, h : h + 1]))

    weighted = jnp.concatenate(weighted_cols, axis=1)
    read_sum = jnp.concatenate(read_rows, axis=0)
    skip_terms = jnp.concatenate(skip_cols, axis=1)
    later = nt(upper_f, read_sum, HIGHEST_PREC) - nn(upper_f, steps * weighted, HIGHEST_PREC)
    step_grad = (weighted + rate * later).astype(BF16).astype(F32)
    decay_terms = steps * later * rate
    pair_b = pair_t.astype(BF16)
    grad_keys = nn(pair_b, reads)
    grad_reads = tn(pair_b, keys)
    raw = step_grad * gate * jax.nn.sigmoid(step_pre)
    terms = jnp.concatenate(
        [raw, decay_terms, skip_terms, jnp.zeros((length, LANES - 3 * heads), F32)], axis=1
    )
    ids_row = jnp.sum(eye * ids, axis=0, keepdims=True)
    return mixes, grad_keys, grad_reads, raw, terms, ids_row, eye_h


def value_columns(mixes):
    return [nn(mix, g_h) * dt_h + skip_h * g_h.astype(F32) for mix, g_h, dt_h, skip_h in mixes]


def sensor_rows(ids_row):
    zeros = jnp.zeros((14, ids_row.shape[1]), F32)
    return jnp.concatenate([1.0 - ids_row, ids_row, zeros], axis=0).astype(BF16)


def series_kernel(heads, model_d, bit, span, pos, recv, w_t, send, own, give, sel):
    tiles, _, width = send.shape
    slab = width - EXT
    mixes, grad_keys, grad_reads, _, terms, ids_row, _ = series_terms(heads, model_d, recv, w_t)
    high = terms.astype(BF16).astype(F32)
    tail = high + pltpu.roll(terms - high, 3 * heads, 1)
    ext_f = jnp.concatenate([grad_keys, grad_reads, tail], axis=1)
    ext = ext_f.astype(BF16)
    back = jnp.concatenate(value_columns(mixes) + [ext_f], axis=1)
    kept, given = halves([back], span, bit_of(pos, bit) == 0)
    own[...] = kept.astype(BF16)
    give[...] = given.astype(BF16)
    for t in range(tiles):
        send[t, :, :EXT] = ext
        send[t, :, EXT:] = recv[:, t * slab : (t + 1) * slab]
    sel[...] = sensor_rows(ids_row)


def direct_series_kernel(heads, model_d, dates, pos, tile, *refs):
    levels, w_t, sends, (own, give, sel, recv) = refs[:4], refs[4], refs[5:-4], refs[-4:]
    levels = tuple(levels[k] for k in (0, 2, 1, 3))
    length = recv.shape[0]
    slab = 2 * LANES
    recv[...] = jnp.concatenate([level[...].astype(F32) for level in levels], axis=0).astype(BF16)
    order = lax.div(pos[0], 2) * (2 * dates)
    mixes, grad_keys, grad_reads, raw, terms, ids_row, eye_h = series_terms(heads, model_d, recv, w_t, order)
    raw_t = nt(eye_h.astype(BF16), raw.astype(BF16))
    total = jnp.sum(terms, axis=0, keepdims=True)
    high = total.astype(BF16).astype(F32)
    misc = jnp.concatenate(
        [lane_pad(raw_t, LANES), high, total - high, jnp.zeros((6, LANES), F32)], axis=0
    )
    grads = jnp.concatenate([grad_keys, grad_reads, misc], axis=0).astype(BF16)
    for k, send in enumerate(sends):
        for block in range(2):
            at = pl.multiple_of((tile[0] ^ k) * slab + block * LANES, LANES)
            send[block * length : (block + 1) * length] = recv[:, pl.ds(at, LANES)]
        send[2 * length :] = grads
    back = jnp.concatenate(value_columns(mixes) + [grad_keys, grad_reads, lane_pad(raw, LANES)], axis=1)
    kept, given = halves([back], dates, bit_of(pos, 0) == 0)
    own[...] = kept.astype(BF16)
    give[...] = given.astype(BF16)
    sel[...] = sensor_rows(ids_row)


def shared_rows(dates, ids, table, params):
    rows = [jnp.where(ids[i] == 1, table[1:2, :], table[0:1, :]) for i in range(dates)]
    embed = jnp.concatenate(rows, axis=0)
    row = lax.broadcasted_iota(jnp.int32, (dates, LANES), 0)
    lane = lax.broadcasted_iota(jnp.int32, (dates, LANES), 1)
    second = jnp.zeros((dates, LANES), F32)
    for i in range(dates):
        second = jnp.where((row == i) & (lane == 1), (ids[i] == 1).astype(F32), second)
    at = 2
    for k in range(3):
        rest = params[k : k + 1, :]
        for _ in range(3):
            term = rest.astype(BF16).astype(F32)
            rest = rest - term
            term = jnp.concatenate([jnp.zeros((1, at), F32), term, jnp.zeros((1, LANES - at - term.shape[1]), F32)], axis=1)
            second = second + term
            at = at + params.shape[1]
    return embed, second


def pack_kernel(pos, tile, ids_in, mask_in, table_in, bias_in, decay_in, skip_in, layer, values, cotangent, out, ids, mask_t, table, params, layer_v, sems):
    pixels, dates, model_d = layer.shape
    small = [
        pltpu.make_async_copy(ids_in, ids, sems.at[0]),
        pltpu.make_async_copy(mask_in, mask_t, sems.at[1]),
        pltpu.make_async_copy(table_in, table, sems.at[2]),
        pltpu.make_async_copy(layer, layer_v, sems.at[3]),
        pltpu.make_async_copy(bias_in, params.at[0:1], sems.at[6]),
        pltpu.make_async_copy(decay_in, params.at[1:2], sems.at[7]),
        pltpu.make_async_copy(skip_in, params.at[2:3], sems.at[8]),
    ]
    large = [
        pltpu.make_async_copy(values, out.at[:, :, model_d : 2 * model_d], sems.at[4]),
        pltpu.make_async_copy(cotangent, out.at[:, :, 2 * model_d : 3 * model_d], sems.at[5]),
    ]
    for copy in small[3:4] + large + small[:3] + small[4:]:
        copy.start()
    for copy in small:
        copy.wait()
    embed, second = shared_rows(dates, ids, table, params)
    lane = lax.broadcasted_iota(jnp.int32, (dates, LANES), 1)
    gate = mask_t[...].astype(F32)
    for p in range(pixels):
        out[p, :, 3 * model_d :] = jnp.where(lane == 0, gate[:, p : p + 1], second).astype(BF16)
        out[p, :, :model_d] = (layer_v[p].astype(F32) + embed).astype(BF16)
    for copy in large:
        copy.wait()


def direct_pack_kernel(
    pos, w_in, ids_in, mask_in, table_in, bias_in, decay_in, skip_in, layer, values, cotangent, keep, give, w_t, *scratch
):
    ids, mask_t, table, params, layer_v, sems = scratch
    levels, _, dates, model_d = layer.shape
    core = bit_of(pos, 0)
    small = [
        pltpu.make_async_copy(ids_in, ids, sems.at[0]),
        pltpu.make_async_copy(mask_in, mask_t, sems.at[1]),
        pltpu.make_async_copy(table_in, table, sems.at[2]),
        pltpu.make_async_copy(bias_in, params.at[0:1], sems.at[3]),
        pltpu.make_async_copy(decay_in, params.at[1:2], sems.at[4]),
        pltpu.make_async_copy(skip_in, params.at[2:3], sems.at[5]),
        pltpu.make_async_copy(layer, layer_v, sems.at[6]),
    ]
    large = [pltpu.make_async_copy(w_in, w_t, sems.at[11])]
    for k, array in enumerate((values, cotangent)):
        to = slice((k + 1) * model_d, (k + 2) * model_d)
        large.append(pltpu.make_async_copy(array.at[:, core], keep.at[:, :, to], sems.at[7 + k]))
        large.append(pltpu.make_async_copy(array.at[:, 1 - core], give.at[:, :, to], sems.at[9 + k]))
    for copy in small[-1:] + large[1:] + small[:-1] + large[:1]:
        copy.start()
    for copy in small:
        copy.wait()
    embed, extra = shared_rows(dates, ids, table, params)
    lane = lax.broadcasted_iota(jnp.int32, (dates, LANES), 1)
    gate = mask_t[...].astype(F32)
    first = core == 0
    for level in range(levels):
        gates = [gate[:, 2 * level + c : 2 * level + c + 1] for c in range(2)]
        mixed = [layer_v[level, c].astype(F32) + embed for c in range(2)]
        for out, mine in ((keep, first), (give, jnp.logical_not(first))):
            chosen = jnp.where(mine, gates[0], gates[1])
            out[level, :, 3 * model_d :] = jnp.where(lane == 0, chosen, extra).astype(BF16)
            out[level, :, :model_d] = jnp.where(mine, mixed[0], mixed[1]).astype(BF16)
    for copy in large:
        copy.wait()


def level_rows_kernel(pos, keep, got, *outs):
    first = bit_of(pos, 0) == 0
    level = lax.div(pos[0], 2)
    for k, out in enumerate(outs):
        mine, theirs = keep[level ^ k].astype(F32), got[level ^ k].astype(F32)
        out[...] = jnp.concatenate(
            [jnp.where(first, mine, theirs), jnp.where(first, theirs, mine)], axis=0
        ).astype(BF16)


def lane_pad(x, width):
    if x.shape[1] == width:
        return x
    return jnp.concatenate([x, jnp.zeros((x.shape[0], width - x.shape[1]), x.dtype)], axis=1)


def sum_rows(sums):
    high = sums.astype(BF16).astype(F32)
    low = (sums - high).astype(BF16).astype(F32)
    rows = jnp.concatenate([high, low, jnp.zeros((4, EXT), F32)], axis=0)
    return [rows[:, b * LANES : (b + 1) * LANES] for b in range(EXT // LANES)]


def rows_sum(block):
    rows = jnp.concatenate([block[8 * b : 8 * b + 8, :] for b in range(EXT // LANES)], axis=1)
    return rows[0:2] + rows[2:4]


def slab_kernel(cols, pos, recv, sel, rows, keep, keep_sums, give):
    tiles, length, width = recv.shape
    slab = width - EXT
    half = slab // 2
    ext = recv[:, :, :EXT].reshape(tiles * length, EXT)
    tokens = recv[:, :, EXT:].reshape(tiles * length, slab)
    part = tn(ext, tokens)[:cols]
    sums = jnp.zeros((16, EXT), F32)
    for t in range(tiles):
        sums = sums + nn(sel[...], recv[t, :, :EXT])
    sums = sums[0:2]
    mine = bit_of(pos, 0) == 0
    first = lane_pad(part[:, :half], LANES)
    second = lane_pad(part[:, half:], LANES)
    keep[...] = jnp.where(mine, first, second)
    keep_sums[...] = sums
    other = jnp.where(mine, second, first)
    blocks = [rows[:, b * LANES : (b + 1) * LANES].astype(F32) for b in range(rows.shape[1] // LANES)]
    give[...] = jnp.concatenate([other] + sum_rows(sums) + blocks, axis=0).astype(BF16)


def join_kernel(cols, dates, pos, keep, keep_sums, got, own, send):
    levels = send.shape[0]
    first = bit_of(pos, 0) == 0
    model_d = own.shape[1] - EXT
    total = keep[...] + got[:cols, :].astype(F32)
    sums = sum_rows(keep_sums[...] + rows_sum(got[cols : cols + 24, :].astype(F32)))
    pair_sums = jnp.concatenate([sums[0][:4], sums[1][:4]], axis=0)
    mine, count = own[...].astype(F32), own.shape[0]
    tall = got[cols + 24 :, :].astype(F32)
    theirs = jnp.concatenate([tall[k : k + count] for k in range(0, tall.shape[0], count)], axis=1)
    firsts, seconds = jnp.where(first, mine, theirs), jnp.where(first, theirs, mine)
    lane = lax.broadcasted_iota(jnp.int32, (8, LANES), 1)
    last = pltpu.roll(sums[2], 64, 1)
    for z in range(levels):
        at = z * dates
        rows = jnp.concatenate([firsts[at : at + dates], seconds[at : at + dates]], axis=0)
        ext = [rows[:, model_d + b * LANES : model_d + (b + 1) * LANES] for b in range(EXT // LANES)]
        misc = jnp.where(lane < 64, ext[2], last)
        value = [rows[:, b * LANES : (b + 1) * LANES] for b in range(model_d // LANES)]
        send[z] = jnp.concatenate([total, ext[0], ext[1], misc, pair_sums] + value, axis=0).astype(BF16)


def total_kernel(cols, recv, send, rest):
    levels = recv.shape[0]
    total = recv[0].astype(F32)
    for z in range(1, levels):
        total = total + recv[z].astype(F32)
    slab = total[:cols].astype(BF16)
    for t in range(send.shape[0]):
        send[t] = slab
    rest[...] = total[cols + 16 : cols + 32]


def store_half(cols, scale, core, half, slabs, weight, held, sems):
    copies = []
    for t in range(slabs.shape[0]):
        held[t] = slabs[t].astype(F32)[:cols] * scale
        at = pl.multiple_of((2 * t + core) * half, half)
        copies.append(pltpu.make_async_copy(held.at[t], weight.at[:, pl.ds(at, half)], sems.at[t]))
        copies[-1].start()
    return copies


def half_kernel(cols, scale, half, pos, slabs, weight_in, weight, held, sems):
    for copy in store_half(cols, scale, 1 - bit_of(pos, 0), half, slabs, weight, held, sems):
        copy.wait()


def local_weight_kernel(heads, scale, cols, half, pos, slabs, recv, rest, w_t, *refs):
    outs, held_outs = refs[:5], refs[5:10]
    held, sems, out_sems = held_outs[4], refs[10], refs[11]
    copies = store_half(cols, scale, bit_of(pos, 0), half, slabs, outs[4], held, sems)
    moves = [pltpu.make_async_copy(held_outs[k], outs[k], out_sems.at[k]) for k in range(4)]
    local_kernel(heads, scale, recv, rest, w_t, *held_outs[:4], moves)
    for copy in copies + moves:
        copy.wait()


def write_sums(heads, scale, sums, w, table, head):
    cols = w.shape[0]
    high, low = split(sums[:, :cols])
    table[...] = (nn(high, w) + nn(low, w)) * scale
    both = sums[0:1] + sums[1:2]
    at = cols - heads
    rows = []
    for k in (1, 0, 2):
        lo = at + k * heads
        rows.append(both[:, lo : lo + heads] + both[:, lo + 3 * heads : lo + 4 * heads])
    head[...] = jnp.concatenate(rows, axis=0) * scale


def local_kernel(heads, scale, recv, rest, w_t, value, inputs, table, head, moves=()):
    levels = recv.shape[0]
    model_d = w_t.shape[1]
    cols = w_t.shape[0]
    dates = value.shape[1]
    w = w_t[...]
    ext_rows = []
    for z in range(levels):
        rows = recv[z].astype(F32)
        ext_rows.append(jnp.concatenate([rows[cols + 8 * b : cols + 8 * b + 8] for b in range(3)], axis=1))
        at = cols + 32
        values = jnp.concatenate([rows[at + 8 * b : at + 8 * b + 8] for b in range(model_d // LANES)], axis=1)
        for c in range(2):
            value[2 * z + c] = values[c * dates : (c + 1) * dates].astype(BF16)
    for move in moves[:1]:
        move.start()
    grads = nn(jnp.concatenate(ext_rows, axis=0).astype(BF16)[:, :cols], w)
    for p in range(2 * levels):
        inputs[p] = grads[p * dates : (p + 1) * dates].astype(BF16)
    for move in moves[1:2]:
        move.start()
    last = pltpu.roll(rest[0:8, :], 64, 1)
    sums = jnp.concatenate([rest[8:12, :], rest[12:16, :], last[0:4]], axis=1)
    sums = sums[0:2] + sums[2:4]
    write_sums(heads, scale, sums, w, table, head)
    for move in moves[2:]:
        move.start()


def gather_kernel(cols, half, scale, pos, own, other, out):
    tiles = own.shape[0]
    mine = bit_of(pos, 0) == 0
    for t in range(tiles):
        a = own[t].astype(F32)
        b = other[t].astype(F32)
        first = jnp.where(mine, a, b)[:cols, :half]
        second = jnp.where(mine, b, a)[:cols, :half]
        out[:, 2 * half * t : 2 * half * (t + 1)] = jnp.concatenate([first, second], axis=1) * scale


VMEM = pl.BlockSpec(memory_space=pltpu.VMEM)
SMEM = pl.BlockSpec(memory_space=pltpu.SMEM)
HBM = pl.BlockSpec(memory_space=pltpu.HBM)


def call(kernel, outs, ins, smem=0, scratch=()):
    return pl.pallas_call(
        kernel,
        out_shape=[jax.ShapeDtypeStruct(s, d) for s, d in outs],
        in_specs=[SMEM] * smem + [VMEM] * (len(ins) - smem),
        out_specs=[VMEM] * len(outs),
        scratch_shapes=list(scratch),
        compiler_params=pltpu.CompilerParams(vmem_limit_bytes=48 * 1024 * 1024),
    )(*ins)


def rows_block(rows):
    return [rows[:, b * LANES : (b + 1) * LANES] for b in range(rows.shape[1] // LANES)]


def block_rows(block, count):
    return jnp.concatenate([block[k : k + count] for k in range(0, block.shape[0], count)], axis=1)


def pack_sums(sums):
    high = sums.astype(BF16).astype(F32)
    return jnp.concatenate([high, sums - high], axis=0)


def unpack_sums(rows):
    return rows[:8] + rows[8:16]


def pair_sum(parts):
    return (parts[0] + parts[1]) + (parts[2] + parts[3])


def direct_slab_kernel(pos, *refs):
    parts, (sel, rows, keep, keep_sums, give) = refs[:4], refs[4:]
    parts = (parts[0], parts[3], parts[2], parts[1])
    cols = keep.shape[0]
    length = sel.shape[1]
    first = bit_of(pos, 0) == 0
    chosen = sel[...]
    tokens, keys, reads, raw_t, sums = [], [], [], [], []
    for part in parts:
        tokens.append(jnp.concatenate([part[:length], part[length : 2 * length]], axis=1))
        keys.append(part[2 * length : 3 * length])
        reads.append(part[3 * length : 4 * length])
        misc = part[4 * length :]
        raw_t.append(misc[:, :length])
        head = misc.astype(F32)[8:10]
        sums.append(
            jnp.concatenate(
                [
                    nn(chosen, keys[-1])[0:2],
                    nn(chosen, reads[-1])[0:2],
                    lane_pad(nt(chosen, raw_t[-1])[0:2], LANES),
                    head[0:1] + head[1:2],
                    jnp.zeros((1, LANES), F32),
                ],
                axis=0,
            )
        )
    tokens = jnp.concatenate(tokens, axis=0)
    slab = jnp.concatenate(
        [
            tn(jnp.concatenate(keys, axis=0), tokens),
            tn(jnp.concatenate(reads, axis=0), tokens),
            nn(jnp.concatenate(raw_t, axis=1), tokens)[: cols - 2 * LANES],
        ],
        axis=0,
    )
    left, right = slab[:, :LANES], slab[:, LANES:]
    keep[...] = jnp.where(first, left, right)
    packed = pack_sums(pair_sum(sums))
    keep_sums[...] = unpack_sums(packed)
    give[...] = jnp.concatenate(
        [jnp.where(first, right, left), packed] + rows_block(rows[...].astype(F32)), axis=0
    ).astype(BF16)


def direct_join_kernel(dates, keep, keep_sums, rows_own, got, rows_keep, own, low, high, both):
    cols = keep.shape[0]
    there = got[...].astype(F32)
    total = keep[...] + there[:cols]
    sums = keep_sums[...] + unpack_sums(there[cols : cols + 16])
    rows = [rows_own[...].astype(F32), block_rows(there[cols + 16 :], rows_own.shape[0])]
    here, low_rows, high_rows, both_rows = (
        jnp.concatenate([part[k * dates : (k + 1) * dates] for part in rows], axis=0) for k in range(4)
    )
    rows_keep[...] = here.astype(BF16)
    common = jnp.concatenate([total, pack_sums(sums)], axis=0).astype(BF16)
    own[...] = common
    for send, part in ((low, low_rows), (high, high_rows), (both, both_rows)):
        send[...] = jnp.concatenate([common] + rows_block(part.astype(BF16)), axis=0)


def direct_total_kernel(own, low, both, high, send, rest):
    cols = send.shape[0]
    total = pair_sum([part[...].astype(F32)[: cols + 16] for part in (own, low, high, both)])
    send[...] = total[:cols].astype(BF16)
    rest[...] = unpack_sums(total[cols:])


def store_slabs(scale, tile, core, slabs, weight, held, sems):
    copies = []
    for k, slab in enumerate(slabs):
        held[k] = slab.astype(F32) * scale
        at = pl.multiple_of((2 * (tile ^ TILE_ORDER[k]) + core) * LANES, LANES)
        copies.append(pltpu.make_async_copy(held.at[k], weight.at[:, pl.ds(at, LANES)], sems.at[k]))
        copies[-1].start()
    return copies


def other_slabs_kernel(scale, pos, tile, slabs, weight_in, weight, held, sems):
    parts = [slabs[k] for k in range(slabs.shape[0])]
    for copy in store_slabs(scale, tile[0], 1 - bit_of(pos, 0), parts, weight, held, sems):
        copy.wait()


def final_kernel(heads, scale, pos, tile, slabs, rows_own, low, high, both, rest, w_t, *refs):
    outs, (value, inputs, table, head), (held, sems, out_sems) = refs[:5], refs[5:9], refs[9:]
    model_d, cols, dates = w_t.shape[1], w_t.shape[0], value.shape[1]
    parts = [slabs[k] for k in range(slabs.shape[0])]
    copies = store_slabs(scale, tile[0], bit_of(pos, 0), parts, outs[4], held, sems)
    moves = [
        pltpu.make_async_copy(source, outs[k], out_sems.at[k])
        for k, source in enumerate((value, inputs, table, head))
    ]
    w = w_t[...]
    rows = [rows_own[...].astype(F32)]
    for part in (low, high, both):
        rows.append(block_rows(part[...].astype(F32)[cols + 16 :], 2 * dates))
    rows = jnp.concatenate(rows, axis=0)
    masks = [0, 1, 2, 3, 4, 5, 6, 7]
    for k, mask in enumerate(masks):
        value[pos[0] ^ mask] = rows[k * dates : (k + 1) * dates, :model_d].astype(BF16)
    moves[0].start()
    grads = nn(rows[:, model_d : model_d + EXT].astype(BF16)[:, :cols], w)
    for k, mask in enumerate(masks):
        inputs[pos[0] ^ mask] = grads[k * dates : (k + 1) * dates].astype(BF16)
    moves[1].start()
    sums = jnp.concatenate([rest[0:2, :], rest[2:4, :], rest[4:6, :]], axis=1)[:, :cols]
    parts_high, parts_low = split(sums)
    table[...] = (nn(parts_high, w) + nn(parts_low, w)) * scale
    total = rest[6:7, :]
    head[...] = jnp.concatenate([total[:, k * heads : (k + 1) * heads] for k in (1, 0, 2)], axis=0) * scale
    for move in moves[2:]:
        move.start()
    for copy in copies + moves:
        copy.wait()


def direct_series(operands, w_t, date_s, dates_dev, model_d, axes, across):
    *small, layer, values, cotangent = operands
    arrays = [a.reshape(4, 2, dates_dev, model_d) for a in (layer, values, cotangent)]
    packed = jax.ShapeDtypeStruct((4, dates_dev, 3 * model_d + LANES), BF16)
    heads = small[-1].shape[1]
    keep, give, w_t = pl.pallas_call(
        direct_pack_kernel,
        out_shape=[packed, packed, jax.ShapeDtypeStruct(w_t.shape, w_t.dtype)],
        in_specs=[SMEM] + [HBM] * 10,
        out_specs=[VMEM] * 3,
        scratch_shapes=[
            pltpu.SMEM((dates_dev,), jnp.int32),
            pltpu.VMEM((dates_dev, 8), jnp.int32),
            pltpu.VMEM((2, model_d), F32),
            pltpu.VMEM((3, heads), F32),
            pltpu.VMEM((4, 2, dates_dev, model_d), BF16),
            pltpu.SemaphoreType.DMA((12,)),
        ],
        compiler_params=pltpu.CompilerParams(vmem_limit_bytes=16 * 1024 * 1024),
    )(date_s, *[pltpu.with_memory_space_constraint(operand, pltpu.HBM) for operand in [w_t] + small + arrays])
    got = lax.ppermute(give, axes, across(1))
    levels = call(
        level_rows_kernel, [((2 * dates_dev, 3 * model_d + LANES), BF16)] * 4, [date_s, keep, got], 1
    )
    arrived = {k: lax.ppermute(levels[k], axes, across(2 * k)) for k in (3, 2, 1)}
    return [levels[0]] + [arrived[k] for k in (2, 1, 3)], w_t


def finish_direct(operands, w_t, date_s, tile_s, heads, scale, pixel_dev, dates_dev, tiles, dates):
    length = dates * dates_dev
    cols, model_d = w_t.shape
    wide = model_d + EXT
    half_rows = length // 2
    payload = cols + 16 + half_rows * wide // LANES
    payload_z = cols + 16 + 2 * dates_dev * wide // LANES
    axes = ("tile", "date")

    def across(mask):
        return [(i, i ^ mask) for i in range(tiles * dates)]

    series, w_t = direct_series(operands, w_t, date_s, dates_dev, model_d, axes, across)
    *sends, rows_own, rows_give, sel = call(
        functools.partial(direct_series_kernel, heads, model_d, dates_dev),
        [((4 * length + 16, LANES), BF16)] * tiles
        + [((half_rows, wide), BF16), ((half_rows, wide), BF16), ((16, length), BF16)],
        [date_s, tile_s, *series, w_t],
        2,
        [pltpu.VMEM((length, 3 * model_d + LANES), BF16)],
    )
    parts = {k: lax.ppermute(sends[k], axes, across(dates * k + k % 2)) for k in (3, 2, 1)}
    keep, keep_sums, give = call(
        direct_slab_kernel,
        [((cols, LANES), F32), ((8, LANES), F32), ((payload, LANES), BF16)],
        [date_s, sends[0], parts[3], parts[2], parts[1], sel, rows_give],
        1,
    )
    got = lax.ppermute(give, axes, across(1))
    rows_own, own, *levels = call(
        functools.partial(direct_join_kernel, dates_dev),
        [((2 * dates_dev, wide), BF16), ((cols + 16, LANES), BF16)] + [((payload_z, LANES), BF16)] * 3,
        [keep, keep_sums, rows_own, got],
    )
    arrived = {k: lax.ppermute(levels[k - 1], axes, across(2 * k)) for k in (3, 2, 1)}
    low, high, both = (arrived[k] for k in (1, 2, 3))
    slab, rest = call(
        direct_total_kernel, [((cols, LANES), BF16), ((8, LANES), F32)], [own, low, both, high]
    )
    gathered = {k: lax.ppermute(slab, axes, across(dates * k)) for k in (3, 2, 1)}
    slabs = jnp.stack([slab] + [gathered[k] for k in TILE_ORDER[1:]])
    other_slabs = lax.ppermute(slabs, axes, across(1))
    outs = [
        jax.ShapeDtypeStruct((pixel_dev, dates_dev, model_d), BF16),
        jax.ShapeDtypeStruct((pixel_dev, dates_dev, model_d), BF16),
        jax.ShapeDtypeStruct((2, model_d), F32),
        jax.ShapeDtypeStruct((3, heads), F32),
        jax.ShapeDtypeStruct((cols, model_d), F32),
    ]
    held = [pltpu.VMEM((tiles, cols, LANES), F32), pltpu.SemaphoreType.DMA((tiles,))]
    limit = pltpu.CompilerParams(vmem_limit_bytes=48 * 1024 * 1024)
    value, inputs, table, head, weight_t = pl.pallas_call(
        functools.partial(final_kernel, heads, scale),
        out_shape=outs,
        in_specs=[SMEM] * 2 + [VMEM] * 7,
        out_specs=[HBM] * 5,
        scratch_shapes=[pltpu.VMEM(o.shape, o.dtype) for o in outs[:4]]
        + held
        + [pltpu.SemaphoreType.DMA((4,))],
        compiler_params=limit,
    )(date_s, tile_s, slabs, rows_own, low, high, both, rest, w_t)
    weight_t = pl.pallas_call(
        functools.partial(other_slabs_kernel, scale),
        out_shape=outs[4],
        in_specs=[SMEM, SMEM, VMEM, HBM],
        out_specs=HBM,
        scratch_shapes=held,
        input_output_aliases={3: 0},
        compiler_params=limit,
    )(date_s, tile_s, other_slabs, weight_t)
    return value, inputs, weight_t.T, table, head


def finish_any(series, w_t, date_s, tile_s, heads, scale, pixel_dev, dates_dev, tiles, dates):
    length = series.shape[0]
    cols, model_d = w_t.shape
    levels = dates // 2
    slab = model_d // tiles
    half = slab // 2
    swap = [(i, i ^ 1) for i in range(dates)]
    planes = [[2 * z + c for z in range(levels)] for c in range(2)]
    rows_core = length // 2
    send_t, own, give_rows, sel = call(
        functools.partial(series_kernel, heads, model_d, 0, dates_dev),
        [
            ((tiles, length, EXT + slab), BF16),
            ((rows_core, model_d + EXT), BF16),
            ((rows_core, model_d + EXT), BF16),
            ((16, length), BF16),
        ],
        [date_s, series, w_t],
        1,
    )
    mixed = [
        [t * dates + 2 * z + (c + t) % 2 for t in range(tiles)] for z in range(levels) for c in range(2)
    ]
    recv_t = lax.all_to_all(
        send_t, ("tile", "date"), split_axis=0, concat_axis=0, tiled=True, axis_index_groups=mixed
    )
    rows_give = cols + 24 + rows_core * (model_d + EXT) // LANES
    keep, keep_sums, give = call(
        functools.partial(slab_kernel, cols),
        [((cols, LANES), F32), ((2, EXT), F32), ((rows_give, LANES), BF16)],
        [date_s, recv_t, sel, give_rows],
        1,
    )
    got = lax.ppermute(give, "date", swap)
    rows_z = cols + 32 + model_d // 16
    (send_z,) = call(
        functools.partial(join_kernel, cols, dates_dev),
        [((levels, rows_z, LANES), BF16)],
        [date_s, keep, keep_sums, got, own],
        1,
    )
    recv_z = lax.all_to_all(
        send_z, "date", split_axis=0, concat_axis=0, tiled=True, axis_index_groups=planes
    )
    send_g, rest = call(
        functools.partial(total_kernel, cols),
        [((tiles, cols, LANES), BF16), ((16, LANES), F32)],
        [recv_z],
    )
    recv_g = lax.all_to_all(send_g, "tile", split_axis=0, concat_axis=0, tiled=True)
    local_outs = [
        ((pixel_dev, dates_dev, model_d), BF16),
        ((pixel_dev, dates_dev, model_d), BF16),
        ((2, model_d), F32),
        ((3, heads), F32),
    ]
    other_g = lax.ppermute(recv_g, "date", swap)
    if half % LANES == 0:
        weight_shape = jax.ShapeDtypeStruct((cols, model_d), F32)
        held = [pltpu.VMEM((tiles, cols, half), F32), pltpu.SemaphoreType.DMA((tiles,))]
        limit = pltpu.CompilerParams(vmem_limit_bytes=48 * 1024 * 1024)
        value, inputs, table, head, weight_t = pl.pallas_call(
            functools.partial(local_weight_kernel, heads, scale, cols, half),
            out_shape=[jax.ShapeDtypeStruct(s, d) for s, d in local_outs] + [weight_shape],
            in_specs=[SMEM] + [VMEM] * 4,
            out_specs=[HBM] * 5,
            scratch_shapes=[pltpu.VMEM(s, d) for s, d in local_outs]
            + held
            + [pltpu.SemaphoreType.DMA((4,))],
            compiler_params=limit,
        )(date_s, recv_g, recv_z, rest, w_t)
        weight_t = pl.pallas_call(
            functools.partial(half_kernel, cols, scale, half),
            out_shape=weight_shape,
            in_specs=[SMEM, VMEM, HBM],
            out_specs=HBM,
            scratch_shapes=held,
            input_output_aliases={2: 0},
            compiler_params=limit,
        )(date_s, other_g, weight_t)
    else:
        value, inputs, table, head = call(
            functools.partial(local_kernel, heads, scale), local_outs, [recv_z, rest, w_t]
        )
        (weight_t,) = call(
            functools.partial(gather_kernel, cols, half, scale),
            [((cols, model_d), F32)],
            [date_s, recv_g, other_g],
            1,
        )
    return (
        value,
        inputs,
        weight_t.T,
        table,
        head,
    )


def on_device(
    layer_input,
    head_input,
    out_grad,
    sensor_ids,
    valid_mask,
    sensor_table,
    proj_weight,
    step_bias,
    decay_log,
    skip_gain,
):
    pixel_dev, dates_dev, model_d = layer_input.shape
    heads = step_bias.shape[0]
    tiles = lax.axis_size("tile")
    dates = lax.axis_size("date")
    assert pixel_dev == dates and dates % 2 == 0
    levels = dates // 2
    length = dates * dates_dev
    slab = model_d // tiles
    half = slab // 2
    date_s = lax.axis_index("date").astype(jnp.int32).reshape(1)
    tile_s = lax.axis_index("tile").astype(jnp.int32).reshape(1)
    w_t = proj_weight.T
    scale = 1.0 / math.sqrt(pixel_dev * dates_dev * tiles * dates)

    operands = [
        sensor_ids,
        valid_mask.T,
        sensor_table,
        step_bias[None],
        decay_log[None],
        skip_gain[None],
        layer_input,
        head_input,
        out_grad,
    ]
    if levels == 4 and tiles == 4 and model_d == 2 * LANES * tiles:
        return finish_direct(operands, w_t, date_s, tile_s, heads, scale, pixel_dev, dates_dev, tiles, dates)
    packed = pl.pallas_call(
        pack_kernel,
        out_shape=jax.ShapeDtypeStruct((pixel_dev, dates_dev, 3 * model_d + LANES), BF16),
        in_specs=[SMEM] * 2 + [HBM] * 9,
        out_specs=VMEM,
        scratch_shapes=[
            pltpu.SMEM((dates_dev,), jnp.int32),
            pltpu.VMEM((dates_dev, pixel_dev), jnp.int32),
            pltpu.VMEM((2, model_d), F32),
            pltpu.VMEM((3, heads), F32),
            pltpu.VMEM((pixel_dev, dates_dev, model_d), BF16),
            pltpu.SemaphoreType.DMA((9,)),
        ],
        compiler_params=pltpu.CompilerParams(vmem_limit_bytes=16 * 1024 * 1024),
    )(date_s, tile_s, *[pltpu.with_memory_space_constraint(operand, pltpu.HBM) for operand in operands])
    series = lax.all_to_all(packed, "date", split_axis=0, concat_axis=0, tiled=True).reshape(
        length, 3 * model_d + LANES
    )

    return finish_any(series, w_t, date_s, tile_s, heads, scale, pixel_dev, dates_dev, tiles, dates)


def solution(mesh):
    in_specs = (
        P("tile", "date", None),
        P("tile", "date", None),
        P("tile", "date", None),
        P("date"),
        P("tile", "date"),
        P(),
        P(),
        P(),
        P(),
        P(),
    )
    out_specs = (P("tile", "date", None), P("tile", "date", None), P(), P(), P())
    return jax.shard_map(
        on_device, mesh=mesh, in_specs=in_specs, out_specs=out_specs, check_vma=False
    )
```
